32 devices in a mesh: ctx: 8 (over z, x), mp: 4 (over y, core).
Axes of the slice: x: 2, y: 2, z: 4, core: 2. Of those that a mesh axis runs over, the one named last changes fastest.
Arguments:
- inputs: bfloat16 [8192, 384], P('ctx'), may hold values from -6 to 6
- w_query: bfloat16 [384, 192], P(None, 'mp'), may hold values from -0.4375 to 0.4375
- b_query: bfloat16 [192], P('mp'), may hold values from -1.5 to 1.5
- w_key: bfloat16 [384, 192], P(None, 'mp'), may hold values from -0.3125 to 0.3125
- w_value: bfloat16 [384, 192], P(None, 'mp'), may hold values from -0.3125 to 0.3125
- b_value: bfloat16 [192], P('mp'), may hold values from -1.5 to 1.5
- depth_kernel: bfloat16 [9, 384], replicated, may hold values from -2 to 2
- w_point: bfloat16 [384, 192], P(None, 'mp'), may hold values from -0.3125 to 0.3125
- b_point: bfloat16 [192], P('mp'), may hold values from -1.5 to 1.5
- w_kernel: bfloat16 [192, 36], P('mp'), may hold values from -0.4375 to 0.4375
- b_kernel: bfloat16 [36], replicated, may hold values from -2.5 to 2.5
- w_conv: bfloat16 [384, 192], P(None, 'mp'), may hold values from -0.3125 to 0.3125
- b_conv: bfloat16 [192], P('mp'), may hold values from -1.5 to 1.5
- w_out: bfloat16 [2, 192, 384], P(None, 'mp'), may hold values from -0.875 to 0.875
- b_out: bfloat16 [384], replicated, may hold values from -1.5 to 1.5
- gain_one: float32 [384], replicated, may hold values from 0.5 to 1.5
- shift_one: float32 [384], replicated, may hold values from -1.5 to 1.5
- w_inner: bfloat16 [2, 192, 768], P(None, None, 'mp'), may hold values from -0.4375 to 0.4375
- b_inner: bfloat16 [2, 768], P(None, 'mp'), may hold values from -1.5 to 1.5
- w_outer: bfloat16 [2, 768, 192], P(None, 'mp'), may hold values from -0.21875 to 0.21875
- b_outer: bfloat16 [384], replicated, may hold values from -1.5 to 1.5
- gain_two: float32 [384], replicated, may hold values from 0.5 to 1.5
- shift_two: float32 [384], replicated, may hold values from -1.5 to 1.5
- cotangent: bfloat16 [8192, 384], P('ctx'), may hold values from -6 to 6
Outputs:
- layer_out: bfloat16 [8192, 384], P('ctx')
- inputs_grad: float32 [8192, 384], P('ctx')
- grad_query: float32 [384, 192], P(None, 'mp')
- grad_qbias: float32 [192], P('mp')
- grad_key: float32 [384, 192], P(None, 'mp')
- grad_value: float32 [384, 192], P(None, 'mp')
- grad_vbias: float32 [192], P('mp')
- grad_depth: float32 [9, 384], replicated
- grad_point: float32 [384, 192], P(None, 'mp')
- grad_pbias: float32 [192], P('mp')
- grad_kernel: float32 [192, 36], P('mp')
- grad_kbias: float32 [36], replicated
- grad_conv: float32 [384, 192], P(None, 'mp')
- grad_cbias: float32 [192], P('mp')
- grad_out: float32 [2, 192, 384], P(None, 'mp')
- grad_obias: float32 [384], replicated
- grad_gain1: float32 [384], replicated
- grad_shift1: float32 [384], replicated
- grad_inner: float32 [2, 192, 768], P(None, None, 'mp')
- grad_ibias: float32 [2, 768], P(None, 'mp')
- grad_outer: float32 [2, 768, 192], P(None, 'mp')
- grad_ubias: float32 [384], replicated
- grad_gain2: float32 [384], replicated
- grad_shift2: float32 [384], replicated
The draws below stay inside these ranges and needn't reach their ends.
All inputs are finite; a program needn't handle non-finite values.
Results may differ from the reference program's by a relative error of at most 0.039.
Values may be sent and summed in bfloat16 or wider, within the bound.
No kernel may reach another device: no remote copies, remote signals or barrier semaphores. Data moves between devices by JAX's collectives and lax.ppermute only.
A program may use at most 128 MiB of HBM per device.

```python
import math
import jax
import jax.numpy as jnp
from jax import lax

D = 384
HEADS = 4
HEAD = 48
FF = 1536
KS = 9
GROUPS = 2
SEQS = 1
A = 192
TOKENS = 8192
SEQ_LEN = 8192


def levels(own_key, dims, pieces, low, largest):
    factor_of = 1.0
    for position, parts in pieces:
        heights = jax.random.uniform(jax.random.fold_in(jax.random.fold_in(own_key, 6), position), (parts,), jnp.float32, low / len(pieces), largest / len(pieces))
        factor_of = factor_of * jnp.repeat(jnp.exp(heights), dims[position] // parts).reshape((-1,) + (1,) * (len(dims) - 1 - position))
    return factor_of


def gaussian(own_key, extent, width, reach, shards=(), dtype=jnp.bfloat16):
    entries = width * jax.random.normal(own_key, extent, jnp.float32)
    if shards:
        entries = entries * levels(own_key, extent, shards, -0.22, 0.18)
    return jnp.clip(entries, -reach, reach).astype(dtype)


def setup_inputs(seed: int = 0) -> dict:
    arg_keys = jax.random.split(jax.random.key(seed), 25)
    inputs = gaussian(arg_keys[0], (TOKENS, D), 1.0, 6.0, ((0, 8),))
    w_query = gaussian(arg_keys[1], (D, A), (D // 2) ** -0.5, 0.4375, ((1, 4),))
    b_query = gaussian(arg_keys[2], (A,), 0.3, 1.5, ((0, 4),))
    w_key = gaussian(arg_keys[3], (D, A), D ** -0.5, 0.3125, ((1, 4),))
    w_value = gaussian(arg_keys[4], (D, A), D ** -0.5, 0.3125, ((1, 4),))
    b_value = gaussian(arg_keys[5], (A,), 0.3, 1.5, ((0, 4),))
    depth_kernel = gaussian(arg_keys[6], (KS, D), 0.33, 2.0)
    w_point = gaussian(arg_keys[7], (D, A), D ** -0.5, 0.3125, ((1, 4),))
    b_point = gaussian(arg_keys[8], (A,), 0.3, 1.5, ((0, 4),))
    w_kernel = gaussian(arg_keys[9], (A, HEADS * KS), A ** -0.5, 0.4375, ((0, 4),))
    b_kernel = gaussian(arg_keys[10], (HEADS * KS,), 0.5, 2.5)
    w_conv = gaussian(arg_keys[11], (D, A), D ** -0.5, 0.3125, ((1, 4),))
    b_conv = gaussian(arg_keys[12], (A,), 0.3, 1.5, ((0, 4),))
    w_out = gaussian(arg_keys[13], (2, A, D), (D // 8) ** -0.5, 0.875, ((1, 4),))
    b_out = gaussian(arg_keys[14], (D,), 0.3, 1.5)
    gain_one = jnp.clip(1.0 + 0.1 * jax.random.normal(arg_keys[15], (D,), jnp.float32), 0.5, 1.5)
    shift_one = gaussian(arg_keys[16], (D,), 0.3, 1.5, (), jnp.float32)
    w_inner = gaussian(arg_keys[17], (GROUPS, D // GROUPS, FF // GROUPS), (D // GROUPS) ** -0.5, 0.4375, ((2, 4),))
    b_inner = gaussian(arg_keys[18], (GROUPS, FF // GROUPS), 0.3, 1.5, ((1, 4),))
    w_outer = gaussian(arg_keys[19], (GROUPS, FF // GROUPS, D // GROUPS), (FF // GROUPS) ** -0.5, 0.21875, ((1, 4),))
    b_outer = gaussian(arg_keys[20], (D,), 0.3, 1.5)
    gain_two = jnp.clip(1.0 + 0.1 * jax.random.normal(arg_keys[21], (D,), jnp.float32), 0.5, 1.5)
    shift_two = gaussian(arg_keys[22], (D,), 0.3, 1.5, (), jnp.float32)
    cotangent = gaussian(arg_keys[23], (TOKENS, D), 1.0, 6.0, ((0, 8),))
    return {"inputs": inputs, "w_query": w_query, "b_query": b_query, "w_key": w_key, "w_value": w_value, "b_value": b_value, "depth_kernel": depth_kernel, "w_point": w_point, "b_point": b_point, "w_kernel": w_kernel, "b_kernel": b_kernel, "w_conv": w_conv, "b_conv": b_conv, "w_out": w_out, "b_out": b_out, "gain_one": gain_one, "shift_one": shift_one, "w_inner": w_inner, "b_inner": b_inner, "w_outer": w_outer, "b_outer": b_outer, "gain_two": gain_two, "shift_two": shift_two, "cotangent": cotangent}


EPSILON = 1e-12

@jax.custom_vjp
def low(v):
    return lax.optimization_barrier(v.astype(jnp.bfloat16)).astype(jnp.float32)

@jax.custom_vjp
def low_back(v):
    return v

def low_keep(v):
    return (low(v), None)

def low_pass(kept, grad):
    return (grad,)

def back_keep(v):
    return (v, None)

def back_low(kept, grad):
    return (low(grad),)
low.defvjp(low_keep, low_pass)
low_back.defvjp(back_keep, back_low)

def product(left, right):
    return jnp.dot(left, right, precision=lax.Precision.HIGHEST)

def layer_norm(hidden, gain, shift):
    centred = hidden - lax.optimization_barrier(jnp.mean(hidden, axis=-1, keepdims=True))
    return centred * lax.rsqrt(lax.optimization_barrier(jnp.mean(centred * centred, axis=-1, keepdims=True)) + EPSILON) * gain + shift

def attention(queries, key_rows, values):
    seq_len = queries.shape[0]
    block_rows = math.gcd(seq_len, 512)
    key_heads = key_rows.reshape(seq_len, HEADS, HEAD)
    val_heads = values.reshape(seq_len, HEADS, HEAD)

    def one_block(query_block):
        raw_scores = jnp.einsum('qhe,khe->hqk', query_block, key_heads, precision=lax.Precision.HIGHEST)
        scores = low_back(raw_scores) * (1.0 / math.sqrt(HEAD))
        attn_probs = low(jax.nn.softmax(scores, axis=-1))
        mixed_heads = jnp.einsum('hqk,khe->qhe', attn_probs, val_heads, precision=lax.Precision.HIGHEST)
        return low(low_back(mixed_heads))
    blocks = lax.map(jax.checkpoint(one_block), queries.reshape(seq_len // block_rows, block_rows, HEADS, HEAD))
    return blocks.reshape(seq_len, HEADS * HEAD)

def forward_seq(inputs, w_query, b_query, w_key, w_value, b_value, depth_kernel, w_point, b_point, w_kernel, b_kernel, w_conv, b_conv, w_out, b_out, gain_one, shift_one, w_inner, b_inner, w_outer, b_outer, gain_two, shift_two):
    seq_len = inputs.shape[0]
    reach_rows = KS // 2
    queries = low(low_back(product(inputs, w_query) + b_query))
    key_rows = low(low_back(product(inputs, w_key)))
    values = low(low_back(product(inputs, w_value) + b_value))
    padded = jnp.pad(inputs, ((reach_rows, reach_rows), (0, 0)))
    depth_vals = padded[0:seq_len] * depth_kernel[0]
    for tap_at in range(1, KS):
        depth_vals = depth_vals + padded[tap_at:tap_at + seq_len] * depth_kernel[tap_at]
    depth_low = low(depth_vals)
    key_conv = low_back(product(depth_low, w_point) + b_point)
    conv_attn = low(key_conv * queries)
    logits = low_back(product(conv_attn, w_kernel) + b_kernel).reshape(seq_len, HEADS, KS)
    tap_probs = jax.nn.softmax(logits, axis=-1)
    conv_vals = low_back(product(inputs, w_conv) + b_conv)
    conv_pad = jnp.pad(conv_vals, ((reach_rows, reach_rows), (0, 0))).reshape(seq_len + 2 * reach_rows, HEADS, HEAD)
    conv_mix = tap_probs[:, :, 0, None] * conv_pad[0:seq_len]
    for tap_at in range(1, KS):
        conv_mix = conv_mix + tap_probs[:, :, tap_at, None] * conv_pad[tap_at:tap_at + seq_len]
    conv_low = low(conv_mix.reshape(seq_len, HEADS * HEAD))
    context = attention(queries, key_rows, values)
    mixed = low_back(product(context, w_out[0]) + product(conv_low, w_out[1]) + b_out)
    norm_one = low(layer_norm(mixed + inputs, gain_one, shift_one))
    grouped = norm_one.reshape(seq_len, GROUPS, D // GROUPS)
    inner_pre = low_back(jnp.einsum('tgd,gdf->tgf', grouped, w_inner, precision=lax.Precision.HIGHEST) + b_inner)
    activated = low(jax.nn.gelu(inner_pre, approximate=False))
    outer_raw = jnp.einsum('tgf,gfd->tgd', activated, w_outer, precision=lax.Precision.HIGHEST).reshape(seq_len, D)
    outer = low_back(outer_raw + b_outer)
    return layer_norm(outer + norm_one, gain_two, shift_two)

def forward(inputs, *weights):
    sequences = inputs.reshape(SEQS, SEQ_LEN, D)
    results = lax.map(lambda one_seq: forward_seq(one_seq, *weights), sequences)
    return results.reshape(SEQS * SEQ_LEN, D)

def reference(inputs, w_query, b_query, w_key, w_value, b_value, depth_kernel, w_point, b_point, w_kernel, b_kernel, w_conv, b_conv, w_out, b_out, gain_one, shift_one, w_inner, b_inner, w_outer, b_outer, gain_two, shift_two, cotangent):
    float_args = [item.astype(jnp.float32) for item in (inputs, w_query, b_query, w_key, w_value, b_value, depth_kernel, w_point, b_point, w_kernel, b_kernel, w_conv, b_conv, w_out, b_out, gain_one, shift_one, w_inner, b_inner, w_outer, b_outer, gain_two, shift_two)]
    layer_final, pullback = jax.vjp(forward, *float_args)
    gradients = pullback(cotangent.astype(jnp.float32))
    return (layer_final.astype(jnp.bfloat16), gradients[0], gradients[1], gradients[2], gradients[3], gradients[4], gradients[5], gradients[6], gradients[7], gradients[8], gradients[9], gradients[10], gradients[11], gradients[12], gradients[13], gradients[14], gradients[15], gradients[16], gradients[17], gradients[18], gradients[19], gradients[20], gradients[21], gradients[22])
```

```python
import functools
import math

import jax
import jax.numpy as jnp
from jax import lax
from jax.experimental import pallas as pl
from jax.experimental.pallas import tpu as pltpu
from jax.sharding import PartitionSpec as P


EPSILON = 1e-12
HIGH_BLOCK = 56 * 2**20
f32 = jnp.float32
bf16 = jnp.bfloat16

WQ, WK, WV, WP, WC, WO, WI, WU, WM, WB = 0, 48, 96, 144, 192, 240, 336, 528, 720, 768
PACK_ROWS = 784
GP, GC, GQ, GO, GI, GU, GM, GV = 0, 48, 96, 144, 240, 432, 624, 672
GRAD_ROWS = 688


def dg(left, right, ld, rd):
    return lax.dot_general(
        left, right, (((ld,), (rd,)), ((), ())), preferred_element_type=f32
    )


def outer_ones(row, width):
    return dg(row, jnp.ones((row.shape[0], width), bf16), 0, 0)


def call(body, outs, args, flops=0, byts=0, trans=0, scratch=(), aliases=None, smem=()):
    specs = [
        pl.BlockSpec(memory_space=pltpu.SMEM if i in smem else pltpu.VMEM)
        for i in range(len(args))
    ]
    return pl.pallas_call(
        body,
        in_specs=specs,
        out_specs=[pl.BlockSpec(memory_space=pltpu.VMEM)] * len(outs),
        out_shape=[jax.ShapeDtypeStruct(s, d) for s, d in outs],
        scratch_shapes=list(scratch),
        input_output_aliases=aliases or {},
        compiler_params=pltpu.CompilerParams(vmem_limit_bytes=HIGH_BLOCK),
        cost_estimate=pl.CostEstimate(flops=flops, bytes_accessed=byts, transcendentals=trans),
    )(*args)


def project_body(x_ref, wq_ref, bq_ref, wk_ref, wv_ref, bv_ref, out_ref):
    x = x_ref[...]
    width = x.shape[0]
    weights = jnp.concatenate([wk_ref[...], wv_ref[...], wq_ref[...]], axis=0)
    found = dg(weights, x, 1, 1)
    out_ref[0:48, :] = found[0:48].astype(bf16)
    out_ref[48:96, :] = (found[48:96] + outer_ones(bv_ref[...], width)).astype(bf16)
    out_ref[96:144, :] = (found[96:144] + outer_ones(bq_ref[...], width)).astype(bf16)


def pack_body(
    wq_ref, wk_ref, wv_ref, wp_ref, wc_ref, wo_ref, wi_ref, wu_ref, wm_ref,
    bq_ref, bp_ref, bc_ref, bi_ref, out_ref,
):
    for at, ref in ((WQ, wq_ref), (WK, wk_ref), (WV, wv_ref), (WP, wp_ref), (WC, wc_ref)):
        out_ref[at : at + 48, :] = ref[...]
    out_ref[WO : WO + 48, :] = wo_ref[0]
    out_ref[WO + 48 : WO + 96, :] = wo_ref[1]
    out_ref[WI : WI + 192, :] = jnp.concatenate([wi_ref[0], wi_ref[1]], axis=1)
    out_ref[WU : WU + 192, :] = jnp.concatenate([wu_ref[0], wu_ref[1]], axis=1)
    out_ref[WM : WM + 64, :] = jnp.zeros((64, 384), bf16)
    out_ref[WM : WM + 36, 0:48] = wm_ref[...]
    zeros = jnp.zeros((1, 336), f32)
    lines = [jnp.concatenate([bi_ref[0:1].astype(f32), bi_ref[1:2].astype(f32)], axis=1)]
    for ref in (bq_ref, bp_ref, bc_ref):
        lines.append(jnp.concatenate([ref[...].astype(f32), zeros], axis=1))
    lines.append(jnp.zeros((12, 384), f32))
    out_ref[WB : WB + 16, :] = jnp.concatenate(lines, axis=0).astype(bf16)


def keys_aug(kv):
    keys = kv[0:48]
    return jnp.concatenate([keys, keys, jnp.ones((16, keys.shape[1]), bf16)], axis=0)


def vals_aug(kv):
    vals = kv[48:96]
    return jnp.concatenate([vals, jnp.ones((16, vals.shape[1]), bf16)], axis=0)


def split3(value):
    high = value.astype(bf16)
    rest = value - high.astype(f32)
    mid = rest.astype(bf16)
    low = (rest - mid.astype(f32)).astype(bf16)
    return high, mid, low


def scaled_queries(q):
    scaled = q.astype(f32) * (math.log2(math.e) / math.sqrt(48.0))
    high = scaled.astype(bf16)
    low = (scaled - high.astype(f32)).astype(bf16)
    return high, low


def flash_body(*refs, first, last, blocks):
    refs = list(refs)
    q_ref = refs.pop(0)
    tp_ref = refs.pop(0) if last else None
    kv_refs = [refs.pop(0) for _ in range(blocks)]
    if first:
        m_out, acc_out = refs
        m_now = acc_now = None
    else:
        m_in, acc_in = refs.pop(0), refs.pop(0)
        m_now, acc_now = m_in[0:1, :], acc_in[...]
    q = q_ref[...]
    width = q.shape[1]
    high, low = scaled_queries(q)
    q_aug = jnp.concatenate([high, low, jnp.zeros((16, width), bf16)], axis=0)
    for kv_ref in kv_refs:
        kv = kv_ref[...]
        scores = dg(keys_aug(kv), q_aug, 0, 0)
        top = jnp.max(scores, axis=0, keepdims=True)
        m_new = top if m_now is None else jnp.maximum(m_now, top)
        probs = jnp.exp2(scores - m_new).astype(bf16)
        part = dg(vals_aug(kv), probs, 1, 0)
        acc_now = part if m_now is None else acc_now * jnp.exp2(m_now - m_new) + part
        m_now = m_new
    if not last:
        if not first:
            m_out, acc_out = refs
        m_out[...] = jnp.broadcast_to(m_now, (8, width))
        acc_out[...] = acc_now
        return
    raw_ref, lse_ref, *sends, low_scr = refs
    total = acc_now[48:49, :]
    raw = acc_now[0:48, :] / total
    raw_ref[...] = raw
    lse_ref[...] = jnp.broadcast_to(m_now + jnp.log2(total), (8, width))
    low_scr[...] = raw.astype(bf16)
    quarter = width // 4
    place = tp_ref[0]
    for s, send in enumerate(sends):
        at = pl.multiple_of((place ^ s) * quarter, quarter)
        send[...] = low_scr[:, pl.ds(at, quarter)]


def flash(q, kvs, state, place=None):
    width = q.shape[1]
    first, last = state is None, place is not None
    args = [q] + ([place] if last else []) + list(kvs) + ([] if first else list(state))
    if last:
        outs = [((48, width), f32), ((8, width), f32)] + [((48, width // 4), bf16)] * 4
        scratch = [pltpu.VMEM((48, width), bf16)]
    else:
        outs, scratch = [((8, width), f32), ((64, width), f32)], []
    cells = len(kvs) * width * kvs[0].shape[1]
    return call(
        functools.partial(flash_body, first=first, last=last, blocks=len(kvs)),
        outs, args, flops=cells * 512, byts=2**20, trans=cells, scratch=scratch,
        smem=(1,) if last else (),
    )


def back_prepare_body(place_ref, q_ref, lse_ref, raw_ref, g0, g1, g2, g3, qa_ref, da_ref):
    q = q_ref[...]
    width = q.shape[1]
    quarter = width // 4
    high, low = scaled_queries(q)
    lines = split3(-lse_ref[0:1, :])
    pad = jnp.zeros((13, width), bf16)
    qa_ref[...] = jnp.concatenate([high, low, *lines, pad], axis=0)
    place = place_ref[0]
    for s, ref in enumerate((g0, g1, g2, g3)):
        at = pl.multiple_of((place ^ s) * quarter, quarter)
        da_ref[0:48, pl.ds(at, quarter)] = ref[...]
    grad = da_ref[0:48, :]
    delta = jnp.sum(grad.astype(f32) * raw_ref[...], axis=0, keepdims=True)
    da_ref[48:64, :] = jnp.concatenate([*split3(-delta), pad], axis=0)


def back_body(*refs, first, plus):
    refs = list(refs)
    q_ref, qa_ref, da_ref, kv_ref = refs[:4]
    refs = refs[4:]
    dq_in = None if first else refs.pop(0)
    plus_ref = refs.pop(0) if plus else None
    dq_out, dkv_out = refs
    kv = kv_ref[...]
    keys, vals = keys_aug(kv), vals_aug(kv)
    width = kv.shape[1]
    q, grad = q_ref[...], da_ref[0:48, :]
    q_aug, grad_aug = qa_ref[...], da_ref[...]
    step = 256
    dq = None if first else dq_in[...]
    for at in range(0, width, step):
        span = slice(at, at + step)
        probs = jnp.exp2(dg(keys[:, span], q_aug, 0, 0))
        grad_probs = dg(vals[:, span], grad_aug, 0, 0)
        grad_scores = (probs * grad_probs).astype(bf16)
        dv = dg(grad, probs.astype(bf16), 1, 1)
        dk = dg(q, grad_scores, 1, 1)
        part = dg(kv[0:48, span], grad_scores, 1, 0)
        dq = part if dq is None else dq + part
        both = jnp.concatenate([dk, dv], axis=0)
        if plus:
            both = both + plus_ref[:, span].astype(f32)
        dkv_out[:, span] = both.astype(dkv_out.dtype)
    dq_out[...] = dq


def back(q, q_aug, grad_aug, kv, dq, plus, out_dtype):
    width = q.shape[1]
    args = [q, q_aug, grad_aug, kv] + ([] if dq is None else [dq])
    args += [] if plus is None else [plus]
    cells = width * kv.shape[1]
    return call(
        functools.partial(back_body, first=dq is None, plus=plus is not None),
        [((48, width), f32), ((96, kv.shape[1]), out_dtype)],
        args, flops=cells * 1280, byts=2**20, trans=cells,
    )


def back_join_body(*refs, parts):
    refs = list(refs)
    dq_ref, dkv_ref = refs[:2]
    news = refs[2 : 2 + parts]
    out_ref = refs[2 + parts]
    scale = 1.0 / math.sqrt(48.0)
    out_ref[0:48, :] = (dq_ref[...] * scale).astype(bf16)
    total = dkv_ref[...]
    for ref in news:
        total = total + ref[...].astype(f32)
    out_ref[48:96, :] = (total[0:48] * scale).astype(bf16)
    out_ref[96:144, :] = total[48:96].astype(bf16)


def tap_places(mp, heads, taps):
    rows = lax.broadcasted_iota(jnp.int32, (48, 8 * taps), 0)
    cols = lax.broadcasted_iota(jnp.int32, (48, 8 * taps), 1)
    s = cols & 7
    wanted = (s ^ mp) * taps + (cols >> 3)
    return ((rows == wanted) & (s < heads)).astype(f32).astype(bf16)


def lift(value, axis, shift, keep):
    size = value.shape[axis]
    rolled = pltpu.roll(value, (size - shift) % size, axis)
    return rolled[:keep] if axis == 0 else rolled[:, :keep]


def conv_body(
    place_ref, xe_ref, dk_ref, bk_ref, p0, p1, p2, p3,
    mix_ref, depth_ref, q_ref, kc_ref, tp_ref, cv_ref, *, rim, quarter, taps,
):
    packs = (p0, p1, p2, p3)
    xe = xe_ref[...]
    x_own = xe[rim : rim + quarter]
    wide = xe.astype(f32)
    reach = taps // 2
    kernel = dk_ref[...].astype(f32)
    depth = None
    for j in range(taps):
        term = lift(wide, 0, rim - reach + j, quarter) * kernel[j : j + 1, :]
        depth = term if depth is None else depth + term
    depth_low = depth.astype(bf16)
    depth_ref[...] = depth_low
    position = place_ref[1] + lax.broadcasted_iota(jnp.int32, (1, xe.shape[0]), 1) - rim
    inside = (position >= 0) & (position < place_ref[2])
    attn = []
    for s, pack in enumerate(packs):
        own = slice(48 * s, 48 * s + 48)
        q = (
            dg(pack[WQ : WQ + 48, :], x_own, 1, 1)
            + outer_ones(pack[WB + 1 : WB + 2, 0:48], quarter)
        ).astype(bf16)
        kc = dg(pack[WP : WP + 48, :], depth_low, 1, 1) + outer_ones(
            pack[WB + 2 : WB + 3, 0:48], quarter
        )
        cv = dg(pack[WC : WC + 48, :], xe, 1, 1) + outer_ones(
            pack[WB + 3 : WB + 4, 0:48], xe.shape[0]
        )
        q_ref[own, :] = q
        kc_ref[own, :] = kc
        cv_ref[own, :] = jnp.where(inside, cv, 0.0)
        attn.append((kc * q.astype(f32)).astype(bf16))
    attn = jnp.concatenate(attn, axis=0)
    hot = tap_places(place_ref[0], 4, taps)
    wk = [dg(pack[WM : WM + 48, 0:48], hot, 0, 0) for pack in packs]
    wk = jnp.concatenate(wk, axis=0).astype(bf16)
    bias = dg(bk_ref[...], hot[0 : bk_ref.shape[1], :], 1, 0).astype(bf16)
    logits = dg(wk, attn, 0, 0) + outer_ones(bias, quarter)
    tiles = [logits[8 * j : 8 * j + 8] for j in range(taps)]
    top = functools.reduce(jnp.maximum, tiles)
    tiles = [jnp.exp(tile - top) for tile in tiles]
    total = functools.reduce(jnp.add, tiles)
    tiles = [tile / total for tile in tiles]
    for j in range(taps):
        tp_ref[8 * j : 8 * j + 8, :] = tiles[j]
    cv = cv_ref[...]
    mix = [None] * 4
    for j in range(taps):
        moved = lift(cv, 1, rim - reach + j, quarter)
        for s in range(4):
            term = tiles[j][s : s + 1, :] * moved[48 * s : 48 * s + 48]
            mix[s] = term if mix[s] is None else mix[s] + term
    for s in range(4):
        mix_ref[48 * s : 48 * s + 48, :] = mix[s].astype(bf16)


def conv_back_body(
    place_ref, xe_ref, dk_ref, p0, p1, p2, p3, q_ref, kc_ref, tp_ref, cv_ref, gm_ref,
    ex_ref, pre_ref, gk_ref, kb_ref, dpt_ref, dep_ref, cve_ref, low_ref, high_ref,
    *, rim, quarter, taps,
):
    packs = (p0, p1, p2, p3)
    reach = taps // 2
    ext = xe_ref.shape[0]
    grad_mix = gm_ref[...]
    cv = cv_ref[...]
    probs = [tp_ref[8 * j : 8 * j + 8, :] for j in range(taps)]
    grads = []
    weighted = None
    for j in range(taps):
        moved = lift(cv, 1, rim - reach + j, quarter) * grad_mix
        lines = [jnp.sum(moved[48 * s : 48 * s + 48], axis=0, keepdims=True) for s in range(4)]
        tile = jnp.concatenate(lines + [jnp.zeros((4, quarter), f32)], axis=0)
        grads.append(tile)
        term = probs[j] * tile
        weighted = term if weighted is None else weighted + term
    gtl = jnp.concatenate(
        [probs[j] * (grads[j] - weighted) for j in range(taps)], axis=0
    ).astype(bf16)
    hot = tap_places(place_ref[0], 4, taps)
    wk = [dg(pack[WM : WM + 48, 0:48], hot, 0, 0) for pack in packs]
    wk = jnp.concatenate(wk, axis=0).astype(bf16)
    q = q_ref[...].astype(f32)
    kc = kc_ref[...]
    attn = (kc * q).astype(bf16)
    plain = dg(hot, gtl, 1, 0).astype(bf16)
    for s in range(4):
        gk_ref[s] = dg(plain, attn[48 * s : 48 * s + 48], 1, 1)
    kb_ref[...] = dg(plain, jnp.ones((128, quarter), bf16), 1, 1)
    grad_attn = dg(wk, gtl, 1, 0)
    ex_ref[...] = (grad_attn * kc).astype(bf16)
    grad_kc = (grad_attn * q).astype(bf16)
    pre_ref[...] = grad_kc
    wp = jnp.concatenate([pack[WP : WP + 48, :] for pack in packs], axis=0)
    dvals = dg(grad_kc, wp, 0, 0)
    wide = xe_ref[...].astype(f32)
    kernel = dk_ref[...].astype(f32)
    tail = jnp.zeros((ext - quarter, dvals.shape[1]), f32)
    padded = jnp.concatenate([dvals, tail], axis=0)
    depth = None
    lines = []
    for j in range(taps):
        moved = lift(wide, 0, rim - reach + j, quarter)
        lines.append(jnp.sum(moved * dvals, axis=0, keepdims=True))
        term = pltpu.roll(padded, rim - reach + j, 0) * kernel[j : j + 1, :]
        depth = term if depth is None else depth + term
    lines.append(jnp.zeros((16 - taps, dvals.shape[1]), f32))
    dpt_ref[...] = jnp.concatenate(lines, axis=0)
    side = jnp.zeros((4 * 48, ext - quarter), f32)
    spread = None
    for j in range(taps):
        rows = [probs[j][s : s + 1, :] * grad_mix[48 * s : 48 * s + 48] for s in range(4)]
        full = jnp.concatenate([jnp.concatenate(rows, axis=0), side], axis=1)
        term = pltpu.roll(full, rim - reach + j, 1)
        spread = term if spread is None else spread + term
    dep_ref[...] = depth[rim : rim + quarter]
    cve_ref[...] = spread
    edge = jnp.transpose(spread[:, 0:128], (1, 0))
    low_ref[...] = jnp.concatenate([depth[rim - 8 : rim], edge[rim - 8 : rim]], axis=1)
    end = rim + quarter
    edge = jnp.transpose(spread[:, end - rim : end - rim + 128], (1, 0))
    high_ref[...] = jnp.concatenate([depth[end : end + 8], edge[rim : rim + 8]], axis=1)


def norm(hidden):
    centred = hidden - jnp.mean(hidden, axis=-1, keepdims=True)
    inverse = lax.rsqrt(jnp.mean(centred * centred, axis=-1, keepdims=True) + EPSILON)
    return centred * inverse, inverse


def norm_back(grad, normed, inverse, gain):
    scaled = grad * gain
    return inverse * (
        scaled
        - jnp.mean(scaled, axis=-1, keepdims=True)
        - normed * jnp.mean(scaled * normed, axis=-1, keepdims=True)
    )


def feed_body(
    r0, r1, r2, r3, mix_ref, p0, p1, p2, p3, x_ref, cot_ref, lines_ref,
    out_ref, c0, c1, c2, c3, gmix_ref, a_ref, act_ref, gpre_ref, low_ref, zed_ref, gm_ref,
    gh_ref, vec_ref, slope_scr,
):
    packs = (p0, p1, p2, p3)
    both = []
    for s, ref in enumerate((r0, r1, r2, r3)):
        both += [ref[...], mix_ref[48 * s : 48 * s + 48, :]]
    both = jnp.concatenate(both, axis=0)
    a_ref[...] = both
    w_out = jnp.concatenate([pack[WO : WO + 96, :] for pack in packs], axis=0)
    mixed = dg(both, w_out, 0, 0) + lines_ref[0:1, :]
    normed1, inverse1 = norm(mixed + x_ref[...].astype(f32))
    gain1, gain2 = lines_ref[1:2, :], lines_ref[4:5, :]
    low = (normed1 * gain1 + lines_ref[2:3, :]).astype(bf16)
    low_ref[...] = low
    halves = [low[:, 0:192], low[:, 192:384]]
    outer = [None, None]
    for g in range(2):
        lanes = slice(192 * g, 192 * g + 192)
        for s, pack in enumerate(packs):
            pre = dg(halves[g], pack[WI : WI + 192, lanes], 1, 0)
            pre = pre + pack[WB : WB + 1, lanes].astype(f32)
            cdf = 0.5 * (1.0 + lax.erf(pre * math.sqrt(0.5)))
            pdf = jnp.exp(-0.5 * pre * pre) * (1.0 / math.sqrt(2.0 * math.pi))
            slope_scr[2 * s + g] = cdf + pre * pdf
            act = (pre * cdf).astype(bf16)
            act_ref[2 * s + g] = act
            term = dg(act, pack[WU : WU + 192, lanes], 1, 0)
            outer[g] = term if outer[g] is None else outer[g] + term
    outer = jnp.concatenate(outer, axis=1) + lines_ref[3:4, :]
    normed2, inverse2 = norm(outer + low.astype(f32))
    out_ref[...] = (normed2 * gain2 + lines_ref[5:6, :]).astype(bf16)
    cot = cot_ref[...].astype(f32)
    grad_h2 = norm_back(cot, normed2, inverse2, gain2)
    zed = grad_h2.astype(bf16)
    zed_ref[...] = zed
    halves = [zed[:, 0:192], zed[:, 192:384]]
    back = [None, None]
    for g in range(2):
        lanes = slice(192 * g, 192 * g + 192)
        for s, pack in enumerate(packs):
            grad_act = dg(halves[g], pack[WU : WU + 192, lanes], 1, 1)
            gpre = (grad_act * slope_scr[2 * s + g]).astype(bf16)
            gpre_ref[2 * s + g] = gpre
            term = dg(gpre, pack[WI : WI + 192, lanes], 1, 1)
            back[g] = term if back[g] is None else back[g] + term
    grad_norm1 = jnp.concatenate(back, axis=1) + grad_h2
    grad_h1 = norm_back(grad_norm1, normed1, inverse1, gain1)
    gh_ref[...] = grad_h1
    gm = grad_h1.astype(bf16)
    gm_ref[...] = gm
    grads = dg(w_out, gm, 1, 1)
    for s, ref in enumerate((c0, c1, c2, c3)):
        ref[...] = grads[96 * s : 96 * s + 48].astype(bf16)
        gmix_ref[48 * s : 48 * s + 48, :] = grads[96 * s + 48 : 96 * s + 96]
    sums = [gm.astype(f32), grad_norm1 * normed1, grad_norm1, zed.astype(f32), cot * normed2, cot]
    lines = [jnp.sum(item, axis=0, keepdims=True) for item in sums]
    lines.append(jnp.zeros((2, 384), f32))
    vec_ref[...] = jnp.concatenate(lines, axis=0)


def weights_body(
    x_ref, p0, p1, p2, p3, a_ref, act_ref, gpre_ref, low_ref, zed_ref, gm_ref, gh_ref, vec_ref,
    pre_ref, depth_ref, gk_ref, kb_ref, dpt_ref, dep_ref, cve_ref, el_ref, eh_ref, ex_ref,
    place_ref, out_ref, keep_ref, give_ref, tok_ref, scr, *, rim, quarter, taps,
):
    packs = (p0, p1, p2, p3)
    outs = (keep_ref.at[0], give_ref.at[0], keep_ref.at[1], give_ref.at[1])
    x_own = x_ref[...]
    ends_low, ends_high = el_ref[...], eh_ref[...]
    blank = jnp.zeros((128 - 8, 192), f32)
    first = jnp.transpose(jnp.concatenate([ends_low[:, 384:576], blank], axis=0), (1, 0))
    last = jnp.transpose(jnp.concatenate([blank, ends_high[:, 384:576]], axis=0), (1, 0))
    mp = place_ref[0]
    scr[0], scr[1] = first, last
    sides = (mp ^ ((mp + 3) & 3), mp ^ ((mp + 1) & 3))
    first, last = (
        jnp.concatenate(
            [scr[n, pl.ds(pl.multiple_of(48 * (side ^ s), 16), 48), :] for s in range(4)], axis=0
        )
        for n, side in enumerate(sides)
    )
    spread = cve_ref[:, rim : rim + quarter]
    spread = spread + jnp.concatenate(
        [first, jnp.zeros((192, quarter - 256), f32), last] if quarter > 256 else [first, last],
        axis=1,
    )
    gcv = spread.astype(bf16)
    grad_depth = dep_ref[...] + jnp.concatenate(
        [ends_low[:, 0:384], jnp.zeros((quarter - 16, 384), f32), ends_high[:, 0:384]], axis=0
    )
    wc = jnp.concatenate([pack[WC : WC + 48, :] for pack in packs], axis=0)
    extra = ex_ref[...]
    wq = jnp.concatenate([pack[WQ : WQ + 48, :] for pack in packs], axis=0)
    tok = dg(gcv, wc, 0, 0) + dg(extra, wq, 0, 0) + grad_depth + gh_ref[...]
    tok_ref[0] = tok.astype(bf16)
    tok_ref[1] = out_ref[...]
    g_query = dg(extra, x_own, 1, 0)
    q_bias = jnp.sum(extra.astype(f32), axis=1, keepdims=True)
    g_conv = dg(gcv, x_own, 1, 0)
    c_bias = jnp.sum(gcv.astype(f32), axis=1, keepdims=True)
    pre = pre_ref[...]
    g_point = dg(pre, depth_ref[...], 1, 0)
    p_bias = jnp.sum(pre.astype(f32), axis=1, keepdims=True)
    low, zed, gm = low_ref[...], zed_ref[...], gm_ref[...]
    lane = lax.broadcasted_iota(jnp.int32, (48, 128), 1)
    ones = jnp.ones((8, quarter), bf16)
    for s, out in enumerate(outs):
        own = slice(48 * s, 48 * s + 48)
        out[GP : GP + 48, :] = g_point[own].astype(bf16)
        out[GC : GC + 48, :] = g_conv[own].astype(bf16)
        out[GQ : GQ + 48, :] = g_query[own].astype(bf16)
        out[GO : GO + 96, :] = dg(a_ref[96 * s : 96 * s + 96, :], gm, 1, 0).astype(bf16)
        inner, outer, bias = [], [], []
        for g in range(2):
            lanes = slice(192 * g, 192 * g + 192)
            gpre = gpre_ref[2 * s + g]
            inner.append(dg(low[:, lanes], gpre, 0, 0))
            outer.append(dg(act_ref[2 * s + g], zed[:, lanes], 0, 0))
            bias.append(dg(ones, gpre, 1, 0)[0:1])
        out[GI : GI + 192, :] = jnp.concatenate(inner, axis=1).astype(bf16)
        out[GU : GU + 192, :] = jnp.concatenate(outer, axis=1).astype(bf16)
        tile = jnp.concatenate([gk_ref[s], jnp.zeros((48, 80), f32)], axis=1)
        tile = jnp.where(lane == 64, p_bias[own], tile)
        tile = jnp.where(lane == 65, c_bias[own], tile)
        tile = jnp.where(lane == 66, kb_ref[...], tile)
        tile = jnp.where(lane == 67, q_bias[own], tile)
        out[GM : GM + 48, 0:128] = tile.astype(bf16)
        out[GM : GM + 48, 128:384] = jnp.zeros((48, 256), bf16)
        bias = jnp.concatenate(bias, axis=1)
        lines = jnp.concatenate([bias, dpt_ref[0:taps, :], vec_ref[0:6, :]], axis=0)
        out[GV : GV + 16, :] = lines.astype(bf16)
        if out.shape[0] > GRAD_ROWS:
            out[GRAD_ROWS:, :] = jnp.zeros((out.shape[0] - GRAD_ROWS, 384), bf16)


def unpack_body(
    place_ref, own_ref, other_ref,
    point_ref, conv_ref, query_ref, out_ref, inner_ref, outer_ref, kernel_ref, bias_ref,
    ib_ref, dep_ref, vec_ref, scr, *, outer, rows, taps,
):
    x, z = place_ref[3], place_ref[4]
    for i in range(outer):
        at = pl.multiple_of((2 * (z ^ i) + x) * rows, 16)
        scr[pl.ds(at, rows), :] = own_ref[i].astype(f32)
        at = pl.multiple_of((2 * (z ^ i) + 1 - x) * rows, 16)
        scr[pl.ds(at, rows), :] = other_ref[i].astype(f32)
    point_ref[...] = scr[GP : GP + 48, :]
    conv_ref[...] = scr[GC : GC + 48, :]
    query_ref[...] = scr[GQ : GQ + 48, :]
    out_ref[0] = scr[GO : GO + 48, :]
    out_ref[1] = scr[GO + 48 : GO + 96, :]
    for g in range(2):
        lanes = slice(192 * g, 192 * g + 192)
        inner_ref[g] = scr[GI : GI + 192, lanes]
        outer_ref[g] = scr[GU : GU + 192, lanes]
        ib_ref[g : g + 1, :] = scr[GV : GV + 1, lanes]
    kernel_ref[...] = scr[GM : GM + 36, 0:48]
    turned = jnp.transpose(scr[GM : GM + 48, 0:128], (1, 0))
    bias_ref[...] = turned[64:72, :]
    dep_ref[...] = scr[GV + 1 : GV + 1 + taps, :]
    vec_ref[...] = scr[GV + 8 : GV + 16, :]


def head_weights_body(g_ref, x_ref, out_ref):
    grads = g_ref[...]
    out_ref[0:144, :] = dg(grads, x_ref[...], 1, 0).astype(bf16)
    out_ref[144:160, :] = jnp.zeros((16, 384), bf16)
    sums = dg(jnp.ones((16, grads.shape[1]), bf16), grads, 1, 1)
    out_ref[144:160, 0:144] = sums.astype(bf16)


def head_unpack_body(a_ref, b_ref, part_ref, bias_ref, q_ref, k_ref, v_ref, qb_ref, vb_ref):
    total = a_ref[...].astype(f32) + b_ref[...].astype(f32)
    q_ref[...] = total[0:48] + part_ref[...]
    k_ref[...] = total[48:96]
    v_ref[...] = total[96:144]
    qb_ref[...] = total[144:145, 0:48] + bias_ref[3:4, :]
    vb_ref[...] = total[144:145, 96:144]


def input_grad_body(
    place_ref, g0, g1, g2, g3, p0, p1, p2, p3, t0, t1, t2, t3, out_ref, *, quarter
):
    total = None
    for grads, pack in ((g0, p0), (g1, p1), (g2, p2), (g3, p3)):
        term = dg(grads[...], pack[WQ : WQ + 144, :], 0, 0)
        total = term if total is None else total + term
    out_ref[...] = total
    mp = place_ref[0]
    for s, ref in enumerate((t0, t1, t2, t3)):
        at = pl.multiple_of((mp ^ s) * quarter, quarter)
        out_ref[pl.ds(at, quarter), :] += ref[0].astype(f32)


def layer_out_body(place_ref, t0, t1, t2, t3, out_ref, *, quarter):
    mp = place_ref[0]
    for s, ref in enumerate((t0, t1, t2, t3)):
        at = pl.multiple_of((mp ^ s) * quarter, quarter)
        out_ref[pl.ds(at, quarter), :] = ref[1]


def local(
    inputs, w_query, b_query, w_key, w_value, b_value, depth_kernel, w_point, b_point, w_kernel,
    b_kernel, w_conv, b_conv, w_out, b_out, gain_one, shift_one, w_inner, b_inner, w_outer,
    b_outer, gain_two, shift_two, cotangent,
):
    blocks = lax.axis_size("ctx")
    outer = blocks // 2
    rows_here = inputs.shape[0]
    quarter = rows_here // 4
    taps = depth_kernel.shape[0]
    rim = 64
    ctx, mp = lax.axis_index("ctx"), lax.axis_index("mp")
    x_at, z_at = ctx % 2, ctx // 2
    place = jnp.stack(
        [mp, ctx * rows_here + mp * quarter, blocks * rows_here, x_at, z_at]
    ).astype(jnp.int32)
    turned_place = ((mp // 2) * 2 + x_at).astype(jnp.int32).reshape(1)

    def table(change):
        pairs = []
        for z in range(outer):
            for x in range(2):
                for y in range(2):
                    for c in range(2):
                        z2, x2, y2, c2 = change(z, x, y, c)
                        pairs.append(((2 * z + x) * 4 + 2 * y + c, (2 * z2 + x2) * 4 + 2 * y2 + c2))
        return pairs

    def send(value, change):
        return lax.ppermute(value, ("ctx", "mp"), table(change))

    def turn(z, x, y, c):
        return (z, c, y, x)

    def across_c(z, x, y, c):
        return (z, x, y, c ^ 1)

    def across_y(z, x, y, c):
        return (z, x, y ^ 1, c)

    def across_x(z, x, y, c):
        return (z, x ^ 1, y, c)

    def across_z(i):
        return lambda z, x, y, c: (z ^ i, x, y, c)

    def to_tokens(s):
        return lambda z, x, y, c: (z, c, y ^ (s >> 1), x ^ (s & 1))

    def to_heads(s):
        return lambda z, x, y, c: (z, c ^ (s & 1), y ^ (s >> 1), x)

    def gather_mp(value):
        beyond = send(value, across_y)
        return [value, send(value, across_c), beyond, send(beyond, across_c)]

    def line(vector):
        return vector.reshape(1, -1)

    def plus(left, right):
        return (left.astype(f32) + right.astype(f32)).astype(bf16)

    projected = call(
        project_body,
        [((144, rows_here), bf16)],
        [inputs, w_query.T, line(b_query), w_key.T, w_value.T, line(b_value)],
        flops=2 * rows_here * 384 * 144, byts=2**20,
    )[0]
    turned = send(projected, turn)
    kv, q = turned[0:96], turned[96:144]
    pack = call(
        pack_body,
        [((PACK_ROWS, 384), bf16)],
        [w_query.T, w_key.T, w_value.T, w_point.T, w_conv.T, w_out, w_inner, w_outer, w_kernel.T,
         line(b_query), line(b_point), line(b_conv), b_inner],
        flops=2 * 10**8, byts=2**20,
    )[0]
    packs = gather_mp(pack)

    up = [(i * 4 + m, (i + 1) * 4 + m) for i in range(blocks - 1) for m in range(4)]
    down = [(b, a) for a, b in up]
    before = lax.ppermute(inputs[rows_here - rim :], ("ctx", "mp"), up)
    after = lax.ppermute(inputs[:rim], ("ctx", "mp"), down)
    extended = jnp.concatenate([before, inputs, after], axis=0)
    x_ext = lax.dynamic_slice_in_dim(extended, mp * quarter, quarter + 2 * rim, 0)
    x_quarter = lax.dynamic_slice_in_dim(inputs, mp * quarter, quarter, 0)
    cot_quarter = lax.dynamic_slice_in_dim(cotangent, mp * quarter, quarter, 0)

    zkv = [kv] + [send(kv, across_z(i)) for i in range(1, outer)]
    skv = [send(item, across_c) for item in zkv]
    state = None
    for i in range(outer - 1):
        state = flash(q, [zkv[i], skv[i]], state)
    raw, lse, *chunks = flash(q, [zkv[outer - 1], skv[outer - 1]], state, turned_place)

    ext = quarter + 2 * rim
    mix, depth, q_conv, key_conv, tap_probs, conv_vals = call(
        functools.partial(conv_body, rim=rim, quarter=quarter, taps=taps),
        [((192, quarter), bf16), ((quarter, 384), bf16), ((192, quarter), bf16),
         ((192, quarter), f32), ((8 * taps, quarter), f32), ((192, ext), f32)],
        [place, x_ext, depth_kernel, line(b_kernel), *packs],
        flops=10**9, byts=2**21, smem=(0,),
    )

    heads = [send(chunk, to_tokens(s)) for s, chunk in enumerate(chunks)]
    blank = jnp.zeros((384,), f32)
    lines = jnp.stack(
        [b_out.astype(f32), gain_one, shift_one, b_outer.astype(f32), gain_two, shift_two]
        + [blank] * 2
    )
    (layer_quarter, c0, c1, c2, c3, grad_mix, both, act, gpre, low, zed, gm, grad_h1, vec) = call(
        feed_body,
        [((quarter, 384), bf16)] + [((48, quarter), bf16)] * 4
        + [((192, quarter), f32), ((384, quarter), bf16), ((8, quarter, 192), bf16),
           ((8, quarter, 192), bf16), ((quarter, 384), bf16), ((quarter, 384), bf16),
           ((quarter, 384), bf16), ((quarter, 384), f32), ((8, 384), f32)],
        [*heads, mix, *packs, x_quarter, cot_quarter, lines],
        flops=2 * 10**9, byts=2**22, scratch=[pltpu.VMEM((8, quarter, 192), f32)],
    )
    grads = [send(item, to_heads(s)) for s, item in enumerate((c0, c1, c2, c3))]

    extra, grad_kc, g_kernel, k_bias, g_depth, own_depth, spread, rim_low, rim_high = call(
        functools.partial(conv_back_body, rim=rim, quarter=quarter, taps=taps),
        [((192, quarter), bf16), ((192, quarter), bf16), ((4, 48, 48), f32), ((48, 128), f32),
         ((16, 384), f32), ((quarter, 384), f32), ((192, ext), f32), ((8, 576), f32),
         ((8, 576), f32)],
        [place, x_ext, depth_kernel, *packs, q_conv, key_conv, tap_probs, conv_vals, grad_mix],
        flops=10**9, byts=2**22, smem=(0,),
    )
    total = blocks * 4
    from_high = lax.ppermute(rim_low, ("ctx", "mp"), [(i + 1, i) for i in range(total - 1)])
    from_low = lax.ppermute(rim_high, ("ctx", "mp"), [(i, i + 1) for i in range(total - 1)])

    q_aug, grad_aug = call(
        back_prepare_body,
        [((112, rows_here), bf16), ((64, rows_here), bf16)],
        [turned_place, q, lse, raw, *grads],
        byts=2**20, smem=(0,),
    )

    chunk_rows = -(-GRAD_ROWS // (16 * blocks)) * 16
    all_rows = chunk_rows * blocks
    keep, give, token_part = call(
        functools.partial(weights_body, rim=rim, quarter=quarter, taps=taps),
        [((2, all_rows, 384), bf16)] * 2 + [((2, quarter, 384), bf16)],
        [x_quarter, *packs, both, act, gpre, low, zed, gm, grad_h1, vec, grad_kc, depth, g_kernel,
         k_bias, g_depth, own_depth, spread, from_low, from_high, extra, place, layer_quarter],
        flops=2 * 10**9, byts=2**22, smem=(23,), scratch=[pltpu.VMEM((2, 192, 128), f32)],
    )

    order = list(range(outer - 1, 0, -1)) + [0]
    dq = None
    others, finals = {}, []
    own_grads = None

    def own_step(i, dq):
        nonlocal own_grads
        dtype = f32 if i == 0 else bf16
        dq, part = back(q, q_aug, grad_aug, zkv[i], dq, others[i], dtype)
        if i == 0:
            own_grads = part
        else:
            finals.append(send(part, across_z(i)))
        return dq

    for n, i in enumerate(order):
        dq, part = back(q, q_aug, grad_aug, skv[i], dq, None, bf16)
        others[i] = send(part, across_c)
        if n >= 1:
            dq = own_step(order[n - 1], dq)
    dq = own_step(0, dq)

    given = send(give, across_c)
    beyond = send(plus(keep[1], given[1]), across_y)
    piece = plus(plus(keep[0], given[0]), beyond).reshape(outer, 2, chunk_rows, 384)
    given = send(lax.dynamic_index_in_dim(piece, 1 - x_at, 1, False), across_x)
    piece = plus(lax.dynamic_index_in_dim(piece, x_at, 1, False), given)
    bit = outer // 2
    while bit:
        piece = piece.reshape(2, bit, chunk_rows, 384)
        mine = (z_at // bit) % 2
        given = send(lax.dynamic_index_in_dim(piece, 1 - mine, 0, False), across_z(bit))
        piece = plus(lax.dynamic_index_in_dim(piece, mine, 0, False), given)
        bit //= 2
    bit = 1
    while bit < outer:
        piece = jnp.concatenate([piece, send(piece, across_z(bit))], axis=0)
        bit *= 2
    other_piece = send(piece, across_x)
    (point, conv, query_part, grad_out, grad_inner, grad_outer, kernel, biases, i_bias, grad_depth,
     vecs) = call(
        functools.partial(unpack_body, outer=outer, rows=chunk_rows, taps=taps),
        [((48, 384), f32)] * 3 + [((2, 48, 384), f32), ((2, 192, 192), f32),
         ((2, 192, 192), f32), ((36, 48), f32), ((8, 48), f32),
         ((2, 192), f32), ((taps, 384), f32), ((8, 384), f32)],
        [place, piece, other_piece], byts=2**21, smem=(0,),
        scratch=[pltpu.VMEM((all_rows, 384), f32)],
    )

    token_parts = gather_mp(token_part)
    layer_out = call(
        functools.partial(layer_out_body, quarter=quarter),
        [((rows_here, 384), bf16)],
        [place, *token_parts], byts=2**20, smem=(0,),
    )[0]

    joined = call(
        functools.partial(back_join_body, parts=len(finals)),
        [((144, rows_here), bf16)],
        [dq, own_grads, *finals], byts=2**20,
    )[0]
    head_grads = send(joined, turn)
    head_w = call(
        head_weights_body, [((160, 384), bf16)], [head_grads, inputs],
        flops=2 * rows_here * 384 * 144, byts=2**20,
    )[0]
    all_heads = gather_mp(head_grads)
    other_w = send(head_w, across_x)
    bit = 1
    while bit < outer:
        head_w = plus(head_w, other_w)
        other_w = send(head_w, across_z(bit))
        bit *= 2
    inputs_grad = call(
        functools.partial(input_grad_body, quarter=quarter),
        [((rows_here, 384), f32)],
        [place, *all_heads, *packs, *token_parts],
        flops=2 * rows_here * 384 * 576, byts=2**22, smem=(0,),
    )[0]
    query, key, value, q_bias, v_bias = call(
        head_unpack_body,
        [((48, 384), f32)] * 3 + [((1, 48), f32)] * 2,
        [head_w, other_w, query_part, biases], byts=2**20,
    )

    return (
        layer_out, inputs_grad, query.T, q_bias.reshape(-1), key.T, value.T, v_bias.reshape(-1),
        grad_depth, point.T, biases[0], kernel.T, biases[2, 0:36], conv.T, biases[1], grad_out,
        vecs[2], vecs[3], vecs[4], grad_inner, i_bias, grad_outer, vecs[5], vecs[6], vecs[7],
    )


def solution(mesh):
    return jax.shard_map(
        local,
        mesh=mesh,
        in_specs=(
            P("ctx", None), P(None, "mp"), P("mp"), P(None, "mp"), P(None, "mp"), P("mp"), P(),
            P(None, "mp"), P("mp"), P("mp", None), P(), P(None, "mp"), P("mp"),
            P(None, "mp", None), P(), P(), P(), P(None, None, "mp"), P(None, "mp"),
            P(None, "mp", None), P(), P(), P(), P("ctx", None),
        ),
        out_specs=(
            P("ctx", None), P("ctx", None), P(None, "mp"), P("mp"), P(None, "mp"), P(None, "mp"),
            P("mp"), P(), P(None, "mp"), P("mp"), P("mp", None), P(), P(None, "mp"), P("mp"),
            P(None, "mp", None), P(), P(), P(), P(None, None, "mp"), P(None, "mp"),
            P(None, "mp", None), P(), P(), P(),
        ),
        check_vma=False,
    )
```

```python
import functools
import math

import jax
import jax.numpy as jnp
from jax import lax
from jax.experimental import pallas as pl
from jax.experimental.pallas import tpu as pltpu
from jax.sharding import PartitionSpec as P


EPSILON = 1e-12
KERNEL_BYTES = 24 * 2**20
PACE = 0.02e9
f32 = jnp.float32
bf16 = jnp.bfloat16

WQ, WK, WV, WP, WC, WO, WI, WU, WM, WB = 0, 48, 96, 144, 192, 240, 336, 528, 720, 768
PACK_ROWS = 784
GP, GC, GQ, GO, GI, GU, GM, GV = 0, 48, 96, 144, 240, 432, 624, 672
GRAD_ROWS = 688


def dg(left, right, ld, rd):
    return lax.dot_general(
        left, right, (((ld,), (rd,)), ((), ())), preferred_element_type=f32
    )


def outer_ones(row, width):
    return dg(row, jnp.ones((row.shape[0], width), bf16), 0, 0)


def call(body, outs, args, us, scratch=(), smem=(), after=(), final=()):
    inputs = len(args)

    def whole(*refs):
        body(*refs[:inputs], *refs[inputs + len(after) :])

    specs = [
        pl.BlockSpec(memory_space=pltpu.SMEM if i in smem else pltpu.VMEM) for i in range(inputs)
    ]
    return pl.pallas_call(
        whole,
        in_specs=specs + [pl.BlockSpec(memory_space=pl.ANY)] * len(after),
        out_specs=[pl.BlockSpec(memory_space=pltpu.VMEM)] * len(outs),
        out_shape=[
            jax.ShapeDtypeStruct(s, d) if i in final else pltpu.VMEM(s, d)
            for i, (s, d) in enumerate(outs)
        ],
        scratch_shapes=list(scratch),
        compiler_params=pltpu.CompilerParams(vmem_limit_bytes=KERNEL_BYTES),
        cost_estimate=pl.CostEstimate(flops=int(us * PACE), bytes_accessed=0, transcendentals=0),
    )(
        *(
            arg if i in smem else pltpu.with_memory_space_constraint(arg, pltpu.VMEM)
            for i, arg in enumerate(args)
        ),
        *after,
    )


def project_body(x_ref, wq_ref, bq_ref, wk_ref, wv_ref, bv_ref, out_ref):
    x = x_ref[...]
    width = x.shape[0]
    weights = jnp.concatenate([wk_ref[...], wv_ref[...], wq_ref[...]], axis=0)
    found = dg(weights, x, 1, 1)
    out_ref[0:48, :] = found[0:48].astype(bf16)
    out_ref[48:96, :] = (found[48:96] + outer_ones(bv_ref[...], width)).astype(bf16)
    out_ref[96:144, :] = (found[96:144] + outer_ones(bq_ref[...], width)).astype(bf16)


def pack_body(
    wq_ref, wk_ref, wv_ref, wp_ref, wc_ref, wo_ref, wi_ref, wu_ref, wm_ref,
    bq_ref, bp_ref, bc_ref, bi_ref, out_ref,
):
    for at, ref in ((WQ, wq_ref), (WK, wk_ref), (WV, wv_ref), (WP, wp_ref), (WC, wc_ref)):
        out_ref[at : at + 48, :] = ref[...]
    out_ref[WO : WO + 48, :] = wo_ref[0]
    out_ref[WO + 48 : WO + 96, :] = wo_ref[1]
    out_ref[WI : WI + 192, :] = jnp.concatenate([wi_ref[0], wi_ref[1]], axis=1)
    out_ref[WU : WU + 192, :] = jnp.concatenate([wu_ref[0], wu_ref[1]], axis=1)
    out_ref[WM : WM + 64, :] = jnp.zeros((64, 384), bf16)
    out_ref[WM : WM + 36, 0:48] = wm_ref[...]
    zeros = jnp.zeros((1, 336), f32)
    lines = [jnp.concatenate([bi_ref[0:1].astype(f32), bi_ref[1:2].astype(f32)], axis=1)]
    for ref in (bq_ref, bp_ref, bc_ref):
        lines.append(jnp.concatenate([ref[...].astype(f32), zeros], axis=1))
    lines.append(jnp.zeros((12, 384), f32))
    out_ref[WB : WB + 16, :] = jnp.concatenate(lines, axis=0).astype(bf16)


def keys_aug(kv):
    keys = kv[0:48]
    return jnp.concatenate([keys, keys, jnp.ones((16, keys.shape[1]), bf16)], axis=0)


def vals_aug(kv):
    vals = kv[48:96]
    return jnp.concatenate([vals, jnp.ones((16, vals.shape[1]), bf16)], axis=0)


def split3(value):
    high = value.astype(bf16)
    rest = value - high.astype(f32)
    mid = rest.astype(bf16)
    low = (rest - mid.astype(f32)).astype(bf16)
    return high, mid, low


def scaled_queries(q):
    scaled = q.astype(f32) * (math.log2(math.e) / math.sqrt(48.0))
    high = scaled.astype(bf16)
    low = (scaled - high.astype(f32)).astype(bf16)
    return high, low


def flash_body(*refs, first, last, blocks):
    refs = list(refs)
    q_ref = refs.pop(0)
    tp_ref = refs.pop(0) if last else None
    kv_refs = [refs.pop(0) for _ in range(blocks)]
    if first:
        m_out, acc_out = refs
        m_now = acc_now = None
    else:
        m_in, acc_in = refs.pop(0), refs.pop(0)
        m_now, acc_now = m_in[0:1, :], acc_in[...]
    q = q_ref[96:144, :]
    width = q.shape[1]
    high, low = scaled_queries(q)
    q_aug = jnp.concatenate([high, low, jnp.zeros((16, width), bf16)], axis=0)
    for kv_ref in [q_ref] + kv_refs if first else kv_refs:
        kv = kv_ref[0:96, :]
        scores = dg(keys_aug(kv), q_aug, 0, 0)
        top = jnp.max(scores, axis=0, keepdims=True)
        m_new = top if m_now is None else jnp.maximum(m_now, top)
        probs = jnp.exp2(scores - m_new).astype(bf16)
        part = dg(vals_aug(kv), probs, 1, 0)
        acc_now = part if m_now is None else acc_now * jnp.exp2(m_now - m_new) + part
        m_now = m_new
    if not last:
        if not first:
            m_out, acc_out = refs
        m_out[...] = jnp.broadcast_to(m_now, (8, width))
        acc_out[...] = acc_now
        return
    raw_ref, lse_ref, *sends, low_scr = refs
    total = acc_now[48:49, :]
    raw = acc_now[0:48, :] / total
    raw_ref[...] = raw
    lse_ref[...] = jnp.broadcast_to(m_now + jnp.log2(total), (8, width))
    low_scr[...] = raw.astype(bf16)
    quarter = width // 4
    place = tp_ref[0]
    for s, send in enumerate(sends):
        at = pl.multiple_of((place ^ s) * quarter, quarter)
        send[...] = low_scr[:, pl.ds(at, quarter)]


def flash(q, kvs, state, place=None, after=()):
    width = q.shape[1]
    first, last = state is None, place is not None
    args = [q] + ([place] if last else []) + list(kvs) + ([] if first else list(state))
    if last:
        outs = [((48, width), f32), ((8, width), f32)] + [((48, width // 4), bf16)] * 4
        scratch = [pltpu.VMEM((48, width), bf16)]
    else:
        outs, scratch = [((8, width), f32), ((64, width), f32)], []
    return call(
        functools.partial(flash_body, first=first, last=last, blocks=len(kvs)),
        outs, args, us=2.4 * len(kvs) + 2.4 * first, scratch=scratch, smem=(1,) if last else (), after=after,
    )


def back_prepare_body(place_ref, q_ref, lse_ref, raw_ref, g0, g1, g2, g3, qa_ref, da_ref):
    q = q_ref[96:144, :]
    width = q.shape[1]
    quarter = width // 4
    high, low = scaled_queries(q)
    lines = split3(-lse_ref[0:1, :])
    pad = jnp.zeros((13, width), bf16)
    qa_ref[...] = jnp.concatenate([high, low, *lines, pad], axis=0)
    place = place_ref[0]
    for s, ref in enumerate((g0, g1, g2, g3)):
        at = pl.multiple_of((place ^ s) * quarter, quarter)
        da_ref[0:48, pl.ds(at, quarter)] = ref[...]
    grad = da_ref[0:48, :]
    delta = jnp.sum(grad.astype(f32) * raw_ref[...], axis=0, keepdims=True)
    da_ref[48:64, :] = jnp.concatenate([*split3(-delta), pad], axis=0)


def back_body(*refs, first, blocks, plus, split):
    refs = list(refs)
    q_ref, qa_ref, da_ref = refs[:3]
    kv_refs = refs[3 : 3 + blocks]
    refs = refs[3 + blocks :]
    dq_in = None if first else refs.pop(0)
    plus_ref = refs.pop(0) if plus else None
    dq_out, *outs = refs
    if not split:
        outs = [outs[0].at[n] for n in range(blocks)]
    q, grad = q_ref[96:144, :], da_ref[0:48, :]
    q_aug, grad_aug = qa_ref[...], da_ref[...]
    step = 256
    dq = None if first else dq_in[...]
    for n, (kv_ref, out) in enumerate(zip(kv_refs, outs, strict=True)):
        kv = kv_ref[...]
        keys, vals = keys_aug(kv), vals_aug(kv)
        for at in range(0, kv.shape[1], step):
            span = slice(at, at + step)
            probs = jnp.exp2(dg(keys[:, span], q_aug, 0, 0))
            grad_probs = dg(vals[:, span], grad_aug, 0, 0)
            grad_scores = (probs * grad_probs).astype(bf16)
            dv = dg(grad, probs.astype(bf16), 1, 1)
            dk = dg(q, grad_scores, 1, 1)
            part = dg(kv[0:48, span], grad_scores, 1, 0)
            dq = part if dq is None else dq + part
            both = jnp.concatenate([dk, dv], axis=0)
            if plus:
                both = both + plus_ref[n, :, span].astype(f32)
            out[:, span] = both.astype(out.dtype)
    dq_out[...] = dq


def back(q, q_aug, grad_aug, kvs, dq, plus, out_dtypes, after=()):
    width = q.shape[1]
    shape = kvs[0].shape
    args = [q, q_aug, grad_aug, *kvs] + ([] if dq is None else [dq])
    args += [] if plus is None else [plus]
    outs = [((len(kvs), *shape), bf16)] if plus is None else [(shape, d) for d in out_dtypes]
    dq, *parts = call(
        functools.partial(
            back_body, first=dq is None, blocks=len(kvs), plus=plus is not None,
            split=plus is not None,
        ),
        [((48, width), f32), *outs], args, us=3.5 * len(kvs), after=after,
    )
    return dq, parts


def back_join_body(place_ref, dq_ref, dkv_ref, *refs, parts):
    news, (out_ref, *sends) = refs[:parts], refs[parts:]
    scale = 1.0 / math.sqrt(48.0)
    out_ref[0:48, :] = (dq_ref[...] * scale).astype(bf16)
    total = dkv_ref[...]
    for ref in news:
        total = total + ref[...].astype(f32)
    out_ref[48:96, :] = (total[0:48] * scale).astype(bf16)
    out_ref[96:144, :] = total[48:96].astype(bf16)
    quarter = dq_ref.shape[1] // 4
    place = place_ref[0]
    for s, send in enumerate(sends):
        at = pl.multiple_of((place ^ s) * quarter, quarter)
        send[...] = out_ref[:, pl.ds(at, quarter)]


def tap_places(mp, heads, taps):
    rows = lax.broadcasted_iota(jnp.int32, (48, 8 * taps), 0)
    cols = lax.broadcasted_iota(jnp.int32, (48, 8 * taps), 1)
    s = cols & 7
    wanted = (s ^ mp) * taps + (cols >> 3)
    return ((rows == wanted) & (s < heads)).astype(f32).astype(bf16)


def lift(value, axis, shift, keep):
    size = value.shape[axis]
    rolled = pltpu.roll(value, (size - shift) % size, axis)
    return rolled[:keep] if axis == 0 else rolled[:, :keep]


def conv_body(
    place_ref, xe_ref, dk_ref, bk_ref, p0, p1, p2, p3,
    mix_ref, depth_ref, q_ref, kc_ref, tp_ref, cv_ref, *, rim, quarter, taps,
):
    packs = (p0, p1, p2, p3)
    xe = xe_ref[...]
    x_own = xe[rim : rim + quarter]
    wide = xe.astype(f32)
    reach = taps // 2
    kernel = dk_ref[...].astype(f32)
    depth = None
    for j in range(taps):
        term = lift(wide, 0, rim - reach + j, quarter) * kernel[j : j + 1, :]
        depth = term if depth is None else depth + term
    depth_low = depth.astype(bf16)
    depth_ref[...] = depth_low
    position = place_ref[1] + lax.broadcasted_iota(jnp.int32, (1, xe.shape[0]), 1) - rim
    inside = (position >= 0) & (position < place_ref[2])
    attn = []
    for s, pack in enumerate(packs):
        own = slice(48 * s, 48 * s + 48)
        q = (
            dg(pack[WQ : WQ + 48, :], x_own, 1, 1)
            + outer_ones(pack[WB + 1 : WB + 2, 0:48], quarter)
        ).astype(bf16)
        kc = dg(pack[WP : WP + 48, :], depth_low, 1, 1) + outer_ones(
            pack[WB + 2 : WB + 3, 0:48], quarter
        )
        cv = dg(pack[WC : WC + 48, :], xe, 1, 1) + outer_ones(
            pack[WB + 3 : WB + 4, 0:48], xe.shape[0]
        )
        q_ref[own, :] = q
        kc_ref[own, :] = kc
        cv_ref[own, :] = jnp.where(inside, cv, 0.0)
        attn.append((kc * q.astype(f32)).astype(bf16))
    attn = jnp.concatenate(attn, axis=0)
    hot = tap_places(place_ref[0], 4, taps)
    wk = [dg(pack[WM : WM + 48, 0:48], hot, 0, 0) for pack in packs]
    wk = jnp.concatenate(wk, axis=0).astype(bf16)
    bias = dg(bk_ref[...], hot[0 : bk_ref.shape[1], :], 1, 0).astype(bf16)
    logits = dg(wk, attn, 0, 0) + outer_ones(bias, quarter)
    tiles = [logits[8 * j : 8 * j + 8] for j in range(taps)]
    top = functools.reduce(jnp.maximum, tiles)
    tiles = [jnp.exp(tile - top) for tile in tiles]
    total = functools.reduce(jnp.add, tiles)
    tiles = [tile / total for tile in tiles]
    for j in range(taps):
        tp_ref[8 * j : 8 * j + 8, :] = tiles[j]
    cv = cv_ref[...]
    mix = [None] * 4
    for j in range(taps):
        moved = lift(cv, 1, rim - reach + j, quarter)
        for s in range(4):
            term = tiles[j][s : s + 1, :] * moved[48 * s : 48 * s + 48]
            mix[s] = term if mix[s] is None else mix[s] + term
    for s in range(4):
        mix_ref[48 * s : 48 * s + 48, :] = mix[s].astype(bf16)


def conv_back_body(
    place_ref, xe_ref, dk_ref, p0, p1, p2, p3, q_ref, kc_ref, tp_ref, cv_ref, gm_ref, gh_ref,
    ex_ref, pre_ref, gk_ref, kb_ref, dpt_ref, cve_ref, tok_ref, edge_ref,
    *, rim, quarter, taps,
):
    packs = (p0, p1, p2, p3)
    reach = taps // 2
    ext = xe_ref.shape[0]
    grad_mix = gm_ref[...]
    cv = cv_ref[...]
    probs = [tp_ref[8 * j : 8 * j + 8, :] for j in range(taps)]
    grads = []
    weighted = None
    for j in range(taps):
        moved = lift(cv, 1, rim - reach + j, quarter) * grad_mix
        lines = [jnp.sum(moved[48 * s : 48 * s + 48], axis=0, keepdims=True) for s in range(4)]
        tile = jnp.concatenate(lines + [jnp.zeros((4, quarter), f32)], axis=0)
        grads.append(tile)
        term = probs[j] * tile
        weighted = term if weighted is None else weighted + term
    gtl = jnp.concatenate(
        [probs[j] * (grads[j] - weighted) for j in range(taps)], axis=0
    ).astype(bf16)
    hot = tap_places(place_ref[0], 4, taps)
    wk = [dg(pack[WM : WM + 48, 0:48], hot, 0, 0) for pack in packs]
    wk = jnp.concatenate(wk, axis=0).astype(bf16)
    q = q_ref[...].astype(f32)
    kc = kc_ref[...]
    attn = (kc * q).astype(bf16)
    plain = dg(hot, gtl, 1, 0).astype(bf16)
    for s in range(4):
        gk_ref[s] = dg(plain, attn[48 * s : 48 * s + 48], 1, 1)
    kb_ref[...] = dg(plain, jnp.ones((128, quarter), bf16), 1, 1)
    grad_attn = dg(wk, gtl, 1, 0)
    extra = (grad_attn * kc).astype(bf16)
    ex_ref[...] = extra
    grad_kc = (grad_attn * q).astype(bf16)
    pre_ref[...] = grad_kc
    wp = jnp.concatenate([pack[WP : WP + 48, :] for pack in packs], axis=0)
    dvals = dg(grad_kc, wp, 0, 0)
    wide = xe_ref[...].astype(f32)
    kernel = dk_ref[...].astype(f32)
    tail = jnp.zeros((ext - quarter, dvals.shape[1]), f32)
    padded = jnp.concatenate([dvals, tail], axis=0)
    depth = None
    lines = []
    for j in range(taps):
        moved = lift(wide, 0, rim - reach + j, quarter)
        lines.append(jnp.sum(moved * dvals, axis=0, keepdims=True))
        term = pltpu.roll(padded, rim - reach + j, 0) * kernel[j : j + 1, :]
        depth = term if depth is None else depth + term
    lines.append(jnp.zeros((16 - taps, dvals.shape[1]), f32))
    dpt_ref[...] = jnp.concatenate(lines, axis=0)
    side = jnp.zeros((4 * 48, ext - quarter), f32)
    spread = None
    for j in range(taps):
        rows = [probs[j][s : s + 1, :] * grad_mix[48 * s : 48 * s + 48] for s in range(4)]
        full = jnp.concatenate([jnp.concatenate(rows, axis=0), side], axis=1)
        term = pltpu.roll(full, rim - reach + j, 1)
        spread = term if spread is None else spread + term
    position = place_ref[1] + lax.broadcasted_iota(jnp.int32, (1, ext), 1) - rim
    inside = (position >= 0) & (position < place_ref[2])
    spread = jnp.where(inside, spread, 0.0).astype(bf16)
    cve_ref[...] = spread
    wc = jnp.concatenate([pack[WC : WC + 48, :] for pack in packs], axis=0)
    wq = jnp.concatenate([pack[WQ : WQ + 48, :] for pack in packs], axis=0)
    tokens = depth + dg(spread, wc, 0, 0)
    own = dg(extra, wq, 0, 0) + gh_ref[...]
    end = rim + quarter
    tok_ref[0:16, :] = tokens[rim - 16 : rim].astype(bf16)
    tok_ref[16 : quarter + 16, :] = (tokens[rim:end] + own).astype(bf16)
    tok_ref[quarter + 16 :, :] = tokens[end : end + 16].astype(bf16)
    edge_ref[...] = jnp.where(place_ref[0] == 0, tokens[rim - 16 : rim], tokens[end : end + 16])


def norm(hidden):
    centred = hidden - jnp.mean(hidden, axis=-1, keepdims=True)
    inverse = lax.rsqrt(jnp.mean(centred * centred, axis=-1, keepdims=True) + EPSILON)
    return centred * inverse, inverse


def norm_back(grad, normed, inverse, gain):
    scaled = grad * gain
    return inverse * (
        scaled
        - jnp.mean(scaled, axis=-1, keepdims=True)
        - normed * jnp.mean(scaled * normed, axis=-1, keepdims=True)
    )


def feed_body(
    r0, r1, r2, r3, mix_ref, p0, p1, p2, p3, x_ref, cot_ref, lines_ref,
    out_ref, c0, c1, c2, c3, gmix_ref, a_ref, act_ref, gpre_ref, low_ref, zed_ref, gm_ref,
    gh_ref, vec_ref, slope_scr,
):
    packs = (p0, p1, p2, p3)
    both = []
    for s, ref in enumerate((r0, r1, r2, r3)):
        both += [ref[...], mix_ref[48 * s : 48 * s + 48, :]]
    both = jnp.concatenate(both, axis=0)
    a_ref[...] = both
    w_out = jnp.concatenate([pack[WO : WO + 96, :] for pack in packs], axis=0)
    mixed = dg(both, w_out, 0, 0) + lines_ref[0:1, :]
    normed1, inverse1 = norm(mixed + x_ref[...].astype(f32))
    gain1, gain2 = lines_ref[1:2, :], lines_ref[4:5, :]
    low = (normed1 * gain1 + lines_ref[2:3, :]).astype(bf16)
    low_ref[...] = low
    halves = [low[:, 0:192], low[:, 192:384]]
    outer = [None, None]
    for g in range(2):
        lanes = slice(192 * g, 192 * g + 192)
        for s, pack in enumerate(packs):
            pre = dg(halves[g], pack[WI : WI + 192, lanes], 1, 0)
            pre = pre + pack[WB : WB + 1, lanes].astype(f32)
            cdf = 0.5 * (1.0 + lax.erf(pre * math.sqrt(0.5)))
            pdf = jnp.exp(-0.5 * pre * pre) * (1.0 / math.sqrt(2.0 * math.pi))
            slope_scr[2 * s + g] = cdf + pre * pdf
            act = (pre * cdf).astype(bf16)
            act_ref[2 * s + g] = act
            term = dg(act, pack[WU : WU + 192, lanes], 1, 0)
            outer[g] = term if outer[g] is None else outer[g] + term
    outer = jnp.concatenate(outer, axis=1) + lines_ref[3:4, :]
    normed2, inverse2 = norm(outer + low.astype(f32))
    out_ref[...] = (normed2 * gain2 + lines_ref[5:6, :]).astype(bf16)
    cot = cot_ref[...].astype(f32)
    grad_h2 = norm_back(cot, normed2, inverse2, gain2)
    zed = grad_h2.astype(bf16)
    zed_ref[...] = zed
    halves = [zed[:, 0:192], zed[:, 192:384]]
    back = [None, None]
    for g in range(2):
        lanes = slice(192 * g, 192 * g + 192)
        for s, pack in enumerate(packs):
            grad_act = dg(halves[g], pack[WU : WU + 192, lanes], 1, 1)
            gpre = (grad_act * slope_scr[2 * s + g]).astype(bf16)
            gpre_ref[2 * s + g] = gpre
            term = dg(gpre, pack[WI : WI + 192, lanes], 1, 1)
            back[g] = term if back[g] is None else back[g] + term
    grad_norm1 = jnp.concatenate(back, axis=1) + grad_h2
    grad_h1 = norm_back(grad_norm1, normed1, inverse1, gain1)
    gh_ref[...] = grad_h1
    gm = grad_h1.astype(bf16)
    gm_ref[...] = gm
    grads = dg(w_out, gm, 1, 1)
    for s, ref in enumerate((c0, c1, c2, c3)):
        ref[...] = grads[96 * s : 96 * s + 48].astype(bf16)
        gmix_ref[48 * s : 48 * s + 48, :] = grads[96 * s + 48 : 96 * s + 96]
    sums = [gm.astype(f32), grad_norm1 * normed1, grad_norm1, zed.astype(f32), cot * normed2, cot]
    lines = [jnp.sum(item, axis=0, keepdims=True) for item in sums]
    lines.append(jnp.zeros((2, 384), f32))
    vec_ref[...] = jnp.concatenate(lines, axis=0)


def weights_body(
    x_ref, xe_ref, a_ref, act_ref, gpre_ref, low_ref, zed_ref, gm_ref, vec_ref,
    pre_ref, depth_ref, gk_ref, kb_ref, dpt_ref, cve_ref, ex_ref, keep_ref, give_ref,
    *, quarter, taps,
):
    outs = (keep_ref.at[0], give_ref.at[0], keep_ref.at[1], give_ref.at[1])
    x_own = x_ref[...]
    extra, spread = ex_ref[...], cve_ref[...]
    g_query = dg(extra, x_own, 1, 0)
    q_bias = jnp.sum(extra.astype(f32), axis=1, keepdims=True)
    g_conv = dg(spread, xe_ref[...], 1, 0)
    c_bias = jnp.sum(spread.astype(f32), axis=1, keepdims=True)
    pre = pre_ref[...]
    g_point = dg(pre, depth_ref[...], 1, 0)
    p_bias = jnp.sum(pre.astype(f32), axis=1, keepdims=True)
    low, zed, gm = low_ref[...], zed_ref[...], gm_ref[...]
    lane = lax.broadcasted_iota(jnp.int32, (48, 128), 1)
    ones = jnp.ones((8, quarter), bf16)
    for s, out in enumerate(outs):
        own = slice(48 * s, 48 * s + 48)
        out[GP : GP + 48, :] = g_point[own].astype(bf16)
        out[GC : GC + 48, :] = g_conv[own].astype(bf16)
        out[GQ : GQ + 48, :] = g_query[own].astype(bf16)
        out[GO : GO + 96, :] = dg(a_ref[96 * s : 96 * s + 96, :], gm, 1, 0).astype(bf16)
        inner, outer, bias = [], [], []
        for g in range(2):
            lanes = slice(192 * g, 192 * g + 192)
            gpre = gpre_ref[2 * s + g]
            inner.append(dg(low[:, lanes], gpre, 0, 0))
            outer.append(dg(act_ref[2 * s + g], zed[:, lanes], 0, 0))
            bias.append(dg(ones, gpre, 1, 0)[0:1])
        out[GI : GI + 192, :] = jnp.concatenate(inner, axis=1).astype(bf16)
        out[GU : GU + 192, :] = jnp.concatenate(outer, axis=1).astype(bf16)
        tile = jnp.concatenate([gk_ref[s], jnp.zeros((48, 80), f32)], axis=1)
        tile = jnp.where(lane == 64, p_bias[own], tile)
        tile = jnp.where(lane == 65, c_bias[own], tile)
        tile = jnp.where(lane == 66, kb_ref[...], tile)
        tile = jnp.where(lane == 67, q_bias[own], tile)
        out[GM : GM + 48, 0:128] = tile.astype(bf16)
        out[GM : GM + 48, 128:384] = jnp.zeros((48, 256), bf16)
        bias = jnp.concatenate(bias, axis=1)
        lines = jnp.concatenate([bias, dpt_ref[0:taps, :], vec_ref[0:6, :]], axis=0)
        out[GV : GV + 16, :] = lines.astype(bf16)
        if out.shape[0] > GRAD_ROWS:
            out[GRAD_ROWS:, :] = jnp.zeros((out.shape[0] - GRAD_ROWS, 384), bf16)


def unpack_body(
    place_ref, own_ref, other_ref,
    point_ref, conv_ref, query_ref, out_ref, inner_ref, outer_ref, kernel_ref, qb_ref, ib_ref,
    dep_ref, pb_ref, cb_ref, kb_ref, *refs, taps,
):
    *vec_refs, scr = refs
    x = place_ref[3]
    half = own_ref.shape[0]
    scr[pl.ds(pl.multiple_of(x * half, 16), half), :] = own_ref[...].astype(f32)
    scr[pl.ds(pl.multiple_of((1 - x) * half, 16), half), :] = other_ref[...].astype(f32)
    point_ref[...] = scr[GP : GP + 48, :]
    conv_ref[...] = scr[GC : GC + 48, :]
    query_ref[...] = scr[GQ : GQ + 48, :]
    out_ref[0] = scr[GO : GO + 48, :]
    out_ref[1] = scr[GO + 48 : GO + 96, :]
    for g in range(2):
        lanes = slice(192 * g, 192 * g + 192)
        inner_ref[g] = scr[GI : GI + 192, lanes]
        outer_ref[g] = scr[GU : GU + 192, lanes]
        ib_ref[g : g + 1, :] = scr[GV : GV + 1, lanes]
    kernel_ref[...] = scr[GM : GM + 36, 0:48]
    turned = jnp.transpose(scr[GM : GM + 48, 0:128], (1, 0))
    pb_ref[...] = turned[64]
    cb_ref[...] = turned[65]
    kb_ref[...] = turned[66, 0:36]
    qb_ref[...] = turned[64:72, :]
    dep_ref[...] = scr[GV + 1 : GV + 1 + taps, :]
    for n, ref in enumerate(vec_refs):
        ref[...] = scr[GV + 1 + taps + n, :]


def head_weights_body(g_ref, x_ref, out_ref):
    grads = g_ref[...]
    out_ref[0:144, :] = dg(grads, x_ref[...], 1, 0).astype(bf16)
    out_ref[144:160, :] = jnp.zeros((16, 384), bf16)
    sums = dg(jnp.ones((16, grads.shape[1]), bf16), grads, 1, 1)
    out_ref[144:160, 0:144] = sums.astype(bf16)


def head_unpack_body(total_ref, part_ref, bias_ref, q_ref, k_ref, v_ref, qb_ref, vb_ref):
    total = total_ref[...].astype(f32)
    q_ref[...] = total[0:48] + part_ref[...]
    k_ref[...] = total[48:96]
    v_ref[...] = total[96:144]
    qb_ref[...] = total[144, 0:48] + bias_ref[3, :]
    vb_ref[...] = total[144, 96:144]


def input_grad_body(g0, g1, g2, g3, p0, p1, p2, p3, tok_ref, out_ref, *, quarter):
    total = None
    for grads, pack in ((g0, p0), (g1, p1), (g2, p2), (g3, p3)):
        term = dg(grads[...], pack[WQ : WQ + 144, :], 0, 0)
        total = term if total is None else total + term
    out_ref[0:16, :] = tok_ref[0:16, :]
    out_ref[16 : quarter + 16, :] = (
        total + tok_ref[16 : quarter + 16, :].astype(f32)
    ).astype(bf16)
    out_ref[quarter + 16 :, :] = tok_ref[quarter + 16 :, :]


def input_join_body(place_ref, t0, t1, t2, t3, out_ref, scr, *, quarter):
    mp = place_ref[0]
    parts = (t0, t1, t2, t3)
    for s, ref in enumerate(parts):
        at = pl.multiple_of((mp ^ s) * quarter, quarter)
        scr[pl.ds(at + 16, quarter), :] = ref[16 : quarter + 16, :].astype(f32)
    for s, ref in enumerate(parts):
        at = pl.multiple_of((mp ^ s) * quarter, quarter)
        scr[pl.ds(at, 16), :] += ref[0:16, :].astype(f32)
        scr[pl.ds(at + quarter + 16, 16), :] += ref[quarter + 16 :, :].astype(f32)
    out_ref[...] = scr[16 : 4 * quarter + 16, :]


def layer_out_body(place_ref, t0, t1, t2, t3, out_ref, *, quarter):
    mp = place_ref[0]
    for s, ref in enumerate((t0, t1, t2, t3)):
        at = pl.multiple_of((mp ^ s) * quarter, quarter)
        out_ref[pl.ds(at, quarter), :] = ref[...]


def local(
    inputs, w_query, b_query, w_key, w_value, b_value, depth_kernel, w_point, b_point, w_kernel,
    b_kernel, w_conv, b_conv, w_out, b_out, gain_one, shift_one, w_inner, b_inner, w_outer,
    b_outer, gain_two, shift_two, cotangent,
):
    blocks = lax.axis_size("ctx")
    outer = blocks // 2
    rows_here = inputs.shape[0]
    quarter = rows_here // 4
    taps = depth_kernel.shape[0]
    rim = 64
    ctx, mp = lax.axis_index("ctx"), lax.axis_index("mp")
    x_at, z_at = ctx % 2, ctx // 2
    place = jnp.stack(
        [mp, ctx * rows_here + mp * quarter, blocks * rows_here, x_at, z_at]
    ).astype(jnp.int32)
    turned_place = ((mp // 2) * 2 + x_at).astype(jnp.int32).reshape(1)

    def table(change):
        pairs = []
        for z in range(outer):
            for x in range(2):
                for y in range(2):
                    for c in range(2):
                        z2, x2, y2, c2 = change(z, x, y, c)
                        pairs.append(((2 * z + x) * 4 + 2 * y + c, (2 * z2 + x2) * 4 + 2 * y2 + c2))
        return pairs

    def send(value, change):
        return lax.ppermute(value, ("ctx", "mp"), table(change))

    def turn(z, x, y, c):
        return (z, c, y, x)

    def across_c(z, x, y, c):
        return (z, x, y, c ^ 1)

    def across_y(z, x, y, c):
        return (z, x, y ^ 1, c)

    def across_x(z, x, y, c):
        return (z, x ^ 1, y, c)

    def across_z(i):
        return lambda z, x, y, c: (z ^ i, x, y, c)

    def to_tokens(s):
        return lambda z, x, y, c: (z, c, y ^ (s >> 1), x ^ (s & 1))

    def to_heads(s):
        return lambda z, x, y, c: (z, c ^ (s & 1), y ^ (s >> 1), x)

    def gather_mp(value):
        beyond = send(value, across_y)
        return [value, send(value, across_c), beyond, send(beyond, across_c)]

    def line(vector):
        return vector.reshape(1, -1)

    def plus(left, right):
        return (left.astype(f32) + right.astype(f32)).astype(bf16)

    def plus(left, right):
        return (left.astype(f32) + right.astype(f32)).astype(bf16)

    def later(value, *others):
        return lax.optimization_barrier((value, *others))[0]

    tick = lax.optimization_barrier
    bits = [1 << n for n in range(outer.bit_length() - 1)]
    rest = [i for i in range(1, outer) if i not in bits]

    projected = call(
        project_body,
        [((144, rows_here), bf16)],
        [inputs, w_query.T, line(b_query), w_key.T, w_value.T, line(b_value)], us=2.4,
    )[0]
    turned = send(projected, turn)
    pack = call(
        pack_body,
        [((PACK_ROWS, 384), bf16)],
        [w_query.T, w_key.T, w_value.T, w_point.T, w_conv.T, w_out, w_inner, w_outer, w_kernel.T,
         line(b_query), line(b_point), line(b_conv), b_inner],
        us=2.2, after=(projected,),
    )[0]
    rims = jnp.where(mp == 0, inputs[rows_here - rim :], inputs[:rim])
    x_quarter = lax.dynamic_slice_in_dim(inputs, mp * quarter, quarter, 0)
    cot_quarter = lax.dynamic_slice_in_dim(cotangent, mp * quarter, quarter, 0)
    blank = jnp.zeros((384,), f32)
    lines = jnp.stack(
        [b_out.astype(f32), gain_one, shift_one, b_outer.astype(f32), gain_two, shift_two]
        + [blank] * 2
    )
    turned, pack, rims, x_quarter, cot_quarter, lines, place = tick(
        (turned, pack, rims, x_quarter, cot_quarter, lines, place)
    )

    kv = turned[0:96]
    zkv, skv = [kv] + [None] * (outer - 1), [send(kv, across_c)] + [None] * (outer - 1)
    for i in bits:
        zkv[i] = send(kv, across_z(i))
    pack_beyond = send(pack, across_y)
    pairs = []
    for i in range(blocks - 1):
        pairs += [(4 * i, 4 * i + 4), (4 * i + 7, 4 * i + 3)]
    beside = lax.ppermute(rims, ("ctx", "mp"), pairs)
    state = flash(turned, [], None)
    state = flash(turned, [skv[0]], state)
    state, kv, beside, pack_beyond, *got = tick(
        (state, kv, beside, pack_beyond, *(zkv[i] for i in bits))
    )
    zkv[0] = kv
    for i, item in zip(bits, got, strict=True):
        zkv[i] = item
        skv[i] = send(item, across_c)
    for i in rest:
        zkv[i] = send(kv, across_z(i))
    packs = [pack, send(pack, across_c), pack_beyond, send(pack_beyond, across_c)]
    extended = jnp.concatenate([beside, inputs, beside], axis=0)
    x_ext = lax.dynamic_slice_in_dim(extended, mp * quarter, quarter + 2 * rim, 0)
    for n in range(0, len(bits), 2):
        state = flash(turned, [zkv[i] for i in bits[n : n + 2]], state)
    ext = quarter + 2 * rim
    mix, depth, q_conv, key_conv, tap_probs, conv_vals = call(
        functools.partial(conv_body, rim=rim, quarter=quarter, taps=taps),
        [((192, quarter), bf16), ((quarter, 384), bf16), ((192, quarter), bf16),
         ((192, quarter), f32), ((8 * taps, quarter), f32), ((192, ext), f32)],
        [place, x_ext, depth_kernel, line(b_kernel), *packs],
        us=4.4, smem=(0,), after=tuple(state),
    )
    state, mix, *got = tick((state, mix, *(zkv[i] for i in rest)))
    for i, item in zip(rest, got, strict=True):
        zkv[i] = item
        skv[i] = send(item, across_c)
    todo = [skv[i] for i in bits] + [item[i] for i in rest for item in (zkv, skv)]
    for n in range(0, len(todo) - 2, 2):
        state = flash(turned, todo[n : n + 2], state)
    raw, lse, *chunks = flash(turned, todo[len(todo) - 2 :], state, turned_place)

    heads = [send(chunk, to_tokens(s)) for s, chunk in enumerate(chunks)]
    (layer_quarter, c0, c1, c2, c3, grad_mix, both, act, gpre, low, zed, gm, grad_h1, vec) = call(
        feed_body,
        [((quarter, 384), bf16)] + [((48, quarter), bf16)] * 4
        + [((192, quarter), f32), ((384, quarter), bf16), ((8, quarter, 192), bf16),
           ((8, quarter, 192), bf16), ((quarter, 384), bf16), ((quarter, 384), bf16),
           ((quarter, 384), bf16), ((quarter, 384), f32), ((8, 384), f32)],
        [*heads, mix, *packs, x_quarter, cot_quarter, lines],
        us=6.8, scratch=[pltpu.VMEM((8, quarter, 192), f32)],
    )
    grads = [send(item, to_heads(s)) for s, item in enumerate((c0, c1, c2, c3))]
    extra, grad_kc, g_kernel, k_bias, g_depth, spread, token_part, edge = call(
        functools.partial(conv_back_body, rim=rim, quarter=quarter, taps=taps),
        [((192, quarter), bf16), ((192, quarter), bf16), ((4, 48, 48), f32), ((48, 128), f32),
         ((16, 384), f32), ((192, ext), bf16), ((quarter + 32, 384), bf16), ((16, 384), f32)],
        [place, x_ext, depth_kernel, *packs, q_conv, key_conv, tap_probs, conv_vals, grad_mix,
         grad_h1],
        us=5.4, smem=(0,),
    )
    grads, extra, edge, layer_quarter = tick((grads, extra, edge, layer_quarter))

    q_aug, grad_aug = call(
        back_prepare_body,
        [((112, rows_here), bf16), ((64, rows_here), bf16)],
        [turned_place, turned, lse, raw, *grads], us=1.8, smem=(0,),
    )
    all_rows = -(-GRAD_ROWS // 32) * 32
    keep, give = call(
        functools.partial(weights_body, quarter=quarter, taps=taps),
        [((2, all_rows, 384), bf16)] * 2,
        [x_quarter, x_ext, both, act, gpre, low, zed, gm, vec, grad_kc, depth, g_kernel,
         k_bias, g_depth, spread, extra],
        us=4.6, after=(q_aug,),
    )

    order = list(range(outer - 1, 0, -1)) + [0]
    pairs = [order[n : n + 2] for n in range(0, outer, 2)]
    finals, waiting = [], []
    dq = None
    piece = None
    inputs_late = inputs
    for n, pair in enumerate(pairs):
        first, last = n == 0, n == len(pairs) - 1
        if first:
            given = send(give, across_c)
            edge_pairs = []
            for i in range(blocks - 1):
                edge_pairs += [(4 * i + 4, 4 * i + 3), (4 * i + 3, 4 * i + 4)]
            edge = lax.ppermute(edge, ("ctx", "mp"), edge_pairs)
        dq, parts = back(
            turned, q_aug, grad_aug, [skv[i] for i in pair], dq, None, None, (keep,) if first else ()
        )
        if first:
            dq, parts, given, edge = tick((dq, parts, given, edge))
        elif last:
            dq, parts, beyond = tick((dq, parts, beyond))
        else:
            dq, parts = tick((dq, parts))
        other = send(parts[0], across_c)
        if first:
            piece = plus(keep[1], given[1])
        if last:
            piece = plus(plus(keep[0], given[0]), beyond).reshape(2, all_rows // 2, 384)
            mine = lax.dynamic_index_in_dim(piece, x_at, 0, False)
            give = lax.dynamic_index_in_dim(piece, 1 - x_at, 0, False)
            other, mine, give = tick((other, mine, give))
            given = send(give, across_x)
        elif first:
            other, piece = tick((other, piece))
            beyond = send(piece, across_y)
        for group in [[i] for i in pair] if last else [pair]:
            dtypes = [bf16 if i else f32 for i in group]
            at = pair.index(group[0])
            dq, parts = back(
                turned, q_aug, grad_aug, [zkv[i] for i in group], dq,
                other[at : at + len(group)], dtypes,
            )
            if first:
                dq, parts, inputs_late = tick((dq, parts, inputs_late))
                inputs_turned = send(inputs_late, turn)
            else:
                dq, parts = tick((dq, parts))
            for part, i in zip(parts, group, strict=True):
                finals.append(send(part, across_z(i)) if i else part)
    layer_quarter, dq = tick((layer_quarter, dq))

    edge = jnp.where(
        mp == 0,
        jnp.pad(edge, ((16, quarter), (0, 0))),
        jnp.pad(edge, ((quarter, 16), (0, 0))),
    )
    token_part = (token_part.astype(f32) + edge).astype(bf16)
    layer_out = call(
        functools.partial(layer_out_body, quarter=quarter),
        [((rows_here, 384), bf16)],
        [place, *gather_mp(layer_quarter)], us=2.3, smem=(0,), final=(0,),
    )[0]

    joined, *chunks = call(
        functools.partial(back_join_body, parts=len(finals) - 1),
        [((144, rows_here), bf16)] + [((144, quarter), bf16)] * 4,
        [turned_place, dq, finals[-1], *finals[:-1]], us=2.1, smem=(0,),
    )
    head_w = call(
        head_weights_body, [((160, 384), bf16)], [joined, inputs_turned], us=2.2,
    )[0]
    heads = [send(chunk, to_tokens(s)) for s, chunk in enumerate(chunks)]
    head_w = plus(head_w, send(head_w, across_c))
    for bit in bits:
        head_w = plus(head_w, send(head_w, across_z(bit)))
    head_w = send(head_w, turn)
    quarter_grad = call(
        functools.partial(input_grad_body, quarter=quarter),
        [((quarter + 32, 384), bf16)],
        [*heads, *packs, token_part], us=2.0,
    )[0]
    inputs_grad = call(
        functools.partial(input_join_body, quarter=quarter),
        [((rows_here, 384), f32)],
        [place, *gather_mp(quarter_grad)], us=3.0, smem=(0,), final=(0,),
        scratch=[pltpu.VMEM((rows_here + 32, 384), f32)],
    )[0]

    piece = plus(mine, given)
    for bit in bits:
        piece = plus(piece, send(piece, across_z(bit)))
    other_piece = send(piece, across_x)
    (point, conv, query_part, grad_out, grad_inner, grad_outer, kernel, biases, i_bias, grad_depth,
     p_bias, c_bias, k_bias, *vecs) = call(
        functools.partial(unpack_body, taps=taps),
        [((48, 384), f32)] * 3 + [((2, 48, 384), f32), ((2, 192, 192), f32),
         ((2, 192, 192), f32), ((36, 48), f32), ((8, 48), f32), ((2, 192), f32), ((taps, 384), f32),
         ((48,), f32), ((48,), f32), ((36,), f32)] + [((384,), f32)] * 6,
        [place, piece, other_piece], us=2.3, smem=(0,), final=(0, 1, 3, 4, 5, 6, *range(8, 19)),
        scratch=[pltpu.VMEM((all_rows, 384), f32)],
    )
    query, key, value, q_bias, v_bias = call(
        head_unpack_body,
        [((48, 384), f32)] * 3 + [((48,), f32)] * 2,
        [head_w, query_part, biases], us=1.7, final=range(5),
    )

    return (
        layer_out, inputs_grad, query.T, q_bias, key.T, value.T, v_bias, grad_depth, point.T,
        p_bias, kernel.T, k_bias, conv.T, c_bias, grad_out, vecs[0], vecs[1], vecs[2], grad_inner,
        i_bias, grad_outer, vecs[3], vecs[4], vecs[5],
    )


def solution(mesh):
    return jax.shard_map(
        local,
        mesh=mesh,
        in_specs=(
            P("ctx", None), P(None, "mp"), P("mp"), P(None, "mp"), P(None, "mp"), P("mp"), P(),
            P(None, "mp"), P("mp"), P("mp", None), P(), P(None, "mp"), P("mp"),
            P(None, "mp", None), P(), P(), P(), P(None, None, "mp"), P(None, "mp"),
            P(None, "mp", None), P(), P(), P(), P("ctx", None),
        ),
        out_specs=(
            P("ctx", None), P("ctx", None), P(None, "mp"), P("mp"), P(None, "mp"), P(None, "mp"),
            P("mp"), P(), P(None, "mp"), P("mp"), P("mp", None), P(), P(None, "mp"), P("mp"),
            P(None, "mp", None), P(), P(), P(), P(None, None, "mp"), P(None, "mp"),
            P(None, "mp", None), P(), P(), P(),
        ),
        check_vma=False,
    )
```

```python
import functools
import math

import jax
import jax.numpy as jnp
from jax import lax
from jax.experimental import pallas as pl
from jax.experimental.pallas import tpu as pltpu
from jax.sharding import PartitionSpec as P


EPSILON = 1e-12
KERNEL_BYTES = 24 * 2**20
PACE = 1e5
f32 = jnp.float32
bf16 = jnp.bfloat16

WQ, WK, WV, WP, WC, WO, WI, WU, WM, WB = 0, 48, 96, 144, 192, 240, 336, 528, 720, 768
PACK_ROWS = 784
GP, GC, GQ, GO, GI, GU, GM, GV = 0, 48, 96, 144, 240, 432, 624, 672
GRAD_ROWS = 688


def dg(left, right, ld, rd):
    return lax.dot_general(
        left, right, (((ld,), (rd,)), ((), ())), preferred_element_type=f32
    )


def row(ref):
    return ref[...].astype(f32).reshape(1, -1)


class Rows:
    def __init__(self, refs, scr, sems, ranges):
        self.scr, self.copies, at = scr, [], 0
        for n, (low, high) in enumerate(ranges):
            span = pl.ds(at, high - low)
            copies = [
                pltpu.make_async_copy(ref.at[pl.ds(low, high - low)], scr.at[s, span], sems.at[s, n])
                for s, ref in enumerate(refs)
            ]
            self.copies.append((low, high, at, copies))
            at += high - low
        for *_, copies in self.copies:
            for copy in copies:
                copy.start()

    def wait(self, n):
        for copy in self.copies[n][3]:
            copy.wait()

    def get(self, s, low, high, lanes=slice(None)):
        for first, last, at, _ in self.copies:
            if first <= low and high <= last:
                return self.scr[s, at + low - first : at + high - first, lanes]
        raise ValueError("rows")

    def all(self, low, high):
        return jnp.concatenate([self.get(s, low, high) for s in range(4)], axis=0)


def row_scratch(ranges):
    rows = sum(high - low for low, high in ranges)
    return [pltpu.VMEM((4, rows, 384), bf16), pltpu.SemaphoreType.DMA((4, len(ranges)))]


CONV_ROWS = ((0, 48), (144, 240), (720, 784))
BACK_ROWS = ((720, 784), (144, 240), (0, 48))
FEED_ROWS = ((240, 336), (336, 784))
HEAD_ROWS = ((0, 144),)


def outer_ones(row, width):
    return dg(row, jnp.ones((row.shape[0], width), bf16), 0, 0)


def call(body, outs, args, us, scratch=(), smem=(), after=(), final=(), hbm=(), raw=()):
    inputs = len(args)

    def whole(*refs):
        body(*refs[:inputs], *refs[inputs + len(after) :])

    specs = [
        pl.BlockSpec(
            memory_space=pltpu.SMEM if i in smem else pltpu.HBM if i in raw else pltpu.VMEM
        )
        for i in range(inputs)
    ]
    return pl.pallas_call(
        whole,
        in_specs=specs + [pl.BlockSpec(memory_space=pl.ANY)] * len(after),
        out_specs=[pl.BlockSpec(memory_space=pltpu.VMEM)] * len(outs),
        out_shape=[
            pltpu.HBM(s, d) if i in final else pltpu.VMEM(s, d)
            for i, (s, d) in enumerate(outs)
        ],
        scratch_shapes=list(scratch),
        compiler_params=pltpu.CompilerParams(vmem_limit_bytes=KERNEL_BYTES),
        cost_estimate=pl.CostEstimate(flops=int(us * PACE), bytes_accessed=0, transcendentals=0),
    )(
        *(
            arg
            if i in smem
            else pltpu.with_memory_space_constraint(arg, pltpu.HBM if i in hbm or i in raw else pltpu.VMEM)
            for i, arg in enumerate(args)
        ),
        *after,
    )


def project_body(x_ref, wq_ref, bq_ref, wk_ref, wv_ref, bv_ref, out_ref):
    x = x_ref[...]
    width = x.shape[0]
    weights = jnp.concatenate([wk_ref[...], wv_ref[...], wq_ref[...]], axis=0)
    found = dg(weights, x, 1, 1)
    out_ref[0:48, :] = found[0:48].astype(bf16)
    out_ref[48:96, :] = (found[48:96] + outer_ones(bv_ref[...], width)).astype(bf16)
    out_ref[96:144, :] = (found[96:144] + outer_ones(bq_ref[...], width)).astype(bf16)


def pack_body(
    wq_ref, wk_ref, wv_ref, wp_ref, wc_ref, wo_ref, wi_ref, wu_ref, wm_ref,
    bq_ref, bp_ref, bc_ref, bi_ref, bo_ref, g1_ref, s1_ref, bu_ref, g2_ref, s2_ref,
    out_ref, lines_ref,
):
    vectors = [row(ref) for ref in (bo_ref, g1_ref, s1_ref, bu_ref, g2_ref, s2_ref)]
    lines_ref[...] = jnp.concatenate([*vectors, jnp.zeros((2, 384), f32)], axis=0)
    for at, ref in ((WQ, wq_ref), (WK, wk_ref), (WV, wv_ref), (WP, wp_ref), (WC, wc_ref)):
        out_ref[at : at + 48, :] = ref[...]
    out_ref[WO : WO + 48, :] = wo_ref[0]
    out_ref[WO + 48 : WO + 96, :] = wo_ref[1]
    out_ref[WI : WI + 192, :] = jnp.concatenate([wi_ref[0], wi_ref[1]], axis=1)
    out_ref[WU : WU + 192, :] = jnp.concatenate([wu_ref[0], wu_ref[1]], axis=1)
    out_ref[WM : WM + 64, :] = jnp.zeros((64, 384), bf16)
    out_ref[WM : WM + 36, 0:48] = wm_ref[...]
    zeros = jnp.zeros((1, 336), f32)
    lines = [jnp.concatenate([bi_ref[0:1].astype(f32), bi_ref[1:2].astype(f32)], axis=1)]
    for ref in (bq_ref, bp_ref, bc_ref):
        lines.append(jnp.concatenate([ref[...].astype(f32), zeros], axis=1))
    lines.append(jnp.zeros((12, 384), f32))
    out_ref[WB : WB + 16, :] = jnp.concatenate(lines, axis=0).astype(bf16)


def keys_aug(kv):
    keys = kv[0:48]
    return jnp.concatenate([keys, keys, jnp.ones((16, keys.shape[1]), bf16)], axis=0)


def vals_aug(kv):
    vals = kv[48:96]
    return jnp.concatenate([vals, jnp.ones((16, vals.shape[1]), bf16)], axis=0)


def split3(value):
    high = value.astype(bf16)
    rest = value - high.astype(f32)
    mid = rest.astype(bf16)
    low = (rest - mid.astype(f32)).astype(bf16)
    return high, mid, low


def scaled_queries(q):
    scaled = q.astype(f32) * (math.log2(math.e) / math.sqrt(48.0))
    high = scaled.astype(bf16)
    low = (scaled - high.astype(f32)).astype(bf16)
    return high, low


def flash_body(*refs, first, last, blocks):
    refs = list(refs)
    q_ref = refs.pop(0)
    tp_ref = refs.pop(0) if last else None
    kv_refs = [refs.pop(0) for _ in range(blocks)]
    if first:
        m_out, acc_out = refs
        m_now = acc_now = None
    else:
        m_in, acc_in = refs.pop(0), refs.pop(0)
        m_now, acc_now = m_in[0:1, :], acc_in[...]
    q = q_ref[96:144, :]
    width = q.shape[1]
    high, low = scaled_queries(q)
    q_aug = jnp.concatenate([high, low, jnp.zeros((16, width), bf16)], axis=0)
    for kv_ref in [q_ref] + kv_refs if first else kv_refs:
        kv = kv_ref[0:96, :]
        scores = dg(keys_aug(kv), q_aug, 0, 0)
        top = jnp.max(scores, axis=0, keepdims=True)
        m_new = top if m_now is None else jnp.maximum(m_now, top)
        probs = jnp.exp2(scores - m_new).astype(bf16)
        part = dg(vals_aug(kv), probs, 1, 0)
        acc_now = part if m_now is None else acc_now * jnp.exp2(m_now - m_new) + part
        m_now = m_new
    if not last:
        if not first:
            m_out, acc_out = refs
        m_out[...] = jnp.broadcast_to(m_now, (8, width))
        acc_out[...] = acc_now
        return
    raw_ref, lse_ref, *sends, low_scr = refs
    total = acc_now[48:49, :]
    raw = acc_now[0:48, :] / total
    raw_ref[...] = raw
    lse_ref[...] = jnp.broadcast_to(m_now + jnp.log2(total), (8, width))
    low_scr[...] = raw.astype(bf16)
    quarter = width // 4
    place = tp_ref[0]
    for s, send in enumerate(sends):
        at = pl.multiple_of((place ^ s) * quarter, quarter)
        send[...] = low_scr[:, pl.ds(at, quarter)]


def flash(q, kvs, state, place=None, after=()):
    width = q.shape[1]
    first, last = state is None, place is not None
    args = [q] + ([place] if last else []) + list(kvs) + ([] if first else list(state))
    if last:
        outs = [((48, width), f32), ((8, width), f32)] + [((48, width // 4), bf16)] * 4
        scratch = [pltpu.VMEM((48, width), bf16)]
    else:
        outs, scratch = [((8, width), f32), ((64, width), f32)], []
    return call(
        functools.partial(flash_body, first=first, last=last, blocks=len(kvs)),
        outs, args, us=2.4 * len(kvs) + 2.4 * first, scratch=scratch, smem=(1,) if last else (), after=after,
    )


def back_prepare_body(place_ref, q_ref, lse_ref, raw_ref, g0, g1, g2, g3, qa_ref, da_ref):
    q = q_ref[96:144, :]
    width = q.shape[1]
    quarter = width // 4
    high, low = scaled_queries(q)
    lines = split3(-lse_ref[0:1, :])
    pad = jnp.zeros((13, width), bf16)
    qa_ref[...] = jnp.concatenate([high, low, *lines, pad], axis=0)
    place = place_ref[0]
    for s, ref in enumerate((g0, g1, g2, g3)):
        at = pl.multiple_of((place ^ s) * quarter, quarter)
        da_ref[0:48, pl.ds(at, quarter)] = ref[...]
    grad = da_ref[0:48, :]
    delta = jnp.sum(grad.astype(f32) * raw_ref[...], axis=0, keepdims=True)
    da_ref[48:64, :] = jnp.concatenate([*split3(-delta), pad], axis=0)


def back_body(*refs, first, blocks, plus):
    refs = list(refs)
    q_ref, qa_ref, da_ref = refs[:3]
    kv_refs = refs[3 : 3 + blocks]
    refs = refs[3 + blocks :]
    dq_in = None if first else refs.pop(0)
    plus_refs = []
    for count, place in plus:
        group = [refs.pop(0) for _ in range(count)]
        plus_refs.append([group[0].at[place], *group[1:]])
    dq_out, *outs = refs
    if not plus:
        outs = [outs[0].at[n] for n in range(blocks)]
        plus_refs = [[]] * blocks
    q, grad = q_ref[96:144, :], da_ref[0:48, :]
    q_aug, grad_aug = qa_ref[...], da_ref[...]
    step = 256
    dq = None if first else dq_in[...]
    for kv_ref, out, group in zip(kv_refs, outs, plus_refs, strict=True):
        kv = kv_ref[...]
        keys, vals = keys_aug(kv), vals_aug(kv)
        for at in range(0, kv.shape[1], step):
            span = slice(at, at + step)
            probs = jnp.exp2(dg(keys[:, span], q_aug, 0, 0))
            grad_probs = dg(vals[:, span], grad_aug, 0, 0)
            grad_scores = (probs * grad_probs).astype(bf16)
            dv = dg(grad, probs.astype(bf16), 1, 1)
            dk = dg(q, grad_scores, 1, 1)
            part = dg(kv[0:48, span], grad_scores, 1, 0)
            dq = part if dq is None else dq + part
            both = jnp.concatenate([dk, dv], axis=0)
            for ref in group:
                both = both + ref[:, span].astype(f32)
            out[:, span] = both.astype(out.dtype)
    dq_out[...] = dq


def back(q, q_aug, grad_aug, kvs, dq, plus=(), dtypes=(), after=()):
    width = q.shape[1]
    shape = kvs[0].shape
    args = [q, q_aug, grad_aug, *kvs] + ([] if dq is None else [dq])
    args += [array for arrays, _ in plus for array in arrays]
    outs = [(shape, dtype) for dtype in dtypes] if plus else [((len(kvs), *shape), bf16)]
    dq, *parts = call(
        functools.partial(
            back_body, first=dq is None, blocks=len(kvs),
            plus=[(len(arrays), place) for arrays, place in plus],
        ),
        [((48, width), f32), *outs], args, us=3.5 * len(kvs), after=after,
    )
    return dq, parts


def back_join_body(dq_ref, dkv_ref, *refs):
    *news, out_ref = refs
    scale = 1.0 / math.sqrt(48.0)
    out_ref[0:48, :] = (dq_ref[...] * scale).astype(bf16)
    total = dkv_ref[...]
    for ref in news:
        total = total + ref[...].astype(f32)
    out_ref[48:96, :] = (total[0:48] * scale).astype(bf16)
    out_ref[96:144, :] = total[48:96].astype(bf16)


def tap_places(mp, heads, taps):
    rows = lax.broadcasted_iota(jnp.int32, (48, 8 * taps), 0)
    cols = lax.broadcasted_iota(jnp.int32, (48, 8 * taps), 1)
    s = cols & 7
    wanted = (s ^ mp) * taps + (cols >> 3)
    return ((rows == wanted) & (s < heads)).astype(f32).astype(bf16)


def lift(value, axis, shift, keep):
    size = value.shape[axis]
    rolled = pltpu.roll(value, (size - shift) % size, axis)
    return rolled[:keep] if axis == 0 else rolled[:, :keep]


def conv_body(
    place_ref, xe_ref, dk_ref, bk_ref, p0, p1, p2, p3,
    mix_ref, depth_ref, q_ref, kc_ref, tp_ref, cv_ref, scr, sems, *, rim, quarter, taps,
):
    packs = Rows((p0, p1, p2, p3), scr, sems, CONV_ROWS)
    xe = xe_ref[...]
    x_own = xe[rim : rim + quarter]
    wide = xe.astype(f32)
    reach = taps // 2
    kernel = dk_ref[...].astype(f32)
    depth = None
    for j in range(taps):
        term = lift(wide, 0, rim - reach + j, quarter) * kernel[j : j + 1, :]
        depth = term if depth is None else depth + term
    depth_low = depth.astype(bf16)
    depth_ref[...] = depth_low
    position = place_ref[1] + lax.broadcasted_iota(jnp.int32, (1, xe.shape[0]), 1) - rim
    inside = (position >= 0) & (position < place_ref[2])
    for n in range(3):
        packs.wait(n)
    attn = []
    for s in range(4):
        own = slice(48 * s, 48 * s + 48)
        bias = packs.get(s, WB, WB + 16, slice(0, 48))
        q = (
            dg(packs.get(s, WQ, WQ + 48), x_own, 1, 1) + outer_ones(bias[1:2], quarter)
        ).astype(bf16)
        kc = dg(packs.get(s, WP, WP + 48), depth_low, 1, 1) + outer_ones(bias[2:3], quarter)
        cv = dg(packs.get(s, WC, WC + 48), xe, 1, 1) + outer_ones(bias[3:4], xe.shape[0])
        q_ref[own, :] = q
        kc_ref[own, :] = kc
        cv_ref[own, :] = jnp.where(inside, cv, 0.0)
        attn.append((kc * q.astype(f32)).astype(bf16))
    attn = jnp.concatenate(attn, axis=0)
    hot = tap_places(place_ref[0], 4, taps)
    wk = [dg(packs.get(s, WM, WM + 48, slice(0, 48)), hot, 0, 0) for s in range(4)]
    wk = jnp.concatenate(wk, axis=0).astype(bf16)
    bias = dg(bk_ref[...], hot[0 : bk_ref.shape[1], :], 1, 0).astype(bf16)
    logits = dg(wk, attn, 0, 0) + outer_ones(bias, quarter)
    tiles = [logits[8 * j : 8 * j + 8] for j in range(taps)]
    top = functools.reduce(jnp.maximum, tiles)
    tiles = [jnp.exp(tile - top) for tile in tiles]
    total = functools.reduce(jnp.add, tiles)
    tiles = [tile / total for tile in tiles]
    for j in range(taps):
        tp_ref[8 * j : 8 * j + 8, :] = tiles[j]
    cv = cv_ref[...]
    mix = [None] * 4
    for j in range(taps):
        moved = lift(cv, 1, rim - reach + j, quarter)
        for s in range(4):
            term = tiles[j][s : s + 1, :] * moved[48 * s : 48 * s + 48]
            mix[s] = term if mix[s] is None else mix[s] + term
    for s in range(4):
        mix_ref[48 * s : 48 * s + 48, :] = mix[s].astype(bf16)


def conv_back_body(
    place_ref, xe_ref, dk_ref, p0, p1, p2, p3, q_ref, kc_ref, tp_ref, cv_ref, gm_ref, gh_ref,
    ex_ref, pre_ref, gk_ref, kb_ref, dpt_ref, cve_ref, tok_ref, edge_ref, scr, sems,
    *, rim, quarter, taps,
):
    packs = Rows((p0, p1, p2, p3), scr, sems, BACK_ROWS)
    reach = taps // 2
    ext = xe_ref.shape[0]
    grad_mix = gm_ref[...]
    cv = cv_ref[...]
    probs = [tp_ref[8 * j : 8 * j + 8, :] for j in range(taps)]
    grads = []
    weighted = None
    for j in range(taps):
        moved = lift(cv, 1, rim - reach + j, quarter) * grad_mix
        lines = [jnp.sum(moved[48 * s : 48 * s + 48], axis=0, keepdims=True) for s in range(4)]
        tile = jnp.concatenate(lines + [jnp.zeros((4, quarter), f32)], axis=0)
        grads.append(tile)
        term = probs[j] * tile
        weighted = term if weighted is None else weighted + term
    gtl = jnp.concatenate(
        [probs[j] * (grads[j] - weighted) for j in range(taps)], axis=0
    ).astype(bf16)
    hot = tap_places(place_ref[0], 4, taps)
    for n in range(3):
        packs.wait(n)
    wk = [dg(packs.get(s, WM, WM + 48, slice(0, 48)), hot, 0, 0) for s in range(4)]
    wk = jnp.concatenate(wk, axis=0).astype(bf16)
    q = q_ref[...].astype(f32)
    kc = kc_ref[...]
    attn = (kc * q).astype(bf16)
    plain = dg(hot, gtl, 1, 0).astype(bf16)
    for s in range(4):
        gk_ref[s] = dg(plain, attn[48 * s : 48 * s + 48], 1, 1)
    kb_ref[...] = dg(plain, jnp.ones((128, quarter), bf16), 1, 1)
    grad_attn = dg(wk, gtl, 1, 0)
    extra = (grad_attn * kc).astype(bf16)
    ex_ref[...] = extra
    grad_kc = (grad_attn * q).astype(bf16)
    pre_ref[...] = grad_kc
    wp = packs.all(WP, WP + 48)
    dvals = dg(grad_kc, wp, 0, 0)
    wide = xe_ref[...].astype(f32)
    kernel = dk_ref[...].astype(f32)
    tail = jnp.zeros((ext - quarter, dvals.shape[1]), f32)
    padded = jnp.concatenate([dvals, tail], axis=0)
    depth = None
    lines = []
    for j in range(taps):
        moved = lift(wide, 0, rim - reach + j, quarter)
        lines.append(jnp.sum(moved * dvals, axis=0, keepdims=True))
        term = pltpu.roll(padded, rim - reach + j, 0) * kernel[j : j + 1, :]
        depth = term if depth is None else depth + term
    lines.append(jnp.zeros((16 - taps, dvals.shape[1]), f32))
    dpt_ref[...] = jnp.concatenate(lines, axis=0)
    side = jnp.zeros((4 * 48, ext - quarter), f32)
    spread = None
    for j in range(taps):
        rows = [probs[j][s : s + 1, :] * grad_mix[48 * s : 48 * s + 48] for s in range(4)]
        full = jnp.concatenate([jnp.concatenate(rows, axis=0), side], axis=1)
        term = pltpu.roll(full, rim - reach + j, 1)
        spread = term if spread is None else spread + term
    position = place_ref[1] + lax.broadcasted_iota(jnp.int32, (1, ext), 1) - rim
    inside = (position >= 0) & (position < place_ref[2])
    spread = jnp.where(inside, spread, 0.0).astype(bf16)
    cve_ref[...] = spread
    wc = packs.all(WC, WC + 48)
    wq = packs.all(WQ, WQ + 48)
    tokens = depth + dg(spread, wc, 0, 0)
    own = dg(extra, wq, 0, 0) + gh_ref[...]
    end = rim + quarter
    tok_ref[0:16, :] = tokens[rim - 16 : rim].astype(bf16)
    tok_ref[16 : quarter + 16, :] = (tokens[rim:end] + own).astype(bf16)
    tok_ref[quarter + 16 :, :] = tokens[end : end + 16].astype(bf16)
    edge_ref[...] = jnp.where(place_ref[0] == 0, tokens[rim - 16 : rim], tokens[end : end + 16])


def norm(hidden):
    centred = hidden - jnp.mean(hidden, axis=-1, keepdims=True)
    inverse = lax.rsqrt(jnp.mean(centred * centred, axis=-1, keepdims=True) + EPSILON)
    return centred * inverse, inverse


def norm_back(grad, normed, inverse, gain):
    scaled = grad * gain
    return inverse * (
        scaled
        - jnp.mean(scaled, axis=-1, keepdims=True)
        - normed * jnp.mean(scaled * normed, axis=-1, keepdims=True)
    )


def feed_body(
    r0, r1, r2, r3, mix_ref, p0, p1, p2, p3, x_ref, cot_ref, lines_ref,
    out_ref, c0, c1, c2, c3, gmix_ref, a_ref, act_ref, gpre_ref, low_ref, zed_ref, gm_ref,
    gh_ref, vec_ref, slope_scr, scr, sems,
):
    packs = Rows((p0, p1, p2, p3), scr, sems, FEED_ROWS)
    both = []
    for s, ref in enumerate((r0, r1, r2, r3)):
        both += [ref[...], mix_ref[48 * s : 48 * s + 48, :]]
    both = jnp.concatenate(both, axis=0)
    a_ref[...] = both
    packs.wait(0)
    w_out = packs.all(WO, WO + 96)
    mixed = dg(both, w_out, 0, 0) + lines_ref[0:1, :]
    normed1, inverse1 = norm(mixed + x_ref[...].astype(f32))
    gain1, gain2 = lines_ref[1:2, :], lines_ref[4:5, :]
    low = (normed1 * gain1 + lines_ref[2:3, :]).astype(bf16)
    low_ref[...] = low
    halves = [low[:, 0:192], low[:, 192:384]]
    packs.wait(1)
    outer = [None, None]
    for g in range(2):
        lanes = slice(192 * g, 192 * g + 192)
        for s in range(4):
            pre = dg(halves[g], packs.get(s, WI, WI + 192, lanes), 1, 0)
            pre = pre + packs.get(s, WB, WB + 16, lanes)[0:1].astype(f32)
            cdf = 0.5 * (1.0 + lax.erf(pre * math.sqrt(0.5)))
            pdf = jnp.exp(-0.5 * pre * pre) * (1.0 / math.sqrt(2.0 * math.pi))
            slope_scr[2 * s + g] = cdf + pre * pdf
            act = (pre * cdf).astype(bf16)
            act_ref[2 * s + g] = act
            term = dg(act, packs.get(s, WU, WU + 192, lanes), 1, 0)
            outer[g] = term if outer[g] is None else outer[g] + term
    outer = jnp.concatenate(outer, axis=1) + lines_ref[3:4, :]
    normed2, inverse2 = norm(outer + low.astype(f32))
    out_ref[...] = (normed2 * gain2 + lines_ref[5:6, :]).astype(bf16)
    cot = cot_ref[...].astype(f32)
    grad_h2 = norm_back(cot, normed2, inverse2, gain2)
    zed = grad_h2.astype(bf16)
    zed_ref[...] = zed
    halves = [zed[:, 0:192], zed[:, 192:384]]
    back = [None, None]
    for g in range(2):
        lanes = slice(192 * g, 192 * g + 192)
        for s in range(4):
            grad_act = dg(halves[g], packs.get(s, WU, WU + 192, lanes), 1, 1)
            gpre = (grad_act * slope_scr[2 * s + g]).astype(bf16)
            gpre_ref[2 * s + g] = gpre
            term = dg(gpre, packs.get(s, WI, WI + 192, lanes), 1, 1)
            back[g] = term if back[g] is None else back[g] + term
    grad_norm1 = jnp.concatenate(back, axis=1) + grad_h2
    grad_h1 = norm_back(grad_norm1, normed1, inverse1, gain1)
    gh_ref[...] = grad_h1
    gm = grad_h1.astype(bf16)
    gm_ref[...] = gm
    grads = dg(w_out, gm, 1, 1)
    for s, ref in enumerate((c0, c1, c2, c3)):
        ref[...] = grads[96 * s : 96 * s + 48].astype(bf16)
        gmix_ref[48 * s : 48 * s + 48, :] = grads[96 * s + 48 : 96 * s + 96]
    sums = [gm.astype(f32), grad_norm1 * normed1, grad_norm1, zed.astype(f32), cot * normed2, cot]
    lines = [jnp.sum(item, axis=0, keepdims=True) for item in sums]
    lines.append(jnp.zeros((2, 384), f32))
    vec_ref[...] = jnp.concatenate(lines, axis=0)


def weights_body(
    x_ref, xe_ref, a_ref, act_ref, gpre_ref, low_ref, zed_ref, gm_ref, vec_ref,
    pre_ref, depth_ref, gk_ref, kb_ref, dpt_ref, cve_ref, ex_ref, o0, o1, o2, o3, mark_ref,
    *, quarter, taps,
):
    outs = (o0, o1, o2, o3)
    mark_ref[...] = jnp.zeros_like(mark_ref)
    x_own = x_ref[...]
    extra, spread = ex_ref[...], cve_ref[...]
    g_query = dg(extra, x_own, 1, 0)
    q_bias = jnp.sum(extra.astype(f32), axis=1, keepdims=True)
    g_conv = dg(spread, xe_ref[...], 1, 0)
    c_bias = jnp.sum(spread.astype(f32), axis=1, keepdims=True)
    pre = pre_ref[...]
    g_point = dg(pre, depth_ref[...], 1, 0)
    p_bias = jnp.sum(pre.astype(f32), axis=1, keepdims=True)
    low, zed, gm = low_ref[...], zed_ref[...], gm_ref[...]
    lane = lax.broadcasted_iota(jnp.int32, (48, 128), 1)
    ones = jnp.ones((8, quarter), bf16)
    for s, out in enumerate(outs):
        own = slice(48 * s, 48 * s + 48)
        out[GP : GP + 48, :] = g_point[own].astype(bf16)
        out[GC : GC + 48, :] = g_conv[own].astype(bf16)
        out[GQ : GQ + 48, :] = g_query[own].astype(bf16)
        out[GO : GO + 96, :] = dg(a_ref[96 * s : 96 * s + 96, :], gm, 1, 0).astype(bf16)
        inner, outer, bias = [], [], []
        for g in range(2):
            lanes = slice(192 * g, 192 * g + 192)
            gpre = gpre_ref[2 * s + g]
            inner.append(dg(low[:, lanes], gpre, 0, 0))
            outer.append(dg(act_ref[2 * s + g], zed[:, lanes], 0, 0))
            bias.append(dg(ones, gpre, 1, 0)[0:1])
        out[GI : GI + 192, :] = jnp.concatenate(inner, axis=1).astype(bf16)
        out[GU : GU + 192, :] = jnp.concatenate(outer, axis=1).astype(bf16)
        tile = jnp.concatenate([gk_ref[s], jnp.zeros((48, 80), f32)], axis=1)
        tile = jnp.where(lane == 64, p_bias[own], tile)
        tile = jnp.where(lane == 65, c_bias[own], tile)
        tile = jnp.where(lane == 66, kb_ref[...], tile)
        tile = jnp.where(lane == 67, q_bias[own], tile)
        out[GM : GM + 48, 0:128] = tile.astype(bf16)
        out[GM : GM + 48, 128:384] = jnp.zeros((48, 256), bf16)
        bias = jnp.concatenate(bias, axis=1)
        lines = jnp.concatenate([bias, dpt_ref[0:taps, :], vec_ref[0:6, :]], axis=0)
        out[GV : GV + 16, :] = lines.astype(bf16)
        if out.shape[0] > GRAD_ROWS:
            out[GRAD_ROWS:, :] = jnp.zeros((out.shape[0] - GRAD_ROWS, 384), bf16)


def add_body(a_ref, b_ref, out_ref):
    out_ref[...] = (a_ref[...].astype(f32) + b_ref[...].astype(f32)).astype(out_ref.dtype)


def fold_body(place_ref, a_ref, b_ref, c_ref, keep_ref, give_ref):
    x = place_ref[3]
    half = keep_ref.shape[0]
    for out, part in ((keep_ref, x), (give_ref, 1 - x)):
        rows = pl.ds(pl.multiple_of(part * half, 16), half)
        first = (a_ref[rows, :].astype(f32) + b_ref[rows, :].astype(f32)).astype(bf16).astype(f32)
        out[...] = (first + c_ref[rows, :].astype(f32)).astype(bf16)


def edge_body(place_ref, tok_ref, edge_ref, layer_ref, out_ref):
    mp = place_ref[0]
    rows = tok_ref.shape[0]
    out_ref[0:rows, :] = tok_ref[...]
    out_ref[rows:, :] = layer_ref[...]
    low, high = slice(16, 32), slice(rows - 32, rows - 16)

    @pl.when(mp == 0)
    def _():
        out_ref[low, :] = (tok_ref[low, :].astype(f32) + edge_ref[...]).astype(bf16)

    @pl.when(mp == 3)
    def _():
        out_ref[high, :] = (tok_ref[high, :].astype(f32) + edge_ref[...]).astype(bf16)


def unpack_body(
    place_ref, own_ref, other_ref,
    point_ref, conv_ref, query_ref, out_ref, inner_ref, outer_ref, kernel_ref, qb_ref, ib_ref,
    dep_ref, pb_ref, cb_ref, kb_ref, *refs, taps,
):
    *vec_refs, scr = refs
    x = place_ref[3]
    half = own_ref.shape[0]
    scr[pl.ds(pl.multiple_of(x * half, 16), half), :] = own_ref[...].astype(f32)
    scr[pl.ds(pl.multiple_of((1 - x) * half, 16), half), :] = other_ref[...].astype(f32)
    point_ref[...] = scr[GP : GP + 48, :]
    conv_ref[...] = scr[GC : GC + 48, :]
    query_ref[...] = scr[GQ : GQ + 48, :]
    out_ref[0] = scr[GO : GO + 48, :]
    out_ref[1] = scr[GO + 48 : GO + 96, :]
    for g in range(2):
        lanes = slice(192 * g, 192 * g + 192)
        inner_ref[g] = scr[GI : GI + 192, lanes]
        outer_ref[g] = scr[GU : GU + 192, lanes]
        ib_ref[g : g + 1, :] = scr[GV : GV + 1, lanes]
    kernel_ref[...] = scr[GM : GM + 36, 0:48]
    turned = jnp.transpose(scr[GM : GM + 48, 0:128], (1, 0))
    pb_ref[...] = turned[64]
    cb_ref[...] = turned[65]
    kb_ref[...] = turned[66, 0:36]
    qb_ref[...] = turned[64:72, :]
    dep_ref[...] = scr[GV + 1 : GV + 1 + taps, :]
    for n, ref in enumerate(vec_refs):
        ref[...] = scr[GV + 1 + taps + n, :]


def head_weights_body(g_ref, x_ref, out_ref):
    grads = g_ref[...]
    out_ref[0:144, :] = dg(grads, x_ref[...], 1, 0).astype(bf16)
    out_ref[144:160, :] = jnp.zeros((16, 384), bf16)
    sums = dg(jnp.ones((16, grads.shape[1]), bf16), grads, 1, 1)
    out_ref[144:160, 0:144] = sums.astype(bf16)


def head_unpack_body(
    total_ref, other_ref, part_ref, bias_ref, q_ref, k_ref, v_ref, qb_ref, vb_ref
):
    total = total_ref[...].astype(f32) + other_ref[...].astype(f32)
    q_ref[...] = total[0:48] + part_ref[...]
    k_ref[...] = total[48:96]
    v_ref[...] = total[96:144]
    qb_ref[...] = total[144, 0:48] + bias_ref[3, :]
    vb_ref[...] = total[144, 96:144]


def input_grad_body(
    place_ref, g0, g1, g2, g3, p0, p1, p2, p3, t0, t1, t2, t3, out_ref, acc, scr, sems, *, quarter
):
    packs = Rows((p0, p1, p2, p3), scr, sems, HEAD_ROWS)
    mp = place_ref[0]
    parts = (t0, t1, t2, t3)
    for s, ref in enumerate(parts):
        at = pl.multiple_of((mp ^ s) * quarter, quarter)
        acc[pl.ds(at + 16, quarter), :] = ref[16 : quarter + 16, :].astype(f32)
    for s, ref in enumerate(parts):
        at = pl.multiple_of((mp ^ s) * quarter, quarter)
        acc[pl.ds(at, 16), :] += ref[0:16, :].astype(f32)
        acc[pl.ds(at + quarter + 16, 16), :] += ref[quarter + 16 : quarter + 32, :].astype(f32)
    packs.wait(0)
    total = None
    for s, grads in enumerate((g0, g1, g2, g3)):
        term = dg(grads[...], packs.get(s, WQ, WQ + 144), 0, 0)
        total = term if total is None else total + term
    out_ref[...] = total + acc[16 : 4 * quarter + 16, :]


def layer_out_body(place_ref, t0, t1, t2, t3, out_ref, *, quarter):
    mp = place_ref[0]
    for s, ref in enumerate((t0, t1, t2, t3)):
        at = pl.multiple_of((mp ^ s) * quarter, quarter)
        out_ref[pl.ds(at, quarter), :] = ref[quarter + 32 :, :]


def local(
    inputs, w_query, b_query, w_key, w_value, b_value, depth_kernel, w_point, b_point, w_kernel,
    b_kernel, w_conv, b_conv, w_out, b_out, gain_one, shift_one, w_inner, b_inner, w_outer,
    b_outer, gain_two, shift_two, cotangent,
):
    blocks = lax.axis_size("ctx")
    outer = blocks // 2
    rows_here = inputs.shape[0]
    quarter = rows_here // 4
    taps = depth_kernel.shape[0]
    rim = 64
    ctx, mp = lax.axis_index("ctx"), lax.axis_index("mp")
    x_at, z_at = ctx % 2, ctx // 2
    place = jnp.stack(
        [mp, ctx * rows_here + mp * quarter, blocks * rows_here, x_at, z_at]
    ).astype(jnp.int32)
    turned_place = ((mp // 2) * 2 + x_at).astype(jnp.int32).reshape(1)

    def table(change):
        pairs = []
        for z in range(outer):
            for x in range(2):
                for y in range(2):
                    for c in range(2):
                        z2, x2, y2, c2 = change(z, x, y, c)
                        pairs.append(((2 * z + x) * 4 + 2 * y + c, (2 * z2 + x2) * 4 + 2 * y2 + c2))
        return pairs

    def send(value, change):
        return lax.ppermute(value, ("ctx", "mp"), table(change))

    def turn(z, x, y, c):
        return (z, c, y, x)

    def across_c(z, x, y, c):
        return (z, x, y, c ^ 1)

    def across_y(z, x, y, c):
        return (z, x, y ^ 1, c)

    def across_x(z, x, y, c):
        return (z, x ^ 1, y, c)

    def across_z(i):
        return lambda z, x, y, c: (z ^ i, x, y, c)

    def to_tokens(s):
        return lambda z, x, y, c: (z, c, y ^ (s >> 1), x ^ (s & 1))

    def to_heads(s):
        return lambda z, x, y, c: (z, c ^ (s & 1), y ^ (s >> 1), x)

    def gather_mp(value):
        beyond = send(value, across_y)
        return [value, send(value, across_c), beyond, send(beyond, across_c)]

    def line(vector):
        return vector.reshape(1, -1)

    def plus(left, right, hbm=(), final=()):
        return call(add_body, [(left.shape, bf16)], [left, right], us=1, hbm=hbm, final=final)[0]

    def later(value, *others):
        return lax.optimization_barrier((value, *others))[0]

    tick = lax.optimization_barrier
    bits = [1 << n for n in range(outer.bit_length() - 1)]
    rest = [i for i in range(1, outer) if i not in bits]

    projected = call(
        project_body,
        [((144, rows_here), bf16)],
        [inputs, w_query.T, line(b_query), w_key.T, w_value.T, line(b_value)], us=2.4,
        hbm=range(6),
    )[0]
    turned = send(projected, turn)
    pack, lines = call(
        pack_body,
        [((PACK_ROWS, 384), bf16), ((8, 384), f32)],
        [w_query.T, w_key.T, w_value.T, w_point.T, w_conv.T, w_out, w_inner, w_outer, w_kernel.T,
         line(b_query), line(b_point), line(b_conv), b_inner, b_out, gain_one, shift_one, b_outer,
         gain_two, shift_two],
        us=2.2, after=(projected,), hbm=range(19), final=(0,),
    )
    rims = jnp.where(mp == 0, inputs[rows_here - rim :], inputs[:rim])
    x_quarter = lax.dynamic_slice_in_dim(inputs, mp * quarter, quarter, 0)
    cot_quarter = lax.dynamic_slice_in_dim(cotangent, mp * quarter, quarter, 0)
    turned, pack, rims, x_quarter, cot_quarter, place, lines = tick(
        (turned, pack, rims, x_quarter, cot_quarter, place, lines)
    )

    kv = turned[0:96]
    zkv, skv = [kv] + [None] * (outer - 1), [send(kv, across_c)] + [None] * (outer - 1)
    for i in bits:
        zkv[i] = send(kv, across_z(i))
    pack_beyond = send(pack, across_y)
    state = flash(turned, [], None)
    state = flash(turned, [skv[0]], state)
    rims, _ = tick((rims, state[0]))
    pairs = []
    for i in range(blocks - 1):
        pairs += [(4 * i, 4 * i + 4), (4 * i + 7, 4 * i + 3)]
    beside = lax.ppermute(rims, ("ctx", "mp"), pairs)
    kv, beside, pack_beyond, *got = tick(
        (kv, beside, pack_beyond, *(zkv[i] for i in bits))
    )
    zkv[0] = kv
    for i, item in zip(bits, got, strict=True):
        zkv[i] = item
        skv[i] = send(item, across_c)
    for i in rest:
        zkv[i] = send(zkv[i & (i - 1)], across_z(i & -i))
    packs = [pack, send(pack, across_c), pack_beyond, send(pack_beyond, across_c)]
    extended = jnp.concatenate([beside, inputs, beside], axis=0)
    x_ext = lax.dynamic_slice_in_dim(extended, mp * quarter, quarter + 2 * rim, 0)
    for n in range(0, len(bits), 2):
        state = flash(turned, [zkv[i] for i in bits[n : n + 2]], state)
    ext = quarter + 2 * rim
    mix, depth, q_conv, key_conv, tap_probs, conv_vals = call(
        functools.partial(conv_body, rim=rim, quarter=quarter, taps=taps),
        [((192, quarter), bf16), ((quarter, 384), bf16), ((192, quarter), bf16),
         ((192, quarter), f32), ((8 * taps, quarter), f32), ((192, ext), f32)],
        [place, x_ext, depth_kernel, line(b_kernel), *packs],
        us=4.4, smem=(0,), after=tuple(state), final=range(1, 6), raw=range(4, 8), hbm=(3,),
        scratch=row_scratch(CONV_ROWS),
    )
    mix, *got = tick((mix, *(zkv[i] for i in rest)))
    for i, item in zip(rest, got, strict=True):
        zkv[i] = item
        skv[i] = send(item, across_c)
    todo = [skv[i] for i in bits] + [item[i] for i in rest for item in (zkv, skv)]
    for n in range(0, len(todo) - 2, 2):
        state = flash(turned, todo[n : n + 2], state)
    raw, lse, *chunks = flash(turned, todo[len(todo) - 2 :], state, turned_place)

    heads = [send(chunk, to_tokens(s)) for s, chunk in enumerate(chunks)]
    (layer_quarter, c0, c1, c2, c3, grad_mix, both, act, gpre, low, zed, gm, grad_h1, vec) = call(
        feed_body,
        [((quarter, 384), bf16)] + [((48, quarter), bf16)] * 4
        + [((192, quarter), f32), ((384, quarter), bf16), ((8, quarter, 192), bf16),
           ((8, quarter, 192), bf16), ((quarter, 384), bf16), ((quarter, 384), bf16),
           ((quarter, 384), bf16), ((quarter, 384), f32), ((8, 384), f32)],
        [*heads, mix, *packs, x_quarter, cot_quarter, lines],
        us=6.8, raw=range(5, 9),
        scratch=[pltpu.VMEM((8, quarter, 192), f32), *row_scratch(FEED_ROWS)],
    )
    grads = [send(item, to_heads(s)) for s, item in enumerate((c0, c1, c2, c3))]
    extra, grad_kc, g_kernel, k_bias, g_depth, spread, token_part, edge = call(
        functools.partial(conv_back_body, rim=rim, quarter=quarter, taps=taps),
        [((192, quarter), bf16), ((192, quarter), bf16), ((4, 48, 48), f32), ((48, 128), f32),
         ((16, 384), f32), ((192, ext), bf16), ((quarter + 32, 384), bf16), ((16, 384), f32)],
        [place, x_ext, depth_kernel, *packs, q_conv, key_conv, tap_probs, conv_vals, grad_mix,
         grad_h1],
        us=5.4, smem=(0,), raw=range(3, 7), scratch=row_scratch(BACK_ROWS),
    )
    grads, extra = tick((grads, extra))

    q_aug, grad_aug = call(
        back_prepare_body,
        [((112, rows_here), bf16), ((64, rows_here), bf16)],
        [turned_place, turned, lse, raw, *grads], us=1.8, smem=(0,),
    )
    all_rows = -(-GRAD_ROWS // 32) * 32
    *sums, mark = call(
        functools.partial(weights_body, quarter=quarter, taps=taps),
        [((all_rows, 384), bf16)] * 4 + [((8, 128), f32)],
        [x_quarter, x_ext, both, act, gpre, low, zed, gm, vec, grad_kc, depth, g_kernel,
         k_bias, g_depth, spread, extra],
        us=4.6, after=(q_aug,), final=range(4),
    )

    order = sorted(range(outer), key=lambda i: (-i.bit_count(), -i))
    edge_pairs = []
    for i in range(blocks - 1):
        edge_pairs += [(4 * i + 4, 4 * i + 3), (4 * i + 3, 4 * i + 4)]
    found = {i: [] for i in range(outer)}
    cross_found = {}

    def cross(pair, dq, after=()):
        dq, (parts,) = back(turned, q_aug, grad_aug, [skv[i] for i in pair], dq, after=after)
        return dq, parts

    def spread_out(pair, parts):
        other = send(parts, across_c)
        for n, i in enumerate(pair):
            cross_found[i] = (other, n)

    def own(group, dq, after=()):
        sums = []
        for i in group:
            other, place = cross_found[i]
            sums.append(([other, *found[i]] if i else [other], place))
        dtypes = [bf16 if i else f32 for i in group]
        dq, parts = back(
            turned, q_aug, grad_aug, [zkv[i] for i in group], dq, sums, dtypes, after
        )
        dq, parts = tick((dq, parts))
        for i, part in zip(group, parts, strict=True):
            if i:
                found[i & (i - 1)].append(send(part, across_z(i & -i)))
                found[i] = []
        return dq, parts[-1]

    givens = [send(sums[3], across_c), send(sums[1], across_c)]
    edge = lax.ppermute(edge, ("ctx", "mp"), edge_pairs)
    piece = plus(sums[2], givens[0], hbm=(0,), final=(0,))
    beyond = send(piece, across_y)
    dq, parts = cross(order[0:2], None, (piece,))
    dq, parts, given, edge, layer_quarter = tick((dq, parts, givens[1], edge, layer_quarter))
    spread_out(order[0:2], parts)
    both_parts = call(
        edge_body, [((2 * quarter + 32, 384), bf16)], [place, token_part, edge, layer_quarter],
        us=1, smem=(0,), final=(0,),
    )[0]
    dq, _ = own(order[:1], dq, (both_parts,))
    for n in range(2, outer, 2):
        dq, parts = cross(order[n : n + 2], dq)
        dq, parts, found = tick((dq, parts, found))
        spread_out(order[n : n + 2], parts)
        if n == outer - 2:
            beyond, dq = tick((beyond, dq))
            mine, give = call(
                fold_body, [((all_rows // 2, 384), bf16)] * 2, [place, sums[0], given, beyond],
                us=1, smem=(0,), hbm=(1, 3),
            )
            given = send(give, across_x)
        dq, _ = own(order[n - 1 : n], dq, (mine, give) if n == outer - 2 else ())
        if n < outer - 2:
            dq, _ = own(order[n : n + 1], dq)
    dq, last_part = own(order[-2:], dq)
    given, both_parts, dq = tick((given, both_parts, dq))
    piece = plus(mine, given)
    given = send(piece, across_z(bits[0]))
    parts_beyond = send(both_parts, across_y)
    parts_beside = send(both_parts, across_c)
    found, dq, _ = tick((found, dq, piece))

    joined = call(
        back_join_body, [((144, rows_here), bf16)], [dq, last_part, *found[0]], us=2.1,
    )[0]
    head_grads = send(joined, turn)
    given, _ = tick((given, joined))
    if len(bits) > 1:
        piece = plus(piece, given)
        given = send(piece, across_z(bits[1]))
    head_grads, parts_beyond, piece = tick((head_grads, parts_beyond, piece))
    parts_other = send(parts_beyond, across_c)
    head_w = call(
        head_weights_body, [((160, 384), bf16)], [head_grads, inputs], us=2.2,
    )[0]
    head_other = send(head_w, across_x)
    grads_beyond = send(head_grads, across_y)
    grads_beside = send(head_grads, across_c)
    parts_other, head_w = tick((parts_other, head_w))
    both = [both_parts, parts_beside, parts_beyond, parts_other]
    layer_out = call(
        functools.partial(layer_out_body, quarter=quarter),
        [((rows_here, 384), bf16)],
        [place, *both], us=2.3, smem=(0,), final=(0,), hbm=(1,), after=(head_w,),
    )[0]
    head_other, _ = tick((head_other, layer_out))
    head_w = plus(head_w, head_other)
    head_other = send(head_w, across_z(bits[0]))
    grads_beyond, head_w = tick((grads_beyond, head_w))
    grads_other = send(grads_beyond, across_c)
    for n, bit in enumerate(bits[1:]):
        head_other = tick((head_other, grads_beyond))[0]
        head_w = plus(head_w, head_other)
        head_other = send(head_w, across_z(bit))
        given = tick((given, head_w))[0]
        piece = plus(piece, given)
        given = send(piece, across_z(bits[n + 2]) if n + 2 < len(bits) else across_x)
    grads_other, _ = tick((grads_other, piece))
    inputs_grad = call(
        functools.partial(input_grad_body, quarter=quarter),
        [((rows_here, 384), f32)],
        [place, head_grads, grads_beside, grads_beyond, grads_other, *packs, *both], us=3.0,
        smem=(0,), raw=range(5, 9), hbm=(9,), final=(0,),
        scratch=[pltpu.VMEM((rows_here + 32, 384), f32), *row_scratch(HEAD_ROWS)],
    )[0]
    other_piece, _ = tick((given, inputs_grad))
    (point, conv, query_part, grad_out, grad_inner, grad_outer, kernel, biases, i_bias, grad_depth,
     p_bias, c_bias, k_bias, *vecs) = call(
        functools.partial(unpack_body, taps=taps),
        [((48, 384), f32)] * 3 + [((2, 48, 384), f32), ((2, 192, 192), f32),
         ((2, 192, 192), f32), ((36, 48), f32), ((8, 48), f32), ((2, 192), f32), ((taps, 384), f32),
         ((48,), f32), ((48,), f32), ((36,), f32)] + [((384,), f32)] * 6,
        [place, piece, other_piece], us=2.3, smem=(0,), final=(0, 1, 3, 4, 5, 6, *range(8, 19)),
        scratch=[pltpu.VMEM((all_rows, 384), f32)],
    )
    query, key, value, q_bias, v_bias = call(
        head_unpack_body,
        [((48, 384), f32)] * 3 + [((48,), f32)] * 2,
        [head_w, head_other, query_part, biases], us=1.7, final=range(5),
    )

    return (
        layer_out, inputs_grad, query.T, q_bias, key.T, value.T, v_bias, grad_depth, point.T,
        p_bias, kernel.T, k_bias, conv.T, c_bias, grad_out, vecs[0], vecs[1], vecs[2], grad_inner,
        i_bias, grad_outer, vecs[3], vecs[4], vecs[5],
    )


def solution(mesh):
    return jax.shard_map(
        local,
        mesh=mesh,
        in_specs=(
            P("ctx", None), P(None, "mp"), P("mp"), P(None, "mp"), P(None, "mp"), P("mp"), P(),
            P(None, "mp"), P("mp"), P("mp", None), P(), P(None, "mp"), P("mp"),
            P(None, "mp", None), P(), P(), P(), P(None, None, "mp"), P(None, "mp"),
            P(None, "mp", None), P(), P(), P(), P("ctx", None),
        ),
        out_specs=(
            P("ctx", None), P("ctx", None), P(None, "mp"), P("mp"), P(None, "mp"), P(None, "mp"),
            P("mp"), P(), P(None, "mp"), P("mp"), P("mp", None), P(), P(None, "mp"), P("mp"),
            P(None, "mp", None), P(), P(), P(), P(None, None, "mp"), P(None, "mp"),
            P(None, "mp", None), P(), P(), P(),
        ),
        check_vma=False,
    )
```

```python
import functools
import math

import jax
import jax.numpy as jnp
from jax import lax
from jax.experimental import pallas as pl
from jax.experimental.pallas import tpu as pltpu
from jax.sharding import PartitionSpec as P


EPSILON = 1e-12
KERNEL_BYTES = 24 * 2**20
PACE = 1e5
JOIN_PACE = 4e4
f32 = jnp.float32
bf16 = jnp.bfloat16

WQ, WK, WV, WP, WC, WO, WI, WU, WM, WB = 0, 48, 96, 144, 192, 240, 336, 528, 720, 768
PACK_ROWS = 784
GP, GC, GQ, GO, GI, GU, GM, GV = 0, 48, 96, 144, 240, 432, 624, 672
GRAD_ROWS = 688


def dg(left, right, ld, rd):
    return lax.dot_general(
        left, right, (((ld,), (rd,)), ((), ())), preferred_element_type=f32
    )


def row(ref):
    return ref[...].astype(f32).reshape(1, -1)


class Rows:
    def __init__(self, refs, scr, sems, ranges):
        self.scr, self.copies, at = scr, [], 0
        for n, (low, high) in enumerate(ranges):
            span = pl.ds(at, high - low)
            copies = [
                pltpu.make_async_copy(ref.at[pl.ds(low, high - low)], scr.at[s, span], sems.at[s, n])
                for s, ref in enumerate(refs)
            ]
            self.copies.append((low, high, at, copies))
            at += high - low
        for *_, copies in self.copies:
            for copy in copies:
                copy.start()

    def wait(self, n):
        for copy in self.copies[n][3]:
            copy.wait()

    def get(self, s, low, high, lanes=slice(None)):
        for first, last, at, _ in self.copies:
            if first <= low and high <= last:
                return self.scr[s, at + low - first : at + high - first, lanes]
        raise ValueError("rows")

    def all(self, low, high):
        return jnp.concatenate([self.get(s, low, high) for s in range(4)], axis=0)


def row_scratch(ranges):
    rows = sum(high - low for low, high in ranges)
    return [pltpu.VMEM((4, rows, 384), bf16), pltpu.SemaphoreType.DMA((4, len(ranges)))]


CONV_ROWS = ((0, 48), (144, 240), (720, 784))
BACK_ROWS = ((720, 784), (144, 240), (0, 48))
FEED_ROWS = ((240, 336), (336, 784))
HEAD_ROWS = ((0, 144),)


def outer_ones(row, width):
    return dg(row, jnp.ones((row.shape[0], width), bf16), 0, 0)


def call(body, outs, args, us, scratch=(), smem=(), after=(), final=(), hbm=(), raw=(), raw_out=()):
    inputs = len(args)

    def whole(*refs):
        body(*refs[:inputs], *refs[inputs + len(after) :])

    specs = [
        pl.BlockSpec(
            memory_space=pltpu.SMEM if i in smem else pltpu.HBM if i in raw else pltpu.VMEM
        )
        for i in range(inputs)
    ]
    return pl.pallas_call(
        whole,
        in_specs=specs + [pl.BlockSpec(memory_space=pl.ANY)] * len(after),
        out_specs=[
            pl.BlockSpec(memory_space=pltpu.HBM if i in raw_out else pltpu.VMEM)
            for i in range(len(outs))
        ],
        out_shape=[
            pltpu.HBM(s, d) if i in final else pltpu.VMEM(s, d)
            for i, (s, d) in enumerate(outs)
        ],
        scratch_shapes=list(scratch),
        compiler_params=pltpu.CompilerParams(vmem_limit_bytes=KERNEL_BYTES),
        cost_estimate=pl.CostEstimate(flops=int(us * PACE), bytes_accessed=0, transcendentals=0),
    )(
        *(
            arg
            if i in smem
            else pltpu.with_memory_space_constraint(arg, pltpu.HBM if i in hbm or i in raw else pltpu.VMEM)
            for i, arg in enumerate(args)
        ),
        *after,
    )


def project_body(x_ref, wq_ref, bq_ref, wk_ref, wv_ref, bv_ref, kv_ref, q_ref):
    x = x_ref[...]
    width = x.shape[0]
    weights = jnp.concatenate([wk_ref[...], wv_ref[...], wq_ref[...]], axis=0)
    found = dg(weights, x, 1, 1)
    kv_ref[0:48, :] = found[0:48].astype(bf16)
    kv_ref[48:96, :] = (found[48:96] + outer_ones(bv_ref[...], width)).astype(bf16)
    q_ref[...] = (found[96:144] + outer_ones(bq_ref[...], width)).astype(bf16)


def pack_body(
    wq_ref, wk_ref, wv_ref, wp_ref, wc_ref, wo_ref, wi_ref, wu_ref, wm_ref,
    bq_ref, bp_ref, bc_ref, bi_ref, bo_ref, g1_ref, s1_ref, bu_ref, g2_ref, s2_ref,
    out_ref, lines_ref,
):
    vectors = [row(ref) for ref in (bo_ref, g1_ref, s1_ref, bu_ref, g2_ref, s2_ref)]
    lines_ref[...] = jnp.concatenate([*vectors, jnp.zeros((2, 384), f32)], axis=0)
    for at, ref in ((WQ, wq_ref), (WK, wk_ref), (WV, wv_ref), (WP, wp_ref), (WC, wc_ref)):
        out_ref[at : at + 48, :] = ref[...]
    out_ref[WO : WO + 48, :] = wo_ref[0]
    out_ref[WO + 48 : WO + 96, :] = wo_ref[1]
    out_ref[WI : WI + 192, :] = jnp.concatenate([wi_ref[0], wi_ref[1]], axis=1)
    out_ref[WU : WU + 192, :] = jnp.concatenate([wu_ref[0], wu_ref[1]], axis=1)
    out_ref[WM : WM + 64, :] = jnp.zeros((64, 384), bf16)
    out_ref[WM : WM + 36, 0:48] = wm_ref[...]
    zeros = jnp.zeros((1, 336), f32)
    lines = [jnp.concatenate([bi_ref[0:1].astype(f32), bi_ref[1:2].astype(f32)], axis=1)]
    for ref in (bq_ref, bp_ref, bc_ref):
        lines.append(jnp.concatenate([ref[...].astype(f32), zeros], axis=1))
    lines.append(jnp.zeros((12, 384), f32))
    out_ref[WB : WB + 16, :] = jnp.concatenate(lines, axis=0).astype(bf16)


def keys_aug(kv):
    keys = kv[0:48]
    return jnp.concatenate([keys, keys, jnp.ones((16, keys.shape[1]), bf16)], axis=0)


def vals_aug(kv):
    vals = kv[48:96]
    return jnp.concatenate([vals, jnp.ones((16, vals.shape[1]), bf16)], axis=0)


def split3(value):
    high = value.astype(bf16)
    rest = value - high.astype(f32)
    mid = rest.astype(bf16)
    low = (rest - mid.astype(f32)).astype(bf16)
    return high, mid, low


def scaled_queries(q):
    scaled = q.astype(f32) * (math.log2(math.e) / math.sqrt(48.0))
    high = scaled.astype(bf16)
    low = (scaled - high.astype(f32)).astype(bf16)
    return high, low


def flash_body(*refs, first, last, blocks):
    refs = list(refs)
    q_ref = refs.pop(0)
    tp_ref = refs.pop(0) if last else None
    kv_refs = [refs.pop(0) for _ in range(blocks)]
    if first:
        m_out, acc_out = refs
        m_now = acc_now = None
    else:
        m_in, acc_in = refs.pop(0), refs.pop(0)
        m_now, acc_now = m_in[0:1, :], acc_in[...]
    q = q_ref[...]
    width = q.shape[1]
    high, low = scaled_queries(q)
    q_aug = jnp.concatenate([high, low, jnp.zeros((16, width), bf16)], axis=0)
    for kv_ref in kv_refs:
        kv = kv_ref[...]
        scores = dg(keys_aug(kv), q_aug, 0, 0)
        top = jnp.max(scores, axis=0, keepdims=True)
        m_new = top if m_now is None else jnp.maximum(m_now, top)
        probs = jnp.exp2(scores - m_new).astype(bf16)
        part = dg(vals_aug(kv), probs, 1, 0)
        acc_now = part if m_now is None else acc_now * jnp.exp2(m_now - m_new) + part
        m_now = m_new
    if not last:
        if not first:
            m_out, acc_out = refs
        m_out[...] = jnp.broadcast_to(m_now, (8, width))
        acc_out[...] = acc_now
        return
    raw_ref, lse_ref, own_ref, beside_ref, beyond_ref, low_scr = refs
    total = acc_now[48:49, :]
    raw = acc_now[0:48, :] / total
    raw_ref[...] = raw
    lse_ref[...] = jnp.broadcast_to(m_now + jnp.log2(total), (8, width))
    low_scr[...] = raw.astype(bf16)
    quarter = width // 4
    mp = tp_ref[0]
    for at, ref in ((mp, own_ref), (mp ^ 1, beside_ref)):
        ref[...] = low_scr[:, pl.ds(pl.multiple_of(at * quarter, quarter), quarter)]
    half = 2 * quarter
    beyond_ref[...] = low_scr[:, pl.ds(pl.multiple_of((1 - (mp >> 1)) * half, half), half)]


def flash(q, kvs, state, place=None, after=()):
    width = q.shape[1]
    first, last = state is None, place is not None
    args = [q] + ([place] if last else []) + list(kvs) + ([] if first else list(state))
    if last:
        outs = [((48, width), f32), ((8, width), f32)] + [
            ((48, width // n), bf16) for n in (4, 4, 2)
        ]
        scratch = [pltpu.VMEM((48, width), bf16)]
    else:
        outs, scratch = [((8, width), f32), ((64, width), f32)], []
    return call(
        functools.partial(flash_body, first=first, last=last, blocks=len(kvs)),
        outs, args, us=2.4 * len(kvs), scratch=scratch, smem=(1,) if last else (), after=after,
    )


def back_prepare_body(place_ref, q_ref, lse_ref, raw_ref, g0, g1, g2, g3, qa_ref, da_ref):
    q = q_ref[...]
    width = q.shape[1]
    quarter = width // 4
    high, low = scaled_queries(q)
    lines = split3(-lse_ref[0:1, :])
    pad = jnp.zeros((13, width), bf16)
    qa_ref[...] = jnp.concatenate([high, low, *lines, pad], axis=0)
    place = place_ref[0]
    for s, ref in enumerate((g0, g1, g2.at[0:48], g3.at[48:96])):
        at = pl.multiple_of((place ^ s) * quarter, quarter)
        da_ref[0:48, pl.ds(at, quarter)] = ref[...]
    grad = da_ref[0:48, :]
    delta = jnp.sum(grad.astype(f32) * raw_ref[...], axis=0, keepdims=True)
    da_ref[48:64, :] = jnp.concatenate([*split3(-delta), pad], axis=0)


def back_body(*refs, first, blocks, plus):
    refs = list(refs)
    q_ref, qa_ref, da_ref = refs[:3]
    kv_refs = refs[3 : 3 + blocks]
    refs = refs[3 + blocks :]
    dq_in = None if first else refs.pop(0)
    plus_refs = []
    for count, place in plus:
        group = [refs.pop(0) for _ in range(count)]
        plus_refs.append([group[0].at[place], *group[1:]])
    dq_out, *outs = refs
    if not plus:
        outs = [outs[0].at[n] for n in range(blocks)]
        plus_refs = [[]] * blocks
    q, grad = q_ref[...], da_ref[0:48, :]
    q_aug, grad_aug = qa_ref[...], da_ref[...]
    step = 256
    dq = None if first else dq_in[...]
    for kv_ref, out, group in zip(kv_refs, outs, plus_refs, strict=True):
        kv = kv_ref[...]
        keys, vals = keys_aug(kv), vals_aug(kv)
        for at in range(0, kv.shape[1], step):
            span = slice(at, at + step)
            probs = jnp.exp2(dg(keys[:, span], q_aug, 0, 0))
            grad_probs = dg(vals[:, span], grad_aug, 0, 0)
            grad_scores = (probs * grad_probs).astype(bf16)
            dv = dg(grad, probs.astype(bf16), 1, 1)
            dk = dg(q, grad_scores, 1, 1)
            part = dg(kv[0:48, span], grad_scores, 1, 0)
            dq = part if dq is None else dq + part
            both = jnp.concatenate([dk, dv], axis=0)
            for ref in group:
                both = both + ref[:, span].astype(f32)
            out[:, span] = both.astype(out.dtype)
    dq_out[...] = dq


def back(q, q_aug, grad_aug, kvs, dq, plus=(), dtypes=(), after=()):
    width = q.shape[1]
    shape = kvs[0].shape
    args = [q, q_aug, grad_aug, *kvs] + ([] if dq is None else [dq])
    args += [array for arrays, _ in plus for array in arrays]
    outs = [(shape, dtype) for dtype in dtypes] if plus else [((len(kvs), *shape), bf16)]
    dq, *parts = call(
        functools.partial(
            back_body, first=dq is None, blocks=len(kvs),
            plus=[(len(arrays), place) for arrays, place in plus],
        ),
        [((48, width), f32), *outs], args, us=3.5 * len(kvs), after=after,
    )
    return dq, parts


def gather_body(*refs):
    *parts, out_ref = refs
    total = parts[0][...]
    for ref in parts[1:]:
        total = total + ref[...].astype(f32)
    out_ref[...] = total


def back_join_body(dq_ref, dkv_ref, *refs):
    *news, out_ref = refs
    scale = 1.0 / math.sqrt(48.0)
    out_ref[0:48, :] = (dq_ref[...] * scale).astype(bf16)
    total = dkv_ref[...]
    for ref in news:
        total = total + ref[...].astype(f32)
    out_ref[48:96, :] = (total[0:48] * scale).astype(bf16)
    out_ref[96:144, :] = total[48:96].astype(bf16)


def tap_places(mp, heads, taps):
    rows = lax.broadcasted_iota(jnp.int32, (48, 8 * taps), 0)
    cols = lax.broadcasted_iota(jnp.int32, (48, 8 * taps), 1)
    s = cols & 7
    wanted = (s ^ mp) * taps + (cols >> 3)
    return ((rows == wanted) & (s < heads)).astype(f32).astype(bf16)


def lift(value, axis, shift, keep):
    size = value.shape[axis]
    rolled = pltpu.roll(value, (size - shift) % size, axis)
    return rolled[:keep] if axis == 0 else rolled[:, :keep]


def conv_body(
    place_ref, xe_ref, dk_ref, bk_ref, p0, p1, p2, p3,
    mix_ref, depth_ref, q_ref, kc_ref, tp_ref, cv_ref, scr, sems, *, rim, quarter, taps,
):
    packs = Rows((p0, p1, p2, p3), scr, sems, CONV_ROWS)
    xe = xe_ref[...]
    x_own = xe[rim : rim + quarter]
    wide = xe.astype(f32)
    reach = taps // 2
    kernel = dk_ref[...].astype(f32)
    depth = None
    for j in range(taps):
        term = lift(wide, 0, rim - reach + j, quarter) * kernel[j : j + 1, :]
        depth = term if depth is None else depth + term
    depth_low = depth.astype(bf16)
    depth_ref[...] = depth_low
    position = place_ref[1] + lax.broadcasted_iota(jnp.int32, (1, xe.shape[0]), 1) - rim
    inside = (position >= 0) & (position < place_ref[2])
    for n in range(3):
        packs.wait(n)
    attn = []
    for s in range(4):
        own = slice(48 * s, 48 * s + 48)
        bias = packs.get(s, WB, WB + 16, slice(0, 48))
        q = (
            dg(packs.get(s, WQ, WQ + 48), x_own, 1, 1) + outer_ones(bias[1:2], quarter)
        ).astype(bf16)
        kc = dg(packs.get(s, WP, WP + 48), depth_low, 1, 1) + outer_ones(bias[2:3], quarter)
        cv = dg(packs.get(s, WC, WC + 48), xe, 1, 1) + outer_ones(bias[3:4], xe.shape[0])
        q_ref[own, :] = q
        kc_ref[own, :] = kc
        cv_ref[own, :] = jnp.where(inside, cv, 0.0)
        attn.append((kc * q.astype(f32)).astype(bf16))
    attn = jnp.concatenate(attn, axis=0)
    hot = tap_places(place_ref[0], 4, taps)
    wk = [dg(packs.get(s, WM, WM + 48, slice(0, 48)), hot, 0, 0) for s in range(4)]
    wk = jnp.concatenate(wk, axis=0).astype(bf16)
    bias = dg(bk_ref[...], hot[0 : bk_ref.shape[1], :], 1, 0).astype(bf16)
    logits = dg(wk, attn, 0, 0) + outer_ones(bias, quarter)
    tiles = [logits[8 * j : 8 * j + 8] for j in range(taps)]
    top = functools.reduce(jnp.maximum, tiles)
    tiles = [jnp.exp(tile - top) for tile in tiles]
    total = functools.reduce(jnp.add, tiles)
    tiles = [tile / total for tile in tiles]
    for j in range(taps):
        tp_ref[8 * j : 8 * j + 8, :] = tiles[j]
    cv = cv_ref[...]
    mix = [None] * 4
    for j in range(taps):
        moved = lift(cv, 1, rim - reach + j, quarter)
        for s in range(4):
            term = tiles[j][s : s + 1, :] * moved[48 * s : 48 * s + 48]
            mix[s] = term if mix[s] is None else mix[s] + term
    for s in range(4):
        mix_ref[48 * s : 48 * s + 48, :] = mix[s].astype(bf16)


def conv_back_body(
    place_ref, xe_ref, dk_ref, p0, p1, p2, p3, q_ref, kc_ref, tp_ref, cv_ref, gm_ref, gh_ref,
    ex_ref, pre_ref, gk_ref, kb_ref, dpt_ref, cve_ref, tok_ref, edge_ref, scr, sems,
    *, rim, quarter, taps,
):
    packs = Rows((p0, p1, p2, p3), scr, sems, BACK_ROWS)
    reach = taps // 2
    ext = xe_ref.shape[0]
    grad_mix = gm_ref[...]
    cv = cv_ref[...]
    probs = [tp_ref[8 * j : 8 * j + 8, :] for j in range(taps)]
    grads = []
    weighted = None
    for j in range(taps):
        moved = lift(cv, 1, rim - reach + j, quarter) * grad_mix
        lines = [jnp.sum(moved[48 * s : 48 * s + 48], axis=0, keepdims=True) for s in range(4)]
        tile = jnp.concatenate(lines + [jnp.zeros((4, quarter), f32)], axis=0)
        grads.append(tile)
        term = probs[j] * tile
        weighted = term if weighted is None else weighted + term
    gtl = jnp.concatenate(
        [probs[j] * (grads[j] - weighted) for j in range(taps)], axis=0
    ).astype(bf16)
    hot = tap_places(place_ref[0], 4, taps)
    for n in range(3):
        packs.wait(n)
    wk = [dg(packs.get(s, WM, WM + 48, slice(0, 48)), hot, 0, 0) for s in range(4)]
    wk = jnp.concatenate(wk, axis=0).astype(bf16)
    q = q_ref[...].astype(f32)
    kc = kc_ref[...]
    attn = (kc * q).astype(bf16)
    plain = dg(hot, gtl, 1, 0).astype(bf16)
    for s in range(4):
        gk_ref[s] = dg(plain, attn[48 * s : 48 * s + 48], 1, 1)
    kb_ref[...] = dg(plain, jnp.ones((128, quarter), bf16), 1, 1)
    grad_attn = dg(wk, gtl, 1, 0)
    extra = (grad_attn * kc).astype(bf16)
    ex_ref[...] = extra
    grad_kc = (grad_attn * q).astype(bf16)
    pre_ref[...] = grad_kc
    wp = packs.all(WP, WP + 48)
    dvals = dg(grad_kc, wp, 0, 0)
    wide = xe_ref[...].astype(f32)
    kernel = dk_ref[...].astype(f32)
    tail = jnp.zeros((ext - quarter, dvals.shape[1]), f32)
    padded = jnp.concatenate([dvals, tail], axis=0)
    depth = None
    lines = []
    for j in range(taps):
        moved = lift(wide, 0, rim - reach + j, quarter)
        lines.append(jnp.sum(moved * dvals, axis=0, keepdims=True))
        term = pltpu.roll(padded, rim - reach + j, 0) * kernel[j : j + 1, :]
        depth = term if depth is None else depth + term
    lines.append(jnp.zeros((16 - taps, dvals.shape[1]), f32))
    dpt_ref[...] = jnp.concatenate(lines, axis=0)
    side = jnp.zeros((4 * 48, ext - quarter), f32)
    spread = None
    for j in range(taps):
        rows = [probs[j][s : s + 1, :] * grad_mix[48 * s : 48 * s + 48] for s in range(4)]
        full = jnp.concatenate([jnp.concatenate(rows, axis=0), side], axis=1)
        term = pltpu.roll(full, rim - reach + j, 1)
        spread = term if spread is None else spread + term
    position = place_ref[1] + lax.broadcasted_iota(jnp.int32, (1, ext), 1) - rim
    inside = (position >= 0) & (position < place_ref[2])
    spread = jnp.where(inside, spread, 0.0).astype(bf16)
    cve_ref[...] = spread
    wc = packs.all(WC, WC + 48)
    wq = packs.all(WQ, WQ + 48)
    tokens = depth + dg(spread, wc, 0, 0)
    own = dg(extra, wq, 0, 0) + gh_ref[...]
    end = rim + quarter
    tok_ref[0:16, :] = tokens[rim - 16 : rim].astype(bf16)
    tok_ref[16 : quarter + 16, :] = (tokens[rim:end] + own).astype(bf16)
    tok_ref[quarter + 16 :, :] = tokens[end : end + 16].astype(bf16)
    edge_ref[...] = jnp.where(place_ref[0] == 0, tokens[rim - 16 : rim], tokens[end : end + 16])


def norm(hidden):
    centred = hidden - jnp.mean(hidden, axis=-1, keepdims=True)
    inverse = lax.rsqrt(jnp.mean(centred * centred, axis=-1, keepdims=True) + EPSILON)
    return centred * inverse, inverse


def norm_back(grad, normed, inverse, gain):
    scaled = grad * gain
    return inverse * (
        scaled
        - jnp.mean(scaled, axis=-1, keepdims=True)
        - normed * jnp.mean(scaled * normed, axis=-1, keepdims=True)
    )


def feed_body(
    place_ref, r0, r1, r2, r3, mix_ref, p0, p1, p2, p3, x_ref, cot_ref, lines_ref,
    out_ref, c0, c1, c23, gmix_ref, a_ref, act_ref, gpre_ref, low_ref, zed_ref, gm_ref,
    gh_ref, vec_ref, slope_scr, scr, sems,
):
    packs = Rows((p0, p1, p2, p3), scr, sems, FEED_ROWS)
    both = []
    quarter = x_ref.shape[0]
    own = pl.ds(pl.multiple_of((place_ref[0] & 1) * quarter, quarter), quarter)
    for s, context in enumerate((r0[...], r1[...], r2[:, own], r3[:, own])):
        both += [context, mix_ref[48 * s : 48 * s + 48, :]]
    both = jnp.concatenate(both, axis=0)
    a_ref[...] = both
    packs.wait(0)
    w_out = packs.all(WO, WO + 96)
    mixed = dg(both, w_out, 0, 0) + lines_ref[0:1, :]
    normed1, inverse1 = norm(mixed + x_ref[...].astype(f32))
    gain1, gain2 = lines_ref[1:2, :], lines_ref[4:5, :]
    low = (normed1 * gain1 + lines_ref[2:3, :]).astype(bf16)
    low_ref[...] = low
    halves = [low[:, 0:192], low[:, 192:384]]
    packs.wait(1)
    outer = [None, None]
    for g in range(2):
        lanes = slice(192 * g, 192 * g + 192)
        for s in range(4):
            pre = dg(halves[g], packs.get(s, WI, WI + 192, lanes), 1, 0)
            pre = pre + packs.get(s, WB, WB + 16, lanes)[0:1].astype(f32)
            cdf = 0.5 * (1.0 + lax.erf(pre * math.sqrt(0.5)))
            pdf = jnp.exp(-0.5 * pre * pre) * (1.0 / math.sqrt(2.0 * math.pi))
            slope_scr[2 * s + g] = cdf + pre * pdf
            act = (pre * cdf).astype(bf16)
            act_ref[2 * s + g] = act
            term = dg(act, packs.get(s, WU, WU + 192, lanes), 1, 0)
            outer[g] = term if outer[g] is None else outer[g] + term
    outer = jnp.concatenate(outer, axis=1) + lines_ref[3:4, :]
    normed2, inverse2 = norm(outer + low.astype(f32))
    out_ref[...] = (normed2 * gain2 + lines_ref[5:6, :]).astype(bf16)
    cot = cot_ref[...].astype(f32)
    grad_h2 = norm_back(cot, normed2, inverse2, gain2)
    zed = grad_h2.astype(bf16)
    zed_ref[...] = zed
    halves = [zed[:, 0:192], zed[:, 192:384]]
    back = [None, None]
    for g in range(2):
        lanes = slice(192 * g, 192 * g + 192)
        for s in range(4):
            grad_act = dg(halves[g], packs.get(s, WU, WU + 192, lanes), 1, 1)
            gpre = (grad_act * slope_scr[2 * s + g]).astype(bf16)
            gpre_ref[2 * s + g] = gpre
            term = dg(gpre, packs.get(s, WI, WI + 192, lanes), 1, 1)
            back[g] = term if back[g] is None else back[g] + term
    grad_norm1 = jnp.concatenate(back, axis=1) + grad_h2
    grad_h1 = norm_back(grad_norm1, normed1, inverse1, gain1)
    gh_ref[...] = grad_h1
    gm = grad_h1.astype(bf16)
    gm_ref[...] = gm
    grads = dg(w_out, gm, 1, 1)
    for s, ref in enumerate((c0, c1, c23.at[0:48], c23.at[48:96])):
        ref[...] = grads[96 * s : 96 * s + 48].astype(bf16)
        gmix_ref[48 * s : 48 * s + 48, :] = grads[96 * s + 48 : 96 * s + 96]
    sums = [gm.astype(f32), grad_norm1 * normed1, grad_norm1, zed.astype(f32), cot * normed2, cot]
    lines = [jnp.sum(item, axis=0, keepdims=True) for item in sums]
    lines.append(jnp.zeros((2, 384), f32))
    vec_ref[...] = jnp.concatenate(lines, axis=0)


def weights_body(
    x_ref, xe_ref, a_ref, act_ref, gpre_ref, low_ref, zed_ref, gm_ref, vec_ref,
    pre_ref, depth_ref, gk_ref, kb_ref, dpt_ref, cve_ref, ex_ref, o0, o1, o2, o3, mark_ref,
    *, quarter, taps,
):
    outs = (o0, o1, o2, o3)
    mark_ref[...] = jnp.zeros_like(mark_ref)
    x_own = x_ref[...]
    extra, spread = ex_ref[...], cve_ref[...]
    g_query = dg(extra, x_own, 1, 0)
    q_bias = jnp.sum(extra.astype(f32), axis=1, keepdims=True)
    g_conv = dg(spread, xe_ref[...], 1, 0)
    c_bias = jnp.sum(spread.astype(f32), axis=1, keepdims=True)
    pre = pre_ref[...]
    g_point = dg(pre, depth_ref[...], 1, 0)
    p_bias = jnp.sum(pre.astype(f32), axis=1, keepdims=True)
    low, zed, gm = low_ref[...], zed_ref[...], gm_ref[...]
    lane = lax.broadcasted_iota(jnp.int32, (48, 128), 1)
    ones = jnp.ones((8, quarter), bf16)
    for s, out in enumerate(outs):
        own = slice(48 * s, 48 * s + 48)
        out[GP : GP + 48, :] = g_point[own].astype(bf16)
        out[GC : GC + 48, :] = g_conv[own].astype(bf16)
        out[GQ : GQ + 48, :] = g_query[own].astype(bf16)
        out[GO : GO + 96, :] = dg(a_ref[96 * s : 96 * s + 96, :], gm, 1, 0).astype(bf16)
        inner, outer, bias = [], [], []
        for g in range(2):
            lanes = slice(192 * g, 192 * g + 192)
            gpre = gpre_ref[2 * s + g]
            inner.append(dg(low[:, lanes], gpre, 0, 0))
            outer.append(dg(act_ref[2 * s + g], zed[:, lanes], 0, 0))
            bias.append(dg(ones, gpre, 1, 0)[0:1])
        out[GI : GI + 192, :] = jnp.concatenate(inner, axis=1).astype(bf16)
        out[GU : GU + 192, :] = jnp.concatenate(outer, axis=1).astype(bf16)
        tile = jnp.concatenate([gk_ref[s], jnp.zeros((48, 80), f32)], axis=1)
        tile = jnp.where(lane == 64, p_bias[own], tile)
        tile = jnp.where(lane == 65, c_bias[own], tile)
        tile = jnp.where(lane == 66, kb_ref[...], tile)
        tile = jnp.where(lane == 67, q_bias[own], tile)
        out[GM : GM + 48, 0:128] = tile.astype(bf16)
        out[GM : GM + 48, 128:384] = jnp.zeros((48, 256), bf16)
        bias = jnp.concatenate(bias, axis=1)
        lines = jnp.concatenate([bias, dpt_ref[0:taps, :], vec_ref[0:6, :]], axis=0)
        out[GV : GV + 16, :] = lines.astype(bf16)
        if out.shape[0] > GRAD_ROWS:
            out[GRAD_ROWS:, :] = jnp.zeros((out.shape[0] - GRAD_ROWS, 384), bf16)


def add_body(a_ref, b_ref, out_ref):
    out_ref[...] = (a_ref[...].astype(f32) + b_ref[...].astype(f32)).astype(out_ref.dtype)


def fold_body(place_ref, a_ref, b_ref, c_ref, keep_ref, give_ref):
    x = place_ref[3]
    half = keep_ref.shape[0]
    for out, part in ((keep_ref, x), (give_ref, 1 - x)):
        rows = pl.ds(pl.multiple_of(part * half, 16), half)
        first = (a_ref[rows, :].astype(f32) + b_ref[rows, :].astype(f32)).astype(bf16).astype(f32)
        out[...] = (first + c_ref[rows, :].astype(f32)).astype(bf16)


def edge_body(place_ref, tok_ref, edge_ref, layer_ref, out_ref):
    mp = place_ref[0]
    rows = tok_ref.shape[0]
    out_ref[0:rows, :] = tok_ref[...]
    out_ref[rows:, :] = layer_ref[...]
    low, high = slice(16, 32), slice(rows - 32, rows - 16)

    @pl.when(mp == 0)
    def _():
        out_ref[low, :] = (tok_ref[low, :].astype(f32) + edge_ref[...]).astype(bf16)

    @pl.when(mp == 3)
    def _():
        out_ref[high, :] = (tok_ref[high, :].astype(f32) + edge_ref[...]).astype(bf16)


def unpack_body(
    place_ref, own_ref, other_ref,
    point_ref, conv_ref, query_ref, out_ref, inner_ref, outer_ref, kernel_ref, qb_ref, ib_ref,
    dep_ref, pb_ref, cb_ref, kb_ref, *refs, taps,
):
    *vec_refs, scr = refs
    x = place_ref[3]
    half = own_ref.shape[0]
    scr[pl.ds(pl.multiple_of(x * half, 16), half), :] = own_ref[...].astype(f32)
    scr[pl.ds(pl.multiple_of((1 - x) * half, 16), half), :] = other_ref[...].astype(f32)
    point_ref[...] = scr[GP : GP + 48, :]
    conv_ref[...] = scr[GC : GC + 48, :]
    query_ref[...] = scr[GQ : GQ + 48, :]
    out_ref[0] = scr[GO : GO + 48, :]
    out_ref[1] = scr[GO + 48 : GO + 96, :]
    for g in range(2):
        lanes = slice(192 * g, 192 * g + 192)
        inner_ref[g] = scr[GI : GI + 192, lanes]
        outer_ref[g] = scr[GU : GU + 192, lanes]
        ib_ref[g : g + 1, :] = scr[GV : GV + 1, lanes]
    kernel_ref[...] = scr[GM : GM + 36, 0:48]
    turned = jnp.transpose(scr[GM : GM + 48, 0:128], (1, 0))
    pb_ref[...] = turned[64]
    cb_ref[...] = turned[65]
    kb_ref[...] = turned[66, 0:36]
    qb_ref[...] = turned[64:72, :]
    dep_ref[...] = scr[GV + 1 : GV + 1 + taps, :]
    for n, ref in enumerate(vec_refs):
        ref[...] = scr[GV + 1 + taps + n, :]


def head_weights_body(g_ref, x_ref, out_ref):
    grads = g_ref[...]
    out_ref[0:144, :] = dg(grads, x_ref[...], 1, 0).astype(bf16)
    out_ref[144:160, :] = jnp.zeros((16, 384), bf16)
    sums = dg(jnp.ones((16, grads.shape[1]), bf16), grads, 1, 1)
    out_ref[144:160, 0:144] = sums.astype(bf16)


def head_unpack_body(
    total_ref, other_ref, part_ref, bias_ref, q_ref, k_ref, v_ref, qb_ref, vb_ref
):
    total = total_ref[...].astype(f32) + other_ref[...].astype(f32)
    q_ref[...] = total[0:48] + part_ref[...]
    k_ref[...] = total[48:96]
    v_ref[...] = total[96:144]
    qb_ref[...] = total[144, 0:48] + bias_ref[3, :]
    vb_ref[...] = total[144, 96:144]


def tokens_body(place_ref, t0, t1, t2, t3, layer_ref, out_ref, acc, *, quarter):
    mp = place_ref[0]
    parts = (t0, t1, t2, t3)
    for s, ref in enumerate(parts):
        at = pl.multiple_of((mp ^ s) * quarter, quarter)
        layer_ref[pl.ds(at, quarter), :] = ref[quarter + 32 :, :]
        acc[pl.ds(at + 16, quarter), :] = ref[16 : quarter + 16, :].astype(f32)
    for s, ref in enumerate(parts):
        at = pl.multiple_of((mp ^ s) * quarter, quarter)
        acc[pl.ds(at, 16), :] += ref[0:16, :].astype(f32)
        acc[pl.ds(at + quarter + 16, 16), :] += ref[quarter + 16 : quarter + 32, :].astype(f32)
    out_ref[...] = acc[16 : 4 * quarter + 16, :]


def input_grad_body(
    g0, g1, g2, g3, p0, p1, p2, p3, tok_ref, out_ref, rows, done, scr, sems, *, quarter
):
    packs = Rows((p0, p1, p2, p3), scr, sems, HEAD_ROWS)
    grads = jnp.concatenate([ref[...] for ref in (g0, g1, g2, g3)], axis=0)
    packs.wait(0)
    weights = packs.all(WQ, WQ + 144)
    copies = []
    for n in range(4):
        span = slice(n * quarter, n * quarter + quarter)
        rows[span, :] = dg(grads[:, span], weights, 0, 0) + tok_ref[span, :]
        at = pl.ds(n * quarter, quarter)
        copies.append(pltpu.make_async_copy(rows.at[at], out_ref.at[at], done.at[n]))
        copies[n].start()
    for copy in copies:
        copy.wait()


def local(
    inputs, w_query, b_query, w_key, w_value, b_value, depth_kernel, w_point, b_point, w_kernel,
    b_kernel, w_conv, b_conv, w_out, b_out, gain_one, shift_one, w_inner, b_inner, w_outer,
    b_outer, gain_two, shift_two, cotangent,
):
    blocks = lax.axis_size("ctx")
    outer = blocks // 2
    rows_here = inputs.shape[0]
    quarter = rows_here // 4
    taps = depth_kernel.shape[0]
    rim = 64
    ctx, mp = lax.axis_index("ctx"), lax.axis_index("mp")
    x_at, z_at = ctx % 2, ctx // 2
    place = jnp.stack(
        [mp, ctx * rows_here + mp * quarter, blocks * rows_here, x_at, z_at]
    ).astype(jnp.int32)

    def table(change):
        pairs = []
        for z in range(outer):
            for x in range(2):
                for y in range(2):
                    for c in range(2):
                        z2, x2, y2, c2 = change(z, x, y, c)
                        pairs.append(((2 * z + x) * 4 + 2 * y + c, (2 * z2 + x2) * 4 + 2 * y2 + c2))
        return pairs

    def send(value, change):
        return lax.ppermute(value, ("ctx", "mp"), table(change))

    def across_c(z, x, y, c):
        return (z, x, y, c ^ 1)

    def across_y(z, x, y, c):
        return (z, x, y ^ 1, c)

    def across_x(z, x, y, c):
        return (z, x ^ 1, y, c)

    def across_z(i):
        return lambda z, x, y, c: (z ^ i, x, y, c)

    def line(vector):
        return vector.reshape(1, -1)

    def plus(left, right, hbm=(), final=()):
        return call(add_body, [(left.shape, bf16)], [left, right], us=1, hbm=hbm, final=final)[0]

    tick = lax.optimization_barrier
    bits = [1 << n for n in range(outer.bit_length() - 1)]
    rest = [i for i in range(1, outer) if i not in bits]

    kv, q = call(
        project_body,
        [((96, rows_here), bf16), ((48, rows_here), bf16)],
        [inputs, w_query.T, line(b_query), w_key.T, w_value.T, line(b_value)], us=2.4,
        hbm=range(6),
    )
    zkv, skv = [kv] + [None] * (outer - 1), [send(kv, across_x)] + [None] * (outer - 1)
    for i in bits:
        zkv[i] = send(kv, across_z(i))
    pack, lines = call(
        pack_body,
        [((PACK_ROWS, 384), bf16), ((8, 384), f32)],
        [w_query.T, w_key.T, w_value.T, w_point.T, w_conv.T, w_out, w_inner, w_outer, w_kernel.T,
         line(b_query), line(b_point), line(b_conv), b_inner, b_out, gain_one, shift_one, b_outer,
         gain_two, shift_two],
        us=2.2, after=(q,), hbm=range(19), final=(0,),
    )
    rims = jnp.where(mp == 0, inputs[rows_here - rim :], inputs[:rim])
    x_quarter = lax.dynamic_slice_in_dim(inputs, mp * quarter, quarter, 0)
    cot_quarter = lax.dynamic_slice_in_dim(cotangent, mp * quarter, quarter, 0)
    state = flash(q, [kv], None)
    pack, rims, x_quarter, cot_quarter, place, lines, state, skv[0], *got = tick(
        (pack, rims, x_quarter, cot_quarter, place, lines, state, skv[0], *(zkv[i] for i in bits))
    )
    for i, item in zip(bits, got, strict=True):
        zkv[i] = item
        skv[i] = send(item, across_x)
    for i in rest:
        zkv[i] = send(zkv[i & (i - 1)], across_z(i & -i))
    pack_beyond = send(pack, across_y)
    pairs = []
    for i in range(blocks - 1):
        pairs += [(4 * i, 4 * i + 4), (4 * i + 7, 4 * i + 3)]
    beside = lax.ppermute(rims, ("ctx", "mp"), pairs)
    todo = [skv[0], *(zkv[i] for i in bits)]
    for n in range(0, len(todo), 2):
        state = flash(q, todo[n : n + 2], state)
    state, beside, skv[bits[0]], *got = tick(
        (state, beside, skv[bits[0]], *(zkv[i] for i in rest))
    )
    for i, item in zip(rest, got, strict=True):
        zkv[i] = item
        skv[i] = send(item, across_x)
    todo = [skv[bits[0]], *got]
    for n in range(0, len(todo), 2):
        state = flash(q, todo[n : n + 2], state)
    state, pack_beyond, *got = tick((state, pack_beyond, *(skv[i] for i in bits[1:])))
    packs = [pack, send(pack, across_c), pack_beyond, send(pack_beyond, across_c)]
    for i, item in zip(bits[1:], got, strict=True):
        skv[i] = item
    todo = got + [skv[i] for i in rest]
    for n in range(0, len(todo) - 2, 2):
        state = flash(q, todo[n : n + 2], state)
    raw, lse, context, context_c, context_y = flash(q, todo[-2:], state, place)

    context, context_c, context_y, packs = tick((context, context_c, context_y, packs))
    heads_y = send(context_y, across_y)
    heads_c = send(context_c, across_c)
    extended = jnp.concatenate([beside, inputs, beside], axis=0)
    x_ext = lax.dynamic_slice_in_dim(extended, mp * quarter, quarter + 2 * rim, 0)
    ext = quarter + 2 * rim
    mix, depth, q_conv, key_conv, tap_probs, conv_vals = call(
        functools.partial(conv_body, rim=rim, quarter=quarter, taps=taps),
        [((192, quarter), bf16), ((quarter, 384), bf16), ((192, quarter), bf16),
         ((192, quarter), f32), ((8 * taps, quarter), f32), ((192, ext), f32)],
        [place, x_ext, depth_kernel, line(b_kernel), *packs],
        us=4.4, smem=(0,), final=range(1, 6), raw=range(4, 8), hbm=(3,),
        scratch=row_scratch(CONV_ROWS),
    )
    heads_y, heads_c, mix = tick((heads_y, heads_c, mix))
    heads = [context, heads_c, heads_y, send(heads_y, across_c)]
    (layer_quarter, c0, c1, c23, grad_mix, both, act, gpre, low, zed, gm, grad_h1, vec) = call(
        feed_body,
        [((quarter, 384), bf16)] + [((48 * n, quarter), bf16) for n in (1, 1, 2)]
        + [((192, quarter), f32), ((384, quarter), bf16), ((8, quarter, 192), bf16),
           ((8, quarter, 192), bf16), ((quarter, 384), bf16), ((quarter, 384), bf16),
           ((quarter, 384), bf16), ((quarter, 384), f32), ((8, 384), f32)],
        [place, *heads, mix, *packs, x_quarter, cot_quarter, lines],
        us=6.8, smem=(0,), raw=range(6, 10),
        scratch=[pltpu.VMEM((8, quarter, 192), f32), *row_scratch(FEED_ROWS)],
    )
    grads_y = send(c23, across_y)
    grads_c = send(c1, across_c)
    extra, grad_kc, g_kernel, k_bias, g_depth, spread, token_part, edge = call(
        functools.partial(conv_back_body, rim=rim, quarter=quarter, taps=taps),
        [((192, quarter), bf16), ((192, quarter), bf16), ((4, 48, 48), f32), ((48, 128), f32),
         ((16, 384), f32), ((192, ext), bf16), ((quarter + 32, 384), bf16), ((16, 384), f32)],
        [place, x_ext, depth_kernel, *packs, q_conv, key_conv, tap_probs, conv_vals, grad_mix,
         grad_h1],
        us=5.4, smem=(0,), raw=range(3, 7), scratch=row_scratch(BACK_ROWS),
    )
    grads_y, grads_c, extra = tick((grads_y, grads_c, extra))
    grads = [c0, grads_c, grads_y, send(grads_y, across_c)]
    all_rows = -(-GRAD_ROWS // 32) * 32
    *sums, mark = call(
        functools.partial(weights_body, quarter=quarter, taps=taps),
        [((all_rows, 384), bf16)] * 4 + [((8, 128), f32)],
        [x_quarter, x_ext, both, act, gpre, low, zed, gm, vec, grad_kc, depth, g_kernel,
         k_bias, g_depth, spread, extra],
        us=4.6, final=range(4),
    )
    grads, mark = tick((grads, mark))
    q_aug, grad_aug = call(
        back_prepare_body,
        [((112, rows_here), bf16), ((64, rows_here), bf16)],
        [place, q, lse, raw, *grads], us=1.8, smem=(0,),
    )

    order = sorted(range(outer), key=lambda i: (-i.bit_count(), -i))
    edge_pairs = []
    for i in range(blocks - 1):
        edge_pairs += [(4 * i + 4, 4 * i + 3), (4 * i + 3, 4 * i + 4)]
    found = {i: [] for i in range(outer)}
    cross_found = {}

    def cross(pair, dq, after=()):
        dq, (parts,) = back(q, q_aug, grad_aug, [skv[i] for i in pair], dq, after=after)
        return dq, parts

    def spread_out(pair, parts):
        other = send(parts, across_x)
        for n, i in enumerate(pair):
            cross_found[i] = (other, n)

    def own(group, dq, after=()):
        sums = []
        for i in group:
            other, place = cross_found[i]
            sums.append(([other, *found[i]] if i else [other], place))
        dtypes = [bf16 if i else f32 for i in group]
        dq, parts = back(
            q, q_aug, grad_aug, [zkv[i] for i in group], dq, sums, dtypes, after
        )
        dq, parts = tick((dq, parts))
        for i, part in zip(group, parts, strict=True):
            if i:
                found[i & (i - 1)].append(send(part, across_z(i & -i)))
                found[i] = []
        return dq, parts[-1]

    givens = [send(sums[3], across_c), send(sums[1], across_c)]
    edge = lax.ppermute(edge, ("ctx", "mp"), edge_pairs)
    piece = plus(sums[2], givens[0], hbm=(0,), final=(0,))
    beyond = send(piece, across_y)
    dq, parts = cross(order[:1], None, (piece,))
    dq, parts, edge, layer_quarter = tick((dq, parts, edge, layer_quarter))
    spread_out(order[:1], parts)
    dq, parts = cross(order[1:2], dq)
    dq, parts, given = tick((dq, parts, givens[1]))
    spread_out(order[1:2], parts)
    for n in range(2, outer, 2):
        dq, parts = cross(order[n : n + 2], dq)
        other, at = cross_found[order[n - 2]]
        dq, parts, other = tick((dq, parts, other))
        cross_found[order[n - 2]] = (other, at)
        spread_out(order[n : n + 2], parts)
        dq, _ = own(order[n - 2 : n - 1], dq)
        other, at = cross_found[order[n - 1]]
        dq, other = tick((dq, other))
        cross_found[order[n - 1]] = (other, at)
        if n == outer - 2:
            both_parts = call(
                edge_body, [((2 * quarter + 32, 384), bf16)],
                [place, token_part, edge, layer_quarter], us=1, smem=(0,), final=(0,),
            )[0]
            beyond, dq, found = tick((beyond, dq, found))
            mine, give = call(
                fold_body, [((all_rows // 2, 384), bf16)] * 2, [place, sums[0], given, beyond],
                us=1, smem=(0,), hbm=(1, 3),
            )
            given = send(give, across_x)
        dq, _ = own(order[n - 1 : n], dq)
    other, _ = cross_found[0]
    dq, other = tick((dq, other, mine))[:2]
    cross_found.update({i: (other, n) for n, i in enumerate(order[-2:])})
    dq, last_part = own(order[-2:], dq, (mine, give))
    given, both_parts, dq = tick((given, both_parts, dq))
    piece = plus(mine, given)
    given = send(piece, across_z(bits[0]))
    parts_beyond = send(both_parts, across_y)
    parts_beside = send(both_parts, across_c)
    *early, late = found[0]
    early, dq, _ = tick((early, dq, piece))
    last_part = call(
        gather_body, [((96, rows_here), f32)], [last_part, *early], us=JOIN_PACE,
    )[0]
    late, last_part = tick((late, last_part))

    head_grads = call(
        back_join_body, [((144, rows_here), bf16)], [dq, last_part, late], us=2.1,
    )[0]
    head_w = call(
        head_weights_body, [((160, 384), bf16)], [head_grads, inputs], us=2.2,
    )[0]
    head_other = send(head_w, across_x)
    grads_beyond = send(head_grads, across_y)
    grads_beside = send(head_grads, across_c)
    given, parts_beyond, head_w = tick((given, parts_beyond, head_w))
    parts_other = send(parts_beyond, across_c)
    if len(bits) > 1:
        piece = plus(piece, given)
        given = send(piece, across_z(bits[1]))
    parts_other = tick((parts_other, piece))[0]
    both = [both_parts, parts_beside, parts_beyond, parts_other]
    layer_out, tokens = call(
        functools.partial(tokens_body, quarter=quarter),
        [((rows_here, 384), bf16), ((rows_here, 384), f32)],
        [place, *both], us=2.3, smem=(0,), final=(0,), hbm=(1,), after=(head_w,),
        scratch=[pltpu.VMEM((rows_here + 32, 384), f32)],
    )
    head_other, _ = tick((head_other, layer_out))
    head_w = plus(head_w, head_other)
    head_other = send(head_w, across_z(bits[0]))
    grads_beyond, head_w = tick((grads_beyond, head_w))
    grads_other = send(grads_beyond, across_c)
    for n, bit in enumerate(bits[1:]):
        head_other = tick((head_other, grads_beyond))[0]
        head_w = plus(head_w, head_other)
        head_other = send(head_w, across_z(bit))
        given = tick((given, head_w))[0]
        piece = plus(piece, given)
        given = send(piece, across_z(bits[n + 2]) if n + 2 < len(bits) else across_x)
    grads_other, _ = tick((grads_other, piece))
    inputs_grad = call(
        functools.partial(input_grad_body, quarter=quarter),
        [((rows_here, 384), f32)],
        [head_grads, grads_beside, grads_beyond, grads_other, *packs, tokens], us=3.0,
        raw=range(4, 8), final=(0,), raw_out=(0,),
        scratch=[
            pltpu.VMEM((rows_here, 384), f32), pltpu.SemaphoreType.DMA((4,)),
            *row_scratch(HEAD_ROWS),
        ],
    )[0]
    other_piece, _ = tick((given, inputs_grad))
    (point, conv, query_part, grad_out, grad_inner, grad_outer, kernel, biases, i_bias, grad_depth,
     p_bias, c_bias, k_bias, *vecs) = call(
        functools.partial(unpack_body, taps=taps),
        [((48, 384), f32)] * 3 + [((2, 48, 384), f32), ((2, 192, 192), f32),
         ((2, 192, 192), f32), ((36, 48), f32), ((8, 48), f32), ((2, 192), f32), ((taps, 384), f32),
         ((48,), f32), ((48,), f32), ((36,), f32)] + [((384,), f32)] * 6,
        [place, piece, other_piece], us=2.3, smem=(0,), final=(0, 1, 3, 4, 5, 6, *range(8, 19)),
        scratch=[pltpu.VMEM((all_rows, 384), f32)],
    )
    query, key, value, q_bias, v_bias = call(
        head_unpack_body,
        [((48, 384), f32)] * 3 + [((48,), f32)] * 2,
        [head_w, head_other, query_part, biases], us=1.7, final=range(5),
    )

    return (
        layer_out, inputs_grad, query.T, q_bias, key.T, value.T, v_bias, grad_depth, point.T,
        p_bias, kernel.T, k_bias, conv.T, c_bias, grad_out, vecs[0], vecs[1], vecs[2], grad_inner,
        i_bias, grad_outer, vecs[3], vecs[4], vecs[5],
    )


def solution(mesh):
    return jax.shard_map(
        local,
        mesh=mesh,
        in_specs=(
            P("ctx", None), P(None, "mp"), P("mp"), P(None, "mp"), P(None, "mp"), P("mp"), P(),
            P(None, "mp"), P("mp"), P("mp", None), P(), P(None, "mp"), P("mp"),
            P(None, "mp", None), P(), P(), P(), P(None, None, "mp"), P(None, "mp"),
            P(None, "mp", None), P(), P(), P(), P("ctx", None),
        ),
        out_specs=(
            P("ctx", None), P("ctx", None), P(None, "mp"), P("mp"), P(None, "mp"), P(None, "mp"),
            P("mp"), P(), P(None, "mp"), P("mp"), P("mp", None), P(), P(None, "mp"), P("mp"),
            P(None, "mp", None), P(), P(), P(), P(None, None, "mp"), P(None, "mp"),
            P(None, "mp", None), P(), P(), P(),
        ),
        check_vma=False,
    )
```

```python
import functools
import math

import jax
import jax.numpy as jnp
from jax import lax
from jax.experimental import pallas as pl
from jax.experimental.pallas import tpu as pltpu
from jax.sharding import PartitionSpec as P


EPSILON = 1e-12
KERNEL_BYTES = 24 * 2**20
PACE = 1e5
JOIN_PACE = 4e4
HINTS = {2: 3e9, 3: 3e9, 11: 1e10, 17: 3e9, 19: 1e10, 35: 1e10, 42: 1e9}
CALLS = []
f32 = jnp.float32
bf16 = jnp.bfloat16

WQ, WK, WV, WP, WC, WO, WI, WU, WM, WB = 0, 48, 96, 144, 192, 240, 336, 528, 720, 768
PACK_ROWS = 784
GP, GC, GQ, GO, GI, GU, GM, GV = 0, 48, 96, 144, 240, 432, 624, 672
GRAD_ROWS = 688


def dg(left, right, ld, rd):
    return lax.dot_general(
        left, right, (((ld,), (rd,)), ((), ())), preferred_element_type=f32
    )


def row(ref):
    return ref[...].astype(f32).reshape(1, -1)


class Rows:
    def __init__(self, refs, scr, sems, ranges):
        self.scr, self.copies, at = scr, [], 0
        for n, (low, high) in enumerate(ranges):
            span = pl.ds(at, high - low)
            copies = [
                pltpu.make_async_copy(ref.at[pl.ds(low, high - low)], scr.at[s, span], sems.at[s, n])
                for s, ref in enumerate(refs)
            ]
            self.copies.append((low, high, at, copies))
            at += high - low
        for *_, copies in self.copies:
            for copy in copies:
                copy.start()

    def wait(self, n):
        for copy in self.copies[n][3]:
            copy.wait()

    def get(self, s, low, high, lanes=slice(None)):
        for first, last, at, _ in self.copies:
            if first <= low and high <= last:
                return self.scr[s, at + low - first : at + high - first, lanes]
        raise ValueError("rows")

    def all(self, low, high):
        return jnp.concatenate([self.get(s, low, high) for s in range(4)], axis=0)


def row_scratch(ranges):
    rows = sum(high - low for low, high in ranges)
    return [pltpu.VMEM((4, rows, 384), bf16), pltpu.SemaphoreType.DMA((4, len(ranges)))]


CONV_ROWS = ((0, 48), (144, 240), (720, 784))
BACK_ROWS = ((720, 784), (144, 240), (0, 48))
FEED_ROWS = ((240, 336), (336, 784))
HEAD_ROWS = ((0, 144),)


def outer_ones(row, width):
    return dg(row, jnp.ones((row.shape[0], width), bf16), 0, 0)


def call(body, outs, args, us, scratch=(), smem=(), after=(), final=(), hbm=(), raw=(), raw_out=()):
    inputs = len(args)
    flops = HINTS.get(len(CALLS), us * PACE)
    CALLS.append(us)

    def whole(*refs):
        body(*refs[:inputs], *refs[inputs + len(after) :])

    specs = [
        pl.BlockSpec(
            memory_space=pltpu.SMEM if i in smem else pltpu.HBM if i in raw else pltpu.VMEM
        )
        for i in range(inputs)
    ]
    return pl.pallas_call(
        whole,
        in_specs=specs + [pl.BlockSpec(memory_space=pl.ANY)] * len(after),
        out_specs=[
            pl.BlockSpec(memory_space=pltpu.HBM if i in raw_out else pltpu.VMEM)
            for i in range(len(outs))
        ],
        out_shape=[
            pltpu.HBM(s, d) if i in final else pltpu.VMEM(s, d)
            for i, (s, d) in enumerate(outs)
        ],
        scratch_shapes=list(scratch),
        compiler_params=pltpu.CompilerParams(vmem_limit_bytes=KERNEL_BYTES),
        cost_estimate=pl.CostEstimate(flops=int(flops), bytes_accessed=0, transcendentals=0),
    )(
        *(
            arg
            if i in smem
            else pltpu.with_memory_space_constraint(arg, pltpu.HBM if i in hbm or i in raw else pltpu.VMEM)
            for i, arg in enumerate(args)
        ),
        *after,
    )


def project_body(x_ref, wq_ref, bq_ref, wk_ref, wv_ref, bv_ref, kv_ref, q_ref):
    x = x_ref[...]
    width = x.shape[0]
    weights = jnp.concatenate([wk_ref[...], wv_ref[...], wq_ref[...]], axis=0)
    found = dg(weights, x, 1, 1)
    kv_ref[0:48, :] = found[0:48].astype(bf16)
    kv_ref[48:96, :] = (found[48:96] + outer_ones(bv_ref[...], width)).astype(bf16)
    q_ref[...] = (found[96:144] + outer_ones(bq_ref[...], width)).astype(bf16)


def pack_body(
    wq_ref, wk_ref, wv_ref, wp_ref, wc_ref, wo_ref, wi_ref, wu_ref, wm_ref,
    bq_ref, bp_ref, bc_ref, bi_ref, bo_ref, g1_ref, s1_ref, bu_ref, g2_ref, s2_ref,
    out_ref, lines_ref,
):
    vectors = [row(ref) for ref in (bo_ref, g1_ref, s1_ref, bu_ref, g2_ref, s2_ref)]
    lines_ref[...] = jnp.concatenate([*vectors, jnp.zeros((2, 384), f32)], axis=0)
    for at, ref in ((WQ, wq_ref), (WK, wk_ref), (WV, wv_ref), (WP, wp_ref), (WC, wc_ref)):
        out_ref[at : at + 48, :] = ref[...]
    out_ref[WO : WO + 48, :] = wo_ref[0]
    out_ref[WO + 48 : WO + 96, :] = wo_ref[1]
    out_ref[WI : WI + 192, :] = jnp.concatenate([wi_ref[0], wi_ref[1]], axis=1)
    out_ref[WU : WU + 192, :] = jnp.concatenate([wu_ref[0], wu_ref[1]], axis=1)
    out_ref[WM : WM + 64, :] = jnp.zeros((64, 384), bf16)
    out_ref[WM : WM + 36, 0:48] = wm_ref[...]
    zeros = jnp.zeros((1, 336), f32)
    lines = [jnp.concatenate([bi_ref[0:1].astype(f32), bi_ref[1:2].astype(f32)], axis=1)]
    for ref in (bq_ref, bp_ref, bc_ref):
        lines.append(jnp.concatenate([ref[...].astype(f32), zeros], axis=1))
    lines.append(jnp.zeros((12, 384), f32))
    out_ref[WB : WB + 16, :] = jnp.concatenate(lines, axis=0).astype(bf16)


def keys_aug(kv):
    keys = kv[0:48]
    return jnp.concatenate([keys, keys, jnp.ones((16, keys.shape[1]), bf16)], axis=0)


def vals_aug(kv):
    vals = kv[48:96]
    return jnp.concatenate([vals, jnp.ones((16, vals.shape[1]), bf16)], axis=0)


def split3(value):
    high = value.astype(bf16)
    rest = value - high.astype(f32)
    mid = rest.astype(bf16)
    low = (rest - mid.astype(f32)).astype(bf16)
    return high, mid, low


def scaled_queries(q):
    scaled = q.astype(f32) * (math.log2(math.e) / math.sqrt(48.0))
    high = scaled.astype(bf16)
    low = (scaled - high.astype(f32)).astype(bf16)
    return high, low


def flash_body(*refs, first, last, blocks):
    refs = list(refs)
    q_ref = refs.pop(0)
    tp_ref = refs.pop(0) if last else None
    kv_refs = [refs.pop(0) for _ in range(blocks)]
    if first:
        m_out, acc_out = refs
        m_now = acc_now = None
    else:
        m_in, acc_in = refs.pop(0), refs.pop(0)
        m_now, acc_now = m_in[0:1, :], acc_in[...]
    q = q_ref[...]
    width = q.shape[1]
    high, low = scaled_queries(q)
    q_aug = jnp.concatenate([high, low, jnp.zeros((16, width), bf16)], axis=0)
    for kv_ref in kv_refs:
        kv = kv_ref[...]
        scores = dg(keys_aug(kv), q_aug, 0, 0)
        top = jnp.max(scores, axis=0, keepdims=True)
        m_new = top if m_now is None else jnp.maximum(m_now, top)
        probs = jnp.exp2(scores - m_new).astype(bf16)
        part = dg(vals_aug(kv), probs, 1, 0)
        acc_now = part if m_now is None else acc_now * jnp.exp2(m_now - m_new) + part
        m_now = m_new
    if not last:
        if not first:
            m_out, acc_out = refs
        m_out[...] = jnp.broadcast_to(m_now, (8, width))
        acc_out[...] = acc_now
        return
    raw_ref, lse_ref, own_ref, beside_ref, beyond_ref, low_scr = refs
    total = acc_now[48:49, :]
    raw = acc_now[0:48, :] / total
    raw_ref[...] = raw
    lse_ref[...] = jnp.broadcast_to(m_now + jnp.log2(total), (8, width))
    low_scr[...] = raw.astype(bf16)
    quarter = width // 4
    mp = tp_ref[0]
    for at, ref in ((mp, own_ref), (mp ^ 1, beside_ref)):
        ref[...] = low_scr[:, pl.ds(pl.multiple_of(at * quarter, quarter), quarter)]
    half = 2 * quarter
    beyond_ref[...] = low_scr[:, pl.ds(pl.multiple_of((1 - (mp >> 1)) * half, half), half)]


def flash(q, kvs, state, place=None, after=()):
    width = q.shape[1]
    first, last = state is None, place is not None
    args = [q] + ([place] if last else []) + list(kvs) + ([] if first else list(state))
    if last:
        outs = [((48, width), f32), ((8, width), f32)] + [
            ((48, width // n), bf16) for n in (4, 4, 2)
        ]
        scratch = [pltpu.VMEM((48, width), bf16)]
    else:
        outs, scratch = [((8, width), f32), ((64, width), f32)], []
    return call(
        functools.partial(flash_body, first=first, last=last, blocks=len(kvs)),
        outs, args, us=2.4 * len(kvs), scratch=scratch, smem=(1,) if last else (), after=after,
    )


def back_prepare_body(place_ref, q_ref, lse_ref, raw_ref, g0, g1, g2, g3, qa_ref, da_ref):
    q = q_ref[...]
    width = q.shape[1]
    quarter = width // 4
    high, low = scaled_queries(q)
    lines = split3(-lse_ref[0:1, :])
    pad = jnp.zeros((13, width), bf16)
    qa_ref[...] = jnp.concatenate([high, low, *lines, pad], axis=0)
    place = place_ref[0]
    for s, ref in enumerate((g0, g1, g2.at[0:48], g3.at[48:96])):
        at = pl.multiple_of((place ^ s) * quarter, quarter)
        da_ref[0:48, pl.ds(at, quarter)] = ref[...]
    grad = da_ref[0:48, :]
    delta = jnp.sum(grad.astype(f32) * raw_ref[...], axis=0, keepdims=True)
    da_ref[48:64, :] = jnp.concatenate([*split3(-delta), pad], axis=0)


def back_body(*refs, first, blocks, plus):
    refs = list(refs)
    q_ref, qa_ref, da_ref = refs[:3]
    kv_refs = refs[3 : 3 + blocks]
    refs = refs[3 + blocks :]
    dq_in = None if first else refs.pop(0)
    plus_refs = []
    for count, place in plus:
        group = [refs.pop(0) for _ in range(count)]
        plus_refs.append([group[0].at[place], *group[1:]])
    dq_out, *outs = refs
    if not plus:
        outs = [outs[0].at[n] for n in range(blocks)]
        plus_refs = [[]] * blocks
    q, grad = q_ref[...], da_ref[0:48, :]
    q_aug, grad_aug = qa_ref[...], da_ref[...]
    step = 256
    dq = None if first else dq_in[...]
    for kv_ref, out, group in zip(kv_refs, outs, plus_refs, strict=True):
        kv = kv_ref[...]
        keys, vals = keys_aug(kv), vals_aug(kv)
        for at in range(0, kv.shape[1], step):
            span = slice(at, at + step)
            probs = jnp.exp2(dg(keys[:, span], q_aug, 0, 0))
            grad_probs = dg(vals[:, span], grad_aug, 0, 0)
            grad_scores = (probs * grad_probs).astype(bf16)
            dv = dg(grad, probs.astype(bf16), 1, 1)
            dk = dg(q, grad_scores, 1, 1)
            part = dg(kv[0:48, span], grad_scores, 1, 0)
            dq = part if dq is None else dq + part
            both = jnp.concatenate([dk, dv], axis=0)
            for ref in group:
                both = both + ref[:, span].astype(f32)
            out[:, span] = both.astype(out.dtype)
    dq_out[...] = dq


def back(q, q_aug, grad_aug, kvs, dq, plus=(), dtypes=(), after=()):
    width = q.shape[1]
    shape = kvs[0].shape
    args = [q, q_aug, grad_aug, *kvs] + ([] if dq is None else [dq])
    args += [array for arrays, _ in plus for array in arrays]
    outs = [(shape, dtype) for dtype in dtypes] if plus else [((len(kvs), *shape), bf16)]
    dq, *parts = call(
        functools.partial(
            back_body, first=dq is None, blocks=len(kvs),
            plus=[(len(arrays), place) for arrays, place in plus],
        ),
        [((48, width), f32), *outs], args, us=3.5 * len(kvs), after=after,
    )
    return dq, parts


def gather_body(*refs):
    *parts, out_ref = refs
    total = parts[0][...]
    for ref in parts[1:]:
        total = total + ref[...].astype(f32)
    out_ref[...] = total


def back_join_body(dq_ref, dkv_ref, *refs):
    *news, out_ref = refs
    scale = 1.0 / math.sqrt(48.0)
    out_ref[0:48, :] = (dq_ref[...] * scale).astype(bf16)
    total = dkv_ref[...]
    for ref in news:
        total = total + ref[...].astype(f32)
    out_ref[48:96, :] = (total[0:48] * scale).astype(bf16)
    out_ref[96:144, :] = total[48:96].astype(bf16)


def tap_places(mp, heads, taps):
    rows = lax.broadcasted_iota(jnp.int32, (48, 8 * taps), 0)
    cols = lax.broadcasted_iota(jnp.int32, (48, 8 * taps), 1)
    s = cols & 7
    wanted = (s ^ mp) * taps + (cols >> 3)
    return ((rows == wanted) & (s < heads)).astype(f32).astype(bf16)


def lift(value, axis, shift, keep):
    size = value.shape[axis]
    rolled = pltpu.roll(value, (size - shift) % size, axis)
    return rolled[:keep] if axis == 0 else rolled[:, :keep]


def conv_body(
    place_ref, xe_ref, dk_ref, bk_ref, p0, p1, p2, p3,
    mix_ref, depth_ref, q_ref, kc_ref, tp_ref, cv_ref, scr, sems, *, rim, quarter, taps,
):
    packs = Rows((p0, p1, p2, p3), scr, sems, CONV_ROWS)
    xe = xe_ref[...]
    x_own = xe[rim : rim + quarter]
    wide = xe.astype(f32)
    reach = taps // 2
    kernel = dk_ref[...].astype(f32)
    depth = None
    for j in range(taps):
        term = lift(wide, 0, rim - reach + j, quarter) * kernel[j : j + 1, :]
        depth = term if depth is None else depth + term
    depth_low = depth.astype(bf16)
    depth_ref[...] = depth_low
    position = place_ref[1] + lax.broadcasted_iota(jnp.int32, (1, xe.shape[0]), 1) - rim
    inside = (position >= 0) & (position < place_ref[2])
    for n in range(3):
        packs.wait(n)
    attn = []
    for s in range(4):
        own = slice(48 * s, 48 * s + 48)
        bias = packs.get(s, WB, WB + 16, slice(0, 48))
        q = (
            dg(packs.get(s, WQ, WQ + 48), x_own, 1, 1) + outer_ones(bias[1:2], quarter)
        ).astype(bf16)
        kc = dg(packs.get(s, WP, WP + 48), depth_low, 1, 1) + outer_ones(bias[2:3], quarter)
        cv = dg(packs.get(s, WC, WC + 48), xe, 1, 1) + outer_ones(bias[3:4], xe.shape[0])
        q_ref[own, :] = q
        kc_ref[own, :] = kc
        cv_ref[own, :] = jnp.where(inside, cv, 0.0)
        attn.append((kc * q.astype(f32)).astype(bf16))
    attn = jnp.concatenate(attn, axis=0)
    hot = tap_places(place_ref[0], 4, taps)
    wk = [dg(packs.get(s, WM, WM + 48, slice(0, 48)), hot, 0, 0) for s in range(4)]
    wk = jnp.concatenate(wk, axis=0).astype(bf16)
    bias = dg(bk_ref[...], hot[0 : bk_ref.shape[1], :], 1, 0).astype(bf16)
    logits = dg(wk, attn, 0, 0) + outer_ones(bias, quarter)
    tiles = [logits[8 * j : 8 * j + 8] for j in range(taps)]
    top = functools.reduce(jnp.maximum, tiles)
    tiles = [jnp.exp(tile - top) for tile in tiles]
    total = functools.reduce(jnp.add, tiles)
    tiles = [tile / total for tile in tiles]
    for j in range(taps):
        tp_ref[8 * j : 8 * j + 8, :] = tiles[j]
    cv = cv_ref[...]
    mix = [None] * 4
    for j in range(taps):
        moved = lift(cv, 1, rim - reach + j, quarter)
        for s in range(4):
            term = tiles[j][s : s + 1, :] * moved[48 * s : 48 * s + 48]
            mix[s] = term if mix[s] is None else mix[s] + term
    for s in range(4):
        mix_ref[48 * s : 48 * s + 48, :] = mix[s].astype(bf16)


def conv_back_body(
    place_ref, xe_ref, dk_ref, p0, p1, p2, p3, q_ref, kc_ref, tp_ref, cv_ref, gm_ref, gh_ref,
    ex_ref, pre_ref, gk_ref, kb_ref, dpt_ref, cve_ref, tok_ref, edge_ref, scr, sems,
    *, rim, quarter, taps,
):
    packs = Rows((p0, p1, p2, p3), scr, sems, BACK_ROWS)
    reach = taps // 2
    ext = xe_ref.shape[0]
    grad_mix = gm_ref[...]
    cv = cv_ref[...]
    probs = [tp_ref[8 * j : 8 * j + 8, :] for j in range(taps)]
    grads = []
    weighted = None
    for j in range(taps):
        moved = lift(cv, 1, rim - reach + j, quarter) * grad_mix
        lines = [jnp.sum(moved[48 * s : 48 * s + 48], axis=0, keepdims=True) for s in range(4)]
        tile = jnp.concatenate(lines + [jnp.zeros((4, quarter), f32)], axis=0)
        grads.append(tile)
        term = probs[j] * tile
        weighted = term if weighted is None else weighted + term
    gtl = jnp.concatenate(
        [probs[j] * (grads[j] - weighted) for j in range(taps)], axis=0
    ).astype(bf16)
    hot = tap_places(place_ref[0], 4, taps)
    for n in range(3):
        packs.wait(n)
    wk = [dg(packs.get(s, WM, WM + 48, slice(0, 48)), hot, 0, 0) for s in range(4)]
    wk = jnp.concatenate(wk, axis=0).astype(bf16)
    q = q_ref[...].astype(f32)
    kc = kc_ref[...]
    attn = (kc * q).astype(bf16)
    plain = dg(hot, gtl, 1, 0).astype(bf16)
    for s in range(4):
        gk_ref[s] = dg(plain, attn[48 * s : 48 * s + 48], 1, 1)
    kb_ref[...] = dg(plain, jnp.ones((128, quarter), bf16), 1, 1)
    grad_attn = dg(wk, gtl, 1, 0)
    extra = (grad_attn * kc).astype(bf16)
    ex_ref[...] = extra
    grad_kc = (grad_attn * q).astype(bf16)
    pre_ref[...] = grad_kc
    wp = packs.all(WP, WP + 48)
    dvals = dg(grad_kc, wp, 0, 0)
    wide = xe_ref[...].astype(f32)
    kernel = dk_ref[...].astype(f32)
    tail = jnp.zeros((ext - quarter, dvals.shape[1]), f32)
    padded = jnp.concatenate([dvals, tail], axis=0)
    depth = None
    lines = []
    for j in range(taps):
        moved = lift(wide, 0, rim - reach + j, quarter)
        lines.append(jnp.sum(moved * dvals, axis=0, keepdims=True))
        term = pltpu.roll(padded, rim - reach + j, 0) * kernel[j : j + 1, :]
        depth = term if depth is None else depth + term
    lines.append(jnp.zeros((16 - taps, dvals.shape[1]), f32))
    dpt_ref[...] = jnp.concatenate(lines, axis=0)
    side = jnp.zeros((4 * 48, ext - quarter), f32)
    spread = None
    for j in range(taps):
        rows = [probs[j][s : s + 1, :] * grad_mix[48 * s : 48 * s + 48] for s in range(4)]
        full = jnp.concatenate([jnp.concatenate(rows, axis=0), side], axis=1)
        term = pltpu.roll(full, rim - reach + j, 1)
        spread = term if spread is None else spread + term
    position = place_ref[1] + lax.broadcasted_iota(jnp.int32, (1, ext), 1) - rim
    inside = (position >= 0) & (position < place_ref[2])
    spread = jnp.where(inside, spread, 0.0).astype(bf16)
    cve_ref[...] = spread
    wc = packs.all(WC, WC + 48)
    wq = packs.all(WQ, WQ + 48)
    tokens = depth + dg(spread, wc, 0, 0)
    own = dg(extra, wq, 0, 0) + gh_ref[...]
    end = rim + quarter
    tok_ref[0:16, :] = tokens[rim - 16 : rim].astype(bf16)
    tok_ref[16 : quarter + 16, :] = (tokens[rim:end] + own).astype(bf16)
    tok_ref[quarter + 16 :, :] = tokens[end : end + 16].astype(bf16)
    edge_ref[...] = jnp.where(place_ref[0] == 0, tokens[rim - 16 : rim], tokens[end : end + 16])


def norm(hidden):
    centred = hidden - jnp.mean(hidden, axis=-1, keepdims=True)
    inverse = lax.rsqrt(jnp.mean(centred * centred, axis=-1, keepdims=True) + EPSILON)
    return centred * inverse, inverse


def norm_back(grad, normed, inverse, gain):
    scaled = grad * gain
    return inverse * (
        scaled
        - jnp.mean(scaled, axis=-1, keepdims=True)
        - normed * jnp.mean(scaled * normed, axis=-1, keepdims=True)
    )


def feed_body(
    place_ref, r0, r1, r2, r3, mix_ref, p0, p1, p2, p3, x_ref, cot_ref, lines_ref,
    out_ref, c0, c1, c23, gmix_ref, a_ref, act_ref, gpre_ref, low_ref, zed_ref, gm_ref,
    gh_ref, vec_ref, slope_scr, scr, sems,
):
    packs = Rows((p0, p1, p2, p3), scr, sems, FEED_ROWS)
    both = []
    quarter = x_ref.shape[0]
    own = pl.ds(pl.multiple_of((place_ref[0] & 1) * quarter, quarter), quarter)
    for s, context in enumerate((r0[...], r1[...], r2[:, own], r3[:, own])):
        both += [context, mix_ref[48 * s : 48 * s + 48, :]]
    both = jnp.concatenate(both, axis=0)
    a_ref[...] = both
    packs.wait(0)
    w_out = packs.all(WO, WO + 96)
    mixed = dg(both, w_out, 0, 0) + lines_ref[0:1, :]
    normed1, inverse1 = norm(mixed + x_ref[...].astype(f32))
    gain1, gain2 = lines_ref[1:2, :], lines_ref[4:5, :]
    low = (normed1 * gain1 + lines_ref[2:3, :]).astype(bf16)
    low_ref[...] = low
    halves = [low[:, 0:192], low[:, 192:384]]
    packs.wait(1)
    outer = [None, None]
    for g in range(2):
        lanes = slice(192 * g, 192 * g + 192)
        for s in range(4):
            pre = dg(halves[g], packs.get(s, WI, WI + 192, lanes), 1, 0)
            pre = pre + packs.get(s, WB, WB + 16, lanes)[0:1].astype(f32)
            cdf = 0.5 * (1.0 + lax.erf(pre * math.sqrt(0.5)))
            pdf = jnp.exp(-0.5 * pre * pre) * (1.0 / math.sqrt(2.0 * math.pi))
            slope_scr[2 * s + g] = cdf + pre * pdf
            act = (pre * cdf).astype(bf16)
            act_ref[2 * s + g] = act
            term = dg(act, packs.get(s, WU, WU + 192, lanes), 1, 0)
            outer[g] = term if outer[g] is None else outer[g] + term
    outer = jnp.concatenate(outer, axis=1) + lines_ref[3:4, :]
    normed2, inverse2 = norm(outer + low.astype(f32))
    out_ref[...] = (normed2 * gain2 + lines_ref[5:6, :]).astype(bf16)
    cot = cot_ref[...].astype(f32)
    grad_h2 = norm_back(cot, normed2, inverse2, gain2)
    zed = grad_h2.astype(bf16)
    zed_ref[...] = zed
    halves = [zed[:, 0:192], zed[:, 192:384]]
    back = [None, None]
    for g in range(2):
        lanes = slice(192 * g, 192 * g + 192)
        for s in range(4):
            grad_act = dg(halves[g], packs.get(s, WU, WU + 192, lanes), 1, 1)
            gpre = (grad_act * slope_scr[2 * s + g]).astype(bf16)
            gpre_ref[2 * s + g] = gpre
            term = dg(gpre, packs.get(s, WI, WI + 192, lanes), 1, 1)
            back[g] = term if back[g] is None else back[g] + term
    grad_norm1 = jnp.concatenate(back, axis=1) + grad_h2
    grad_h1 = norm_back(grad_norm1, normed1, inverse1, gain1)
    gh_ref[...] = grad_h1
    gm = grad_h1.astype(bf16)
    gm_ref[...] = gm
    grads = dg(w_out, gm, 1, 1)
    for s, ref in enumerate((c0, c1, c23.at[0:48], c23.at[48:96])):
        ref[...] = grads[96 * s : 96 * s + 48].astype(bf16)
        gmix_ref[48 * s : 48 * s + 48, :] = grads[96 * s + 48 : 96 * s + 96]
    sums = [gm.astype(f32), grad_norm1 * normed1, grad_norm1, zed.astype(f32), cot * normed2, cot]
    lines = [jnp.sum(item, axis=0, keepdims=True) for item in sums]
    lines.append(jnp.zeros((2, 384), f32))
    vec_ref[...] = jnp.concatenate(lines, axis=0)


def weights_body(
    x_ref, xe_ref, a_ref, act_ref, gpre_ref, low_ref, zed_ref, gm_ref, vec_ref,
    pre_ref, depth_ref, gk_ref, kb_ref, dpt_ref, cve_ref, ex_ref, o0, o1, o2, o3, mark_ref,
    *, quarter, taps,
):
    outs = (o0, o1, o2, o3)
    mark_ref[...] = jnp.zeros_like(mark_ref)
    x_own = x_ref[...]
    extra, spread = ex_ref[...], cve_ref[...]
    g_query = dg(extra, x_own, 1, 0)
    q_bias = jnp.sum(extra.astype(f32), axis=1, keepdims=True)
    g_conv = dg(spread, xe_ref[...], 1, 0)
    c_bias = jnp.sum(spread.astype(f32), axis=1, keepdims=True)
    pre = pre_ref[...]
    g_point = dg(pre, depth_ref[...], 1, 0)
    p_bias = jnp.sum(pre.astype(f32), axis=1, keepdims=True)
    low, zed, gm = low_ref[...], zed_ref[...], gm_ref[...]
    lane = lax.broadcasted_iota(jnp.int32, (48, 128), 1)
    ones = jnp.ones((8, quarter), bf16)
    for s, out in enumerate(outs):
        own = slice(48 * s, 48 * s + 48)
        out[GP : GP + 48, :] = g_point[own].astype(bf16)
        out[GC : GC + 48, :] = g_conv[own].astype(bf16)
        out[GQ : GQ + 48, :] = g_query[own].astype(bf16)
        out[GO : GO + 96, :] = dg(a_ref[96 * s : 96 * s + 96, :], gm, 1, 0).astype(bf16)
        inner, outer, bias = [], [], []
        for g in range(2):
            lanes = slice(192 * g, 192 * g + 192)
            gpre = gpre_ref[2 * s + g]
            inner.append(dg(low[:, lanes], gpre, 0, 0))
            outer.append(dg(act_ref[2 * s + g], zed[:, lanes], 0, 0))
            bias.append(dg(ones, gpre, 1, 0)[0:1])
        out[GI : GI + 192, :] = jnp.concatenate(inner, axis=1).astype(bf16)
        out[GU : GU + 192, :] = jnp.concatenate(outer, axis=1).astype(bf16)
        tile = jnp.concatenate([gk_ref[s], jnp.zeros((48, 80), f32)], axis=1)
        tile = jnp.where(lane == 64, p_bias[own], tile)
        tile = jnp.where(lane == 65, c_bias[own], tile)
        tile = jnp.where(lane == 66, kb_ref[...], tile)
        tile = jnp.where(lane == 67, q_bias[own], tile)
        out[GM : GM + 48, 0:128] = tile.astype(bf16)
        out[GM : GM + 48, 128:384] = jnp.zeros((48, 256), bf16)
        bias = jnp.concatenate(bias, axis=1)
        lines = jnp.concatenate([bias, dpt_ref[0:taps, :], vec_ref[0:6, :]], axis=0)
        out[GV : GV + 16, :] = lines.astype(bf16)
        if out.shape[0] > GRAD_ROWS:
            out[GRAD_ROWS:, :] = jnp.zeros((out.shape[0] - GRAD_ROWS, 384), bf16)


def add_body(a_ref, b_ref, out_ref):
    out_ref[...] = (a_ref[...].astype(f32) + b_ref[...].astype(f32)).astype(out_ref.dtype)


def fold_body(place_ref, a_ref, b_ref, c_ref, keep_ref, give_ref):
    x = place_ref[3]
    half = keep_ref.shape[0]
    for out, part in ((keep_ref, x), (give_ref, 1 - x)):
        rows = pl.ds(pl.multiple_of(part * half, 16), half)
        first = (a_ref[rows, :].astype(f32) + b_ref[rows, :].astype(f32)).astype(bf16).astype(f32)
        out[...] = (first + c_ref[rows, :].astype(f32)).astype(bf16)


def edge_body(place_ref, tok_ref, edge_ref, layer_ref, out_ref):
    mp = place_ref[0]
    rows = tok_ref.shape[0]
    out_ref[0:rows, :] = tok_ref[...]
    out_ref[rows:, :] = layer_ref[...]
    low, high = slice(16, 32), slice(rows - 32, rows - 16)

    @pl.when(mp == 0)
    def _():
        out_ref[low, :] = (tok_ref[low, :].astype(f32) + edge_ref[...]).astype(bf16)

    @pl.when(mp == 3)
    def _():
        out_ref[high, :] = (tok_ref[high, :].astype(f32) + edge_ref[...]).astype(bf16)


def unpack_body(
    place_ref, own_ref, other_ref,
    point_ref, conv_ref, query_ref, out_ref, inner_ref, outer_ref, kernel_ref, qb_ref, ib_ref,
    dep_ref, pb_ref, cb_ref, kb_ref, *refs, taps,
):
    *vec_refs, scr = refs
    x = place_ref[3]
    half = own_ref.shape[0]
    scr[pl.ds(pl.multiple_of(x * half, 16), half), :] = own_ref[...].astype(f32)
    scr[pl.ds(pl.multiple_of((1 - x) * half, 16), half), :] = other_ref[...].astype(f32)
    point_ref[...] = scr[GP : GP + 48, :]
    conv_ref[...] = scr[GC : GC + 48, :]
    query_ref[...] = scr[GQ : GQ + 48, :]
    out_ref[0] = scr[GO : GO + 48, :]
    out_ref[1] = scr[GO + 48 : GO + 96, :]
    for g in range(2):
        lanes = slice(192 * g, 192 * g + 192)
        inner_ref[g] = scr[GI : GI + 192, lanes]
        outer_ref[g] = scr[GU : GU + 192, lanes]
        ib_ref[g : g + 1, :] = scr[GV : GV + 1, lanes]
    kernel_ref[...] = scr[GM : GM + 36, 0:48]
    turned = jnp.transpose(scr[GM : GM + 48, 0:128], (1, 0))
    pb_ref[...] = turned[64]
    cb_ref[...] = turned[65]
    kb_ref[...] = turned[66, 0:36]
    qb_ref[...] = turned[64:72, :]
    dep_ref[...] = scr[GV + 1 : GV + 1 + taps, :]
    for n, ref in enumerate(vec_refs):
        ref[...] = scr[GV + 1 + taps + n, :]


def head_weights_body(g_ref, x_ref, out_ref):
    grads = g_ref[...]
    out_ref[0:144, :] = dg(grads, x_ref[...], 1, 0).astype(bf16)
    out_ref[144:160, :] = jnp.zeros((16, 384), bf16)
    sums = dg(jnp.ones((16, grads.shape[1]), bf16), grads, 1, 1)
    out_ref[144:160, 0:144] = sums.astype(bf16)


def head_unpack_body(
    total_ref, other_ref, part_ref, bias_ref, q_ref, k_ref, v_ref, qb_ref, vb_ref
):
    total = total_ref[...].astype(f32) + other_ref[...].astype(f32)
    q_ref[...] = total[0:48] + part_ref[...]
    k_ref[...] = total[48:96]
    v_ref[...] = total[96:144]
    qb_ref[...] = total[144, 0:48] + bias_ref[3, :]
    vb_ref[...] = total[144, 96:144]


def tokens_body(place_ref, t0, t1, t2, t3, layer_ref, out_ref, acc, *, quarter):
    mp = place_ref[0]
    parts = (t0, t1, t2, t3)
    for s, ref in enumerate(parts):
        at = pl.multiple_of((mp ^ s) * quarter, quarter)
        layer_ref[pl.ds(at, quarter), :] = ref[quarter + 32 :, :]
        acc[pl.ds(at + 16, quarter), :] = ref[16 : quarter + 16, :].astype(f32)
    for s, ref in enumerate(parts):
        at = pl.multiple_of((mp ^ s) * quarter, quarter)
        acc[pl.ds(at, 16), :] += ref[0:16, :].astype(f32)
        acc[pl.ds(at + quarter + 16, 16), :] += ref[quarter + 16 : quarter + 32, :].astype(f32)
    out_ref[...] = acc[16 : 4 * quarter + 16, :]


def input_grad_body(
    g0, g1, g2, g3, p0, p1, p2, p3, tok_ref, out_ref, rows, done, scr, sems, *, quarter
):
    packs = Rows((p0, p1, p2, p3), scr, sems, HEAD_ROWS)
    grads = jnp.concatenate([ref[...] for ref in (g0, g1, g2, g3)], axis=0)
    packs.wait(0)
    weights = packs.all(WQ, WQ + 144)
    copies = []
    for n in range(4):
        span = slice(n * quarter, n * quarter + quarter)
        rows[span, :] = dg(grads[:, span], weights, 0, 0) + tok_ref[span, :]
        at = pl.ds(n * quarter, quarter)
        copies.append(pltpu.make_async_copy(rows.at[at], out_ref.at[at], done.at[n]))
        copies[n].start()
    for copy in copies:
        copy.wait()


def local(
    inputs, w_query, b_query, w_key, w_value, b_value, depth_kernel, w_point, b_point, w_kernel,
    b_kernel, w_conv, b_conv, w_out, b_out, gain_one, shift_one, w_inner, b_inner, w_outer,
    b_outer, gain_two, shift_two, cotangent,
):
    CALLS.clear()
    blocks = lax.axis_size("ctx")
    outer = blocks // 2
    rows_here = inputs.shape[0]
    quarter = rows_here // 4
    taps = depth_kernel.shape[0]
    rim = 64
    ctx, mp = lax.axis_index("ctx"), lax.axis_index("mp")
    x_at, z_at = ctx % 2, ctx // 2
    place = jnp.stack(
        [mp, ctx * rows_here + mp * quarter, blocks * rows_here, x_at, z_at]
    ).astype(jnp.int32)

    def table(change):
        pairs = []
        for z in range(outer):
            for x in range(2):
                for y in range(2):
                    for c in range(2):
                        z2, x2, y2, c2 = change(z, x, y, c)
                        pairs.append(((2 * z + x) * 4 + 2 * y + c, (2 * z2 + x2) * 4 + 2 * y2 + c2))
        return pairs

    def send(value, change):
        return lax.ppermute(value, ("ctx", "mp"), table(change))

    def across_c(z, x, y, c):
        return (z, x, y, c ^ 1)

    def across_y(z, x, y, c):
        return (z, x, y ^ 1, c)

    def across_x(z, x, y, c):
        return (z, x ^ 1, y, c)

    def across_z(i):
        return lambda z, x, y, c: (z ^ i, x, y, c)

    def line(vector):
        return vector.reshape(1, -1)

    def plus(left, right, hbm=(), final=()):
        return call(add_body, [(left.shape, bf16)], [left, right], us=1, hbm=hbm, final=final)[0]

    tick = lax.optimization_barrier
    bits = [1 << n for n in range(outer.bit_length() - 1)]
    rest = [i for i in range(1, outer) if i not in bits]

    kv, q = call(
        project_body,
        [((96, rows_here), bf16), ((48, rows_here), bf16)],
        [inputs, w_query.T, line(b_query), w_key.T, w_value.T, line(b_value)], us=2.4,
        hbm=range(6),
    )
    zkv, skv = [kv] + [None] * (outer - 1), [send(kv, across_x)] + [None] * (outer - 1)
    for i in bits:
        zkv[i] = send(kv, across_z(i))
    pack, lines = call(
        pack_body,
        [((PACK_ROWS, 384), bf16), ((8, 384), f32)],
        [w_query.T, w_key.T, w_value.T, w_point.T, w_conv.T, w_out, w_inner, w_outer, w_kernel.T,
         line(b_query), line(b_point), line(b_conv), b_inner, b_out, gain_one, shift_one, b_outer,
         gain_two, shift_two],
        us=2.2, after=(q,), hbm=range(19), final=(0,),
    )
    rims = jnp.where(mp == 0, inputs[rows_here - rim :], inputs[:rim])
    x_quarter = lax.dynamic_slice_in_dim(inputs, mp * quarter, quarter, 0)
    cot_quarter = lax.dynamic_slice_in_dim(cotangent, mp * quarter, quarter, 0)
    state = flash(q, [kv], None)
    pack, rims, x_quarter, cot_quarter, place, lines, state, skv[0], *got = tick(
        (pack, rims, x_quarter, cot_quarter, place, lines, state, skv[0], *(zkv[i] for i in bits))
    )
    for i, item in zip(bits, got, strict=True):
        zkv[i] = item
        skv[i] = send(item, across_x)
    for i in rest:
        zkv[i] = send(zkv[i & (i - 1)], across_z(i & -i))
    pack_beyond = send(pack, across_y)
    pairs = []
    for i in range(blocks - 1):
        pairs += [(4 * i, 4 * i + 4), (4 * i + 7, 4 * i + 3)]
    beside = lax.ppermute(rims, ("ctx", "mp"), pairs)
    todo = [skv[0], *(zkv[i] for i in bits)]
    for n in range(0, len(todo), 2):
        state = flash(q, todo[n : n + 2], state)
    state, beside, skv[bits[0]], *got = tick(
        (state, beside, skv[bits[0]], *(zkv[i] for i in rest))
    )
    for i, item in zip(rest, got, strict=True):
        zkv[i] = item
        skv[i] = send(item, across_x)
    todo = [skv[bits[0]], *got]
    for n in range(0, len(todo), 2):
        state = flash(q, todo[n : n + 2], state)
    state, pack_beyond, *got = tick((state, pack_beyond, *(skv[i] for i in bits[1:])))
    packs = [pack, send(pack, across_c), pack_beyond, send(pack_beyond, across_c)]
    for i, item in zip(bits[1:], got, strict=True):
        skv[i] = item
    todo = got + [skv[i] for i in rest]
    for n in range(0, len(todo) - 2, 2):
        state = flash(q, todo[n : n + 2], state)
    raw, lse, context, context_c, context_y = flash(q, todo[-2:], state, place)

    context, context_c, context_y, packs = tick((context, context_c, context_y, packs))
    heads_y = send(context_y, across_y)
    heads_c = send(context_c, across_c)
    extended = jnp.concatenate([beside, inputs, beside], axis=0)
    x_ext = lax.dynamic_slice_in_dim(extended, mp * quarter, quarter + 2 * rim, 0)
    ext = quarter + 2 * rim
    mix, depth, q_conv, key_conv, tap_probs, conv_vals = call(
        functools.partial(conv_body, rim=rim, quarter=quarter, taps=taps),
        [((192, quarter), bf16), ((quarter, 384), bf16), ((192, quarter), bf16),
         ((192, quarter), f32), ((8 * taps, quarter), f32), ((192, ext), f32)],
        [place, x_ext, depth_kernel, line(b_kernel), *packs],
        us=4.4, smem=(0,), final=range(1, 6), raw=range(4, 8), hbm=(3,),
        scratch=row_scratch(CONV_ROWS),
    )
    heads_y, heads_c, mix = tick((heads_y, heads_c, mix))
    heads = [context, heads_c, heads_y, send(heads_y, across_c)]
    (layer_quarter, c0, c1, c23, grad_mix, both, act, gpre, low, zed, gm, grad_h1, vec) = call(
        feed_body,
        [((quarter, 384), bf16)] + [((48 * n, quarter), bf16) for n in (1, 1, 2)]
        + [((192, quarter), f32), ((384, quarter), bf16), ((8, quarter, 192), bf16),
           ((8, quarter, 192), bf16), ((quarter, 384), bf16), ((quarter, 384), bf16),
           ((quarter, 384), bf16), ((quarter, 384), f32), ((8, 384), f32)],
        [place, *heads, mix, *packs, x_quarter, cot_quarter, lines],
        us=6.8, smem=(0,), raw=range(6, 10),
        scratch=[pltpu.VMEM((8, quarter, 192), f32), *row_scratch(FEED_ROWS)],
    )
    grads_y = send(c23, across_y)
    grads_c = send(c1, across_c)
    extra, grad_kc, g_kernel, k_bias, g_depth, spread, token_part, edge = call(
        functools.partial(conv_back_body, rim=rim, quarter=quarter, taps=taps),
        [((192, quarter), bf16), ((192, quarter), bf16), ((4, 48, 48), f32), ((48, 128), f32),
         ((16, 384), f32), ((192, ext), bf16), ((quarter + 32, 384), bf16), ((16, 384), f32)],
        [place, x_ext, depth_kernel, *packs, q_conv, key_conv, tap_probs, conv_vals, grad_mix,
         grad_h1],
        us=5.4, smem=(0,), raw=range(3, 7), scratch=row_scratch(BACK_ROWS),
    )
    grads_y, grads_c, extra = tick((grads_y, grads_c, extra))
    grads = [c0, grads_c, grads_y, send(grads_y, across_c)]
    all_rows = -(-GRAD_ROWS // 32) * 32
    *sums, mark = call(
        functools.partial(weights_body, quarter=quarter, taps=taps),
        [((all_rows, 384), bf16)] * 4 + [((8, 128), f32)],
        [x_quarter, x_ext, both, act, gpre, low, zed, gm, vec, grad_kc, depth, g_kernel,
         k_bias, g_depth, spread, extra],
        us=4.6, final=range(4),
    )
    grads, mark = tick((grads, mark))
    q_aug, grad_aug = call(
        back_prepare_body,
        [((112, rows_here), bf16), ((64, rows_here), bf16)],
        [place, q, lse, raw, *grads], us=1.8, smem=(0,),
    )

    order = sorted(range(outer), key=lambda i: (-i.bit_count(), -i))
    edge_pairs = []
    for i in range(blocks - 1):
        edge_pairs += [(4 * i + 4, 4 * i + 3), (4 * i + 3, 4 * i + 4)]
    found = {i: [] for i in range(outer)}
    cross_found = {}

    def cross(pair, dq, after=()):
        dq, (parts,) = back(q, q_aug, grad_aug, [skv[i] for i in pair], dq, after=after)
        return dq, parts

    def spread_out(pair, parts):
        other = send(parts, across_x)
        for n, i in enumerate(pair):
            cross_found[i] = (other, n)

    def own(group, dq, after=()):
        sums = []
        for i in group:
            other, place = cross_found[i]
            sums.append(([other, *found[i]] if i else [other], place))
        dtypes = [bf16 if i else f32 for i in group]
        dq, parts = back(
            q, q_aug, grad_aug, [zkv[i] for i in group], dq, sums, dtypes, after
        )
        dq, parts = tick((dq, parts))
        for i, part in zip(group, parts, strict=True):
            if i:
                found[i & (i - 1)].append(send(part, across_z(i & -i)))
                found[i] = []
        return dq, parts[-1]

    givens = [send(sums[3], across_c), send(sums[1], across_c)]
    edge = lax.ppermute(edge, ("ctx", "mp"), edge_pairs)
    piece = plus(sums[2], givens[0], hbm=(0,), final=(0,))
    beyond = send(piece, across_y)
    piece, grad_aug = tick((piece, grad_aug))
    dq, parts = cross(order[:1], None)
    dq, parts, edge, layer_quarter = tick((dq, parts, edge, layer_quarter))
    spread_out(order[:1], parts)
    dq, parts = cross(order[1:2], dq)
    dq, parts, given = tick((dq, parts, givens[1]))
    spread_out(order[1:2], parts)
    for n in range(2, outer, 2):
        dq, parts = cross(order[n : n + 2], dq)
        other, at = cross_found[order[n - 2]]
        dq, parts, other = tick((dq, parts, other))
        cross_found[order[n - 2]] = (other, at)
        spread_out(order[n : n + 2], parts)
        dq, _ = own(order[n - 2 : n - 1], dq)
        other, at = cross_found[order[n - 1]]
        dq, other = tick((dq, other))
        cross_found[order[n - 1]] = (other, at)
        if n == outer - 2:
            both_parts = call(
                edge_body, [((2 * quarter + 32, 384), bf16)],
                [place, token_part, edge, layer_quarter], us=1, smem=(0,), final=(0,),
            )[0]
            beyond, dq, found = tick((beyond, dq, found))
            mine, give = call(
                fold_body, [((all_rows // 2, 384), bf16)] * 2, [place, sums[0], given, beyond],
                us=1, smem=(0,), hbm=(1,),
            )
            given = send(give, across_x)
        dq, _ = own(order[n - 1 : n], dq)
    other, _ = cross_found[0]
    dq, other = tick((dq, other, mine))[:2]
    cross_found.update({i: (other, n) for n, i in enumerate(order[-2:])})
    dq, last_part = own(order[-2:], dq, (mine, give))
    given, both_parts, dq = tick((given, both_parts, dq))
    piece = plus(mine, given)
    given = send(piece, across_z(bits[-1]))
    parts_beyond = send(both_parts, across_y)
    parts_beside = send(both_parts, across_c)
    *early, late = found[0]
    early, dq, _ = tick((early, dq, piece))
    last_part = call(
        gather_body, [((96, rows_here), f32)], [last_part, *early], us=JOIN_PACE,
    )[0]
    late, last_part = tick((late, last_part))

    head_grads = call(
        back_join_body, [((144, rows_here), bf16)], [dq, last_part, late], us=2.1,
    )[0]
    head_w = call(
        head_weights_body, [((160, 384), bf16)], [head_grads, inputs], us=2.2,
    )[0]
    head_other = send(head_w, across_x)
    grads_beyond = send(head_grads, across_y)
    grads_beside = send(head_grads, across_c)
    given, parts_beyond, head_w = tick((given, parts_beyond, head_w))
    parts_other = send(parts_beyond, across_c)
    if len(bits) > 1:
        piece = plus(piece, given)
        given = send(piece, across_z(bits[-2]))
    parts_other = tick((parts_other, piece))[0]
    both = [both_parts, parts_beside, parts_beyond, parts_other]
    layer_out, tokens = call(
        functools.partial(tokens_body, quarter=quarter),
        [((rows_here, 384), bf16), ((rows_here, 384), f32)],
        [place, *both], us=2.3, smem=(0,), final=(0,), hbm=(1,), after=(head_w,),
        scratch=[pltpu.VMEM((rows_here + 32, 384), f32)],
    )
    head_other, _ = tick((head_other, layer_out))
    head_w = plus(head_w, head_other)
    head_other = send(head_w, across_z(bits[0]))
    grads_beyond, head_w = tick((grads_beyond, head_w))
    grads_other = send(grads_beyond, across_c)
    for n, bit in enumerate(bits[1:]):
        head_other = tick((head_other, grads_beyond))[0]
        head_w = plus(head_w, head_other)
        head_other = send(head_w, across_z(bit))
        given = tick((given, head_w))[0]
        piece = plus(piece, given)
        given = send(piece, across_z(bits[-3 - n]) if n + 2 < len(bits) else across_x)
    grads_other, _ = tick((grads_other, piece))
    inputs_grad = call(
        functools.partial(input_grad_body, quarter=quarter),
        [((rows_here, 384), f32)],
        [head_grads, grads_beside, grads_beyond, grads_other, *packs, tokens], us=3.0,
        raw=range(4, 8), final=(0,), raw_out=(0,),
        scratch=[
            pltpu.VMEM((rows_here, 384), f32), pltpu.SemaphoreType.DMA((4,)),
            *row_scratch(HEAD_ROWS),
        ],
    )[0]
    other_piece, _ = tick((given, inputs_grad))
    (point, conv, query_part, grad_out, grad_inner, grad_outer, kernel, biases, i_bias, grad_depth,
     p_bias, c_bias, k_bias, *vecs) = call(
        functools.partial(unpack_body, taps=taps),
        [((48, 384), f32)] * 3 + [((2, 48, 384), f32), ((2, 192, 192), f32),
         ((2, 192, 192), f32), ((36, 48), f32), ((8, 48), f32), ((2, 192), f32), ((taps, 384), f32),
         ((48,), f32), ((48,), f32), ((36,), f32)] + [((384,), f32)] * 6,
        [place, piece, other_piece], us=2.3, smem=(0,), final=(0, 1, 3, 4, 5, 6, *range(8, 19)),
        scratch=[pltpu.VMEM((all_rows, 384), f32)],
    )
    query, key, value, q_bias, v_bias = call(
        head_unpack_body,
        [((48, 384), f32)] * 3 + [((48,), f32)] * 2,
        [head_w, head_other, query_part, biases], us=1.7, final=range(5),
    )

    return (
        layer_out, inputs_grad, query.T, q_bias, key.T, value.T, v_bias, grad_depth, point.T,
        p_bias, kernel.T, k_bias, conv.T, c_bias, grad_out, vecs[0], vecs[1], vecs[2], grad_inner,
        i_bias, grad_outer, vecs[3], vecs[4], vecs[5],
    )


def solution(mesh):
    return jax.shard_map(
        local,
        mesh=mesh,
        in_specs=(
            P("ctx", None), P(None, "mp"), P("mp"), P(None, "mp"), P(None, "mp"), P("mp"), P(),
            P(None, "mp"), P("mp"), P("mp", None), P(), P(None, "mp"), P("mp"),
            P(None, "mp", None), P(), P(), P(), P(None, None, "mp"), P(None, "mp"),
            P(None, "mp", None), P(), P(), P(), P("ctx", None),
        ),
        out_specs=(
            P("ctx", None), P("ctx", None), P(None, "mp"), P("mp"), P(None, "mp"), P(None, "mp"),
            P("mp"), P(), P(None, "mp"), P("mp"), P("mp", None), P(), P(None, "mp"), P("mp"),
            P(None, "mp", None), P(), P(), P(), P(None, None, "mp"), P(None, "mp"),
            P(None, "mp", None), P(), P(), P(),
        ),
        check_vma=False,
    )
```

```python
import functools
import math

import jax
import jax.numpy as jnp
from jax import lax
from jax.experimental import pallas as pl
from jax.experimental.pallas import tpu as pltpu
from jax.sharding import PartitionSpec as P


EPSILON = 1e-12
KERNEL_BYTES = 24 * 2**20
PACE = 1e5
JOIN_PACE = 4e4
HINTS = {2: 3e9, 3: 3e9, 11: 1e10, 17: 3e9, 19: 1e10, 35: 1e10, 42: 1e9}
CALLS = []
f32 = jnp.float32
bf16 = jnp.bfloat16

WQ, WK, WV, WP, WC, WO, WI, WU, WM, WB = 0, 48, 96, 144, 192, 240, 336, 528, 720, 768
PACK_ROWS = 784
GP, GC, GQ, GO, GI, GU, GM, GV = 0, 48, 96, 144, 240, 432, 624, 672
GRAD_ROWS = 688


def dg(left, right, ld, rd):
    return lax.dot_general(
        left, right, (((ld,), (rd,)), ((), ())), preferred_element_type=f32
    )


def row(ref):
    return ref[...].astype(f32).reshape(1, -1)


class Rows:
    def __init__(self, refs, scr, sems, ranges):
        self.scr, self.copies, at = scr, [], 0
        for n, (low, high) in enumerate(ranges):
            span = pl.ds(at, high - low)
            copies = [
                pltpu.make_async_copy(ref.at[pl.ds(low, high - low)], scr.at[s, span], sems.at[s, n])
                for s, ref in enumerate(refs)
            ]
            self.copies.append((low, high, at, copies))
            at += high - low
        for *_, copies in self.copies:
            for copy in copies:
                copy.start()

    def wait(self, n):
        for copy in self.copies[n][3]:
            copy.wait()

    def get(self, s, low, high, lanes=slice(None)):
        for first, last, at, _ in self.copies:
            if first <= low and high <= last:
                return self.scr[s, at + low - first : at + high - first, lanes]
        raise ValueError("rows")

    def all(self, low, high):
        return jnp.concatenate([self.get(s, low, high) for s in range(4)], axis=0)


def row_scratch(ranges):
    rows = sum(high - low for low, high in ranges)
    return [pltpu.VMEM((4, rows, 384), bf16), pltpu.SemaphoreType.DMA((4, len(ranges)))]


CONV_ROWS = ((0, 48), (144, 240), (720, 784))
BACK_ROWS = ((720, 784), (144, 240), (0, 48))
FEED_ROWS = ((240, 336), (336, 784))
HEAD_ROWS = ((0, 144),)


def outer_ones(row, width):
    return dg(row, jnp.ones((row.shape[0], width), bf16), 0, 0)


def call(body, outs, args, us, scratch=(), smem=(), after=(), final=(), hbm=(), raw=(), raw_out=()):
    inputs = len(args)
    flops = HINTS.get(len(CALLS), us * PACE)
    CALLS.append(us)

    def whole(*refs):
        body(*refs[:inputs], *refs[inputs + len(after) :])

    specs = [
        pl.BlockSpec(
            memory_space=pltpu.SMEM if i in smem else pltpu.HBM if i in raw else pltpu.VMEM
        )
        for i in range(inputs)
    ]
    return pl.pallas_call(
        whole,
        in_specs=specs + [pl.BlockSpec(memory_space=pl.ANY)] * len(after),
        out_specs=[
            pl.BlockSpec(memory_space=pltpu.HBM if i in raw_out else pltpu.VMEM)
            for i in range(len(outs))
        ],
        out_shape=[
            pltpu.HBM(s, d) if i in final else pltpu.VMEM(s, d)
            for i, (s, d) in enumerate(outs)
        ],
        scratch_shapes=list(scratch),
        compiler_params=pltpu.CompilerParams(vmem_limit_bytes=KERNEL_BYTES),
        cost_estimate=pl.CostEstimate(flops=int(flops), bytes_accessed=0, transcendentals=0),
    )(
        *(
            arg
            if i in smem
            else pltpu.with_memory_space_constraint(arg, pltpu.HBM if i in hbm or i in raw else pltpu.VMEM)
            for i, arg in enumerate(args)
        ),
        *after,
    )


def project_body(x_ref, wq_ref, bq_ref, wk_ref, wv_ref, bv_ref, kv_ref, q_ref):
    x = x_ref[...]
    width = x.shape[0]
    weights = jnp.concatenate([wk_ref[...], wv_ref[...], wq_ref[...]], axis=0)
    found = dg(weights, x, 1, 1)
    kv_ref[0:48, :] = found[0:48].astype(bf16)
    kv_ref[48:96, :] = (found[48:96] + outer_ones(bv_ref[...], width)).astype(bf16)
    q_ref[...] = (found[96:144] + outer_ones(bq_ref[...], width)).astype(bf16)


def pack_body(
    wq_ref, wk_ref, wv_ref, wp_ref, wc_ref, wo_ref, wi_ref, wu_ref, wm_ref,
    bq_ref, bp_ref, bc_ref, bi_ref, bo_ref, g1_ref, s1_ref, bu_ref, g2_ref, s2_ref,
    out_ref, lines_ref,
):
    vectors = [row(ref) for ref in (bo_ref, g1_ref, s1_ref, bu_ref, g2_ref, s2_ref)]
    lines_ref[...] = jnp.concatenate([*vectors, jnp.zeros((2, 384), f32)], axis=0)
    for at, ref in ((WQ, wq_ref), (WK, wk_ref), (WV, wv_ref), (WP, wp_ref), (WC, wc_ref)):
        out_ref[at : at + 48, :] = ref[...]
    out_ref[WO : WO + 48, :] = wo_ref[0]
    out_ref[WO + 48 : WO + 96, :] = wo_ref[1]
    out_ref[WI : WI + 192, :] = jnp.concatenate([wi_ref[0], wi_ref[1]], axis=1)
    out_ref[WU : WU + 192, :] = jnp.concatenate([wu_ref[0], wu_ref[1]], axis=1)
    out_ref[WM : WM + 64, :] = jnp.zeros((64, 384), bf16)
    out_ref[WM : WM + 36, 0:48] = wm_ref[...]
    zeros = jnp.zeros((1, 336), f32)
    lines = [jnp.concatenate([bi_ref[0:1].astype(f32), bi_ref[1:2].astype(f32)], axis=1)]
    for ref in (bq_ref, bp_ref, bc_ref):
        lines.append(jnp.concatenate([ref[...].astype(f32), zeros], axis=1))
    lines.append(jnp.zeros((12, 384), f32))
    out_ref[WB : WB + 16, :] = jnp.concatenate(lines, axis=0).astype(bf16)


def keys_aug(kv):
    keys = kv[0:48]
    return jnp.concatenate([keys, keys, jnp.ones((16, keys.shape[1]), bf16)], axis=0)


def vals_aug(kv):
    vals = kv[48:96]
    return jnp.concatenate([vals, jnp.ones((16, vals.shape[1]), bf16)], axis=0)


def split3(value):
    high = value.astype(bf16)
    rest = value - high.astype(f32)
    mid = rest.astype(bf16)
    low = (rest - mid.astype(f32)).astype(bf16)
    return high, mid, low


def scaled_queries(q):
    scaled = q.astype(f32) * (math.log2(math.e) / math.sqrt(48.0))
    high = scaled.astype(bf16)
    low = (scaled - high.astype(f32)).astype(bf16)
    return high, low


def flash_body(*refs, first, last, blocks):
    refs = list(refs)
    q_ref = refs.pop(0)
    tp_ref = refs.pop(0) if last else None
    kv_refs = [refs.pop(0) for _ in range(blocks)]
    if first:
        m_out, acc_out = refs
        m_now = acc_now = None
    else:
        m_in, acc_in = refs.pop(0), refs.pop(0)
        m_now, acc_now = m_in[0:1, :], acc_in[...]
    q = q_ref[...]
    width = q.shape[1]
    high, low = scaled_queries(q)
    q_aug = jnp.concatenate([high, low, jnp.zeros((16, width), bf16)], axis=0)
    for kv_ref in kv_refs:
        kv = kv_ref[...]
        scores = dg(keys_aug(kv), q_aug, 0, 0)
        top = jnp.max(scores, axis=0, keepdims=True)
        m_new = top if m_now is None else jnp.maximum(m_now, top)
        probs = jnp.exp2(scores - m_new).astype(bf16)
        part = dg(vals_aug(kv), probs, 1, 0)
        acc_now = part if m_now is None else acc_now * jnp.exp2(m_now - m_new) + part
        m_now = m_new
    if not last:
        if not first:
            m_out, acc_out = refs
        m_out[...] = jnp.broadcast_to(m_now, (8, width))
        acc_out[...] = acc_now
        return
    raw_ref, lse_ref, own_ref, beside_ref, beyond_ref, low_scr = refs
    total = acc_now[48:49, :]
    raw = acc_now[0:48, :] / total
    raw_ref[...] = raw
    lse_ref[...] = jnp.broadcast_to(m_now + jnp.log2(total), (8, width))
    low_scr[...] = raw.astype(bf16)
    quarter = width // 4
    mp = tp_ref[0]
    for at, ref in ((mp, own_ref), (mp ^ 1, beside_ref)):
        ref[...] = low_scr[:, pl.ds(pl.multiple_of(at * quarter, quarter), quarter)]
    half = 2 * quarter
    beyond_ref[...] = low_scr[:, pl.ds(pl.multiple_of((1 - (mp >> 1)) * half, half), half)]


def flash(q, kvs, state, place=None, after=()):
    width = q.shape[1]
    first, last = state is None, place is not None
    args = [q] + ([place] if last else []) + list(kvs) + ([] if first else list(state))
    if last:
        outs = [((48, width), f32), ((8, width), f32)] + [
            ((48, width // n), bf16) for n in (4, 4, 2)
        ]
        scratch = [pltpu.VMEM((48, width), bf16)]
    else:
        outs, scratch = [((8, width), f32), ((64, width), f32)], []
    return call(
        functools.partial(flash_body, first=first, last=last, blocks=len(kvs)),
        outs, args, us=2.4 * len(kvs), scratch=scratch, smem=(1,) if last else (), after=after,
    )


def back_prepare_body(place_ref, q_ref, lse_ref, raw_ref, g0, g1, g2, g3, qa_ref, da_ref):
    q = q_ref[...]
    width = q.shape[1]
    quarter = width // 4
    high, low = scaled_queries(q)
    lines = split3(-lse_ref[0:1, :])
    pad = jnp.zeros((13, width), bf16)
    qa_ref[...] = jnp.concatenate([high, low, *lines, pad], axis=0)
    place = place_ref[0]
    for s, ref in enumerate((g0, g1, g2.at[0:48], g3.at[48:96])):
        at = pl.multiple_of((place ^ s) * quarter, quarter)
        da_ref[0:48, pl.ds(at, quarter)] = ref[...]
    grad = da_ref[0:48, :]
    delta = jnp.sum(grad.astype(f32) * raw_ref[...], axis=0, keepdims=True)
    da_ref[48:64, :] = jnp.concatenate([*split3(-delta), pad], axis=0)


def back_body(*refs, first, blocks, plus):
    refs = list(refs)
    q_ref, qa_ref, da_ref = refs[:3]
    kv_refs = refs[3 : 3 + blocks]
    refs = refs[3 + blocks :]
    dq_in = None if first else refs.pop(0)
    plus_refs = []
    for count, place in plus:
        group = [refs.pop(0) for _ in range(count)]
        plus_refs.append([group[0].at[place], *group[1:]])
    dq_out, *outs = refs
    if not plus:
        outs = [outs[0].at[n] for n in range(blocks)]
        plus_refs = [[]] * blocks
    q, grad = q_ref[...], da_ref[0:48, :]
    q_aug, grad_aug = qa_ref[...], da_ref[...]
    step = 256
    dq = None if first else dq_in[...]
    for kv_ref, out, group in zip(kv_refs, outs, plus_refs, strict=True):
        kv = kv_ref[...]
        keys, vals = keys_aug(kv), vals_aug(kv)
        for at in range(0, kv.shape[1], step):
            span = slice(at, at + step)
            probs = jnp.exp2(dg(keys[:, span], q_aug, 0, 0))
            grad_probs = dg(vals[:, span], grad_aug, 0, 0)
            grad_scores = (probs * grad_probs).astype(bf16)
            dv = dg(grad, probs.astype(bf16), 1, 1)
            dk = dg(q, grad_scores, 1, 1)
            part = dg(kv[0:48, span], grad_scores, 1, 0)
            dq = part if dq is None else dq + part
            both = jnp.concatenate([dk, dv], axis=0)
            for ref in group:
                both = both + ref[:, span].astype(f32)
            out[:, span] = both.astype(out.dtype)
    dq_out[...] = dq


def back(q, q_aug, grad_aug, kvs, dq, plus=(), dtypes=(), after=()):
    width = q.shape[1]
    shape = kvs[0].shape
    args = [q, q_aug, grad_aug, *kvs] + ([] if dq is None else [dq])
    args += [array for arrays, _ in plus for array in arrays]
    outs = [(shape, dtype) for dtype in dtypes] if plus else [((len(kvs), *shape), bf16)]
    dq, *parts = call(
        functools.partial(
            back_body, first=dq is None, blocks=len(kvs),
            plus=[(len(arrays), place) for arrays, place in plus],
        ),
        [((48, width), f32), *outs], args, us=3.5 * len(kvs), after=after,
    )
    return dq, parts


def gather_body(*refs):
    *parts, out_ref = refs
    total = parts[0][...]
    for ref in parts[1:]:
        total = total + ref[...].astype(f32)
    out_ref[...] = total


def back_join_body(dq_ref, dkv_ref, *refs):
    *news, out_ref = refs
    scale = 1.0 / math.sqrt(48.0)
    out_ref[0:48, :] = (dq_ref[...] * scale).astype(bf16)
    total = dkv_ref[...]
    for ref in news:
        total = total + ref[...].astype(f32)
    out_ref[48:96, :] = (total[0:48] * scale).astype(bf16)
    out_ref[96:144, :] = total[48:96].astype(bf16)


def tap_places(mp, heads, taps):
    rows = lax.broadcasted_iota(jnp.int32, (48, 8 * taps), 0)
    cols = lax.broadcasted_iota(jnp.int32, (48, 8 * taps), 1)
    s = cols & 7
    wanted = (s ^ mp) * taps + (cols >> 3)
    return ((rows == wanted) & (s < heads)).astype(f32).astype(bf16)


def lift(value, axis, shift, keep):
    size = value.shape[axis]
    rolled = pltpu.roll(value, (size - shift) % size, axis)
    return rolled[:keep] if axis == 0 else rolled[:, :keep]


def conv_body(
    place_ref, xe_ref, dk_ref, bk_ref, p0, p1, p2, p3,
    mix_ref, depth_ref, q_ref, kc_ref, tp_ref, cv_ref, scr, sems, *, rim, quarter, taps,
):
    packs = Rows((p0, p1, p2, p3), scr, sems, CONV_ROWS)
    xe = xe_ref[...]
    x_own = xe[rim : rim + quarter]
    wide = xe.astype(f32)
    reach = taps // 2
    kernel = dk_ref[...].astype(f32)
    depth = None
    for j in range(taps):
        term = lift(wide, 0, rim - reach + j, quarter) * kernel[j : j + 1, :]
        depth = term if depth is None else depth + term
    depth_low = depth.astype(bf16)
    depth_ref[...] = depth_low
    position = place_ref[1] + lax.broadcasted_iota(jnp.int32, (1, xe.shape[0]), 1) - rim
    inside = (position >= 0) & (position < place_ref[2])
    for n in range(3):
        packs.wait(n)
    attn = []
    for s in range(4):
        own = slice(48 * s, 48 * s + 48)
        bias = packs.get(s, WB, WB + 16, slice(0, 48))
        q = (
            dg(packs.get(s, WQ, WQ + 48), x_own, 1, 1) + outer_ones(bias[1:2], quarter)
        ).astype(bf16)
        kc = dg(packs.get(s, WP, WP + 48), depth_low, 1, 1) + outer_ones(bias[2:3], quarter)
        cv = dg(packs.get(s, WC, WC + 48), xe, 1, 1) + outer_ones(bias[3:4], xe.shape[0])
        q_ref[own, :] = q
        kc_ref[own, :] = kc
        cv_ref[own, :] = jnp.where(inside, cv, 0.0)
        attn.append((kc * q.astype(f32)).astype(bf16))
    attn = jnp.concatenate(attn, axis=0)
    hot = tap_places(place_ref[0], 4, taps)
    wk = [dg(packs.get(s, WM, WM + 48, slice(0, 48)), hot, 0, 0) for s in range(4)]
    wk = jnp.concatenate(wk, axis=0).astype(bf16)
    bias = dg(bk_ref[...], hot[0 : bk_ref.shape[1], :], 1, 0).astype(bf16)
    logits = dg(wk, attn, 0, 0) + outer_ones(bias, quarter)
    tiles = [logits[8 * j : 8 * j + 8] for j in range(taps)]
    top = functools.reduce(jnp.maximum, tiles)
    tiles = [jnp.exp(tile - top) for tile in tiles]
    total = functools.reduce(jnp.add, tiles)
    tiles = [tile / total for tile in tiles]
    for j in range(taps):
        tp_ref[8 * j : 8 * j + 8, :] = tiles[j]
    cv = cv_ref[...]
    mix = [None] * 4
    for j in range(taps):
        moved = lift(cv, 1, rim - reach + j, quarter)
        for s in range(4):
            term = tiles[j][s : s + 1, :] * moved[48 * s : 48 * s + 48]
            mix[s] = term if mix[s] is None else mix[s] + term
    for s in range(4):
        mix_ref[48 * s : 48 * s + 48, :] = mix[s].astype(bf16)


def conv_back_body(
    place_ref, xe_ref, dk_ref, p0, p1, p2, p3, q_ref, kc_ref, tp_ref, cv_ref, gm_ref, gh_ref,
    ex_ref, pre_ref, gk_ref, kb_ref, dpt_ref, cve_ref, tok_ref, edge_ref, scr, sems,
    *, rim, quarter, taps,
):
    packs = Rows((p0, p1, p2, p3), scr, sems, BACK_ROWS)
    reach = taps // 2
    ext = xe_ref.shape[0]
    grad_mix = gm_ref[...]
    cv = cv_ref[...]
    probs = [tp_ref[8 * j : 8 * j + 8, :] for j in range(taps)]
    grads = []
    weighted = None
    for j in range(taps):
        moved = lift(cv, 1, rim - reach + j, quarter) * grad_mix
        lines = [jnp.sum(moved[48 * s : 48 * s + 48], axis=0, keepdims=True) for s in range(4)]
        tile = jnp.concatenate(lines + [jnp.zeros((4, quarter), f32)], axis=0)
        grads.append(tile)
        term = probs[j] * tile
        weighted = term if weighted is None else weighted + term
    gtl = jnp.concatenate(
        [probs[j] * (grads[j] - weighted) for j in range(taps)], axis=0
    ).astype(bf16)
    hot = tap_places(place_ref[0], 4, taps)
    for n in range(3):
        packs.wait(n)
    wk = [dg(packs.get(s, WM, WM + 48, slice(0, 48)), hot, 0, 0) for s in range(4)]
    wk = jnp.concatenate(wk, axis=0).astype(bf16)
    q = q_ref[...].astype(f32)
    kc = kc_ref[...]
    attn = (kc * q).astype(bf16)
    plain = dg(hot, gtl, 1, 0).astype(bf16)
    for s in range(4):
        gk_ref[s] = dg(plain, attn[48 * s : 48 * s + 48], 1, 1)
    kb_ref[...] = dg(plain, jnp.ones((128, quarter), bf16), 1, 1)
    grad_attn = dg(wk, gtl, 1, 0)
    extra = (grad_attn * kc).astype(bf16)
    ex_ref[...] = extra
    grad_kc = (grad_attn * q).astype(bf16)
    pre_ref[...] = grad_kc
    wp = packs.all(WP, WP + 48)
    dvals = dg(grad_kc, wp, 0, 0)
    wide = xe_ref[...].astype(f32)
    kernel = dk_ref[...].astype(f32)
    tail = jnp.zeros((ext - quarter, dvals.shape[1]), f32)
    padded = jnp.concatenate([dvals, tail], axis=0)
    depth = None
    lines = []
    for j in range(taps):
        moved = lift(wide, 0, rim - reach + j, quarter)
        lines.append(jnp.sum(moved * dvals, axis=0, keepdims=True))
        term = pltpu.roll(padded, rim - reach + j, 0) * kernel[j : j + 1, :]
        depth = term if depth is None else depth + term
    lines.append(jnp.zeros((16 - taps, dvals.shape[1]), f32))
    dpt_ref[...] = jnp.concatenate(lines, axis=0)
    side = jnp.zeros((4 * 48, ext - quarter), f32)
    spread = None
    for j in range(taps):
        rows = [probs[j][s : s + 1, :] * grad_mix[48 * s : 48 * s + 48] for s in range(4)]
        full = jnp.concatenate([jnp.concatenate(rows, axis=0), side], axis=1)
        term = pltpu.roll(full, rim - reach + j, 1)
        spread = term if spread is None else spread + term
    position = place_ref[1] + lax.broadcasted_iota(jnp.int32, (1, ext), 1) - rim
    inside = (position >= 0) & (position < place_ref[2])
    spread = jnp.where(inside, spread, 0.0).astype(bf16)
    cve_ref[...] = spread
    wc = packs.all(WC, WC + 48)
    wq = packs.all(WQ, WQ + 48)
    tokens = depth + dg(spread, wc, 0, 0)
    own = dg(extra, wq, 0, 0) + gh_ref[...]
    end = rim + quarter
    tok_ref[0:16, :] = tokens[rim - 16 : rim].astype(bf16)
    tok_ref[16 : quarter + 16, :] = (tokens[rim:end] + own).astype(bf16)
    tok_ref[quarter + 16 :, :] = tokens[end : end + 16].astype(bf16)
    edge_ref[...] = jnp.where(place_ref[0] == 0, tokens[rim - 16 : rim], tokens[end : end + 16])


def norm(hidden):
    centred = hidden - jnp.mean(hidden, axis=-1, keepdims=True)
    inverse = lax.rsqrt(jnp.mean(centred * centred, axis=-1, keepdims=True) + EPSILON)
    return centred * inverse, inverse


def norm_back(grad, normed, inverse, gain):
    scaled = grad * gain
    return inverse * (
        scaled
        - jnp.mean(scaled, axis=-1, keepdims=True)
        - normed * jnp.mean(scaled * normed, axis=-1, keepdims=True)
    )


def feed_body(
    place_ref, r0, r1, r2, r3, mix_ref, p0, p1, p2, p3, x_ref, cot_ref, lines_ref,
    out_ref, c0, c1, c23, gmix_ref, a_ref, act_ref, gpre_ref, low_ref, zed_ref, gm_ref,
    gh_ref, vec_ref, slope_scr, scr, sems,
):
    packs = Rows((p0, p1, p2, p3), scr, sems, FEED_ROWS)
    both = []
    quarter = x_ref.shape[0]
    own = pl.ds(pl.multiple_of((place_ref[0] & 1) * quarter, quarter), quarter)
    for s, context in enumerate((r0[...], r1[...], r2[:, own], r3[:, own])):
        both += [context, mix_ref[48 * s : 48 * s + 48, :]]
    both = jnp.concatenate(both, axis=0)
    a_ref[...] = both
    packs.wait(0)
    w_out = packs.all(WO, WO + 96)
    mixed = dg(both, w_out, 0, 0) + lines_ref[0:1, :]
    normed1, inverse1 = norm(mixed + x_ref[...].astype(f32))
    gain1, gain2 = lines_ref[1:2, :], lines_ref[4:5, :]
    low = (normed1 * gain1 + lines_ref[2:3, :]).astype(bf16)
    low_ref[...] = low
    halves = [low[:, 0:192], low[:, 192:384]]
    packs.wait(1)
    outer = [None, None]
    for g in range(2):
        lanes = slice(192 * g, 192 * g + 192)
        for s in range(4):
            pre = dg(halves[g], packs.get(s, WI, WI + 192, lanes), 1, 0)
            pre = pre + packs.get(s, WB, WB + 16, lanes)[0:1].astype(f32)
            cdf = 0.5 * (1.0 + lax.erf(pre * math.sqrt(0.5)))
            pdf = jnp.exp(-0.5 * pre * pre) * (1.0 / math.sqrt(2.0 * math.pi))
            slope_scr[2 * s + g] = cdf + pre * pdf
            act = (pre * cdf).astype(bf16)
            act_ref[2 * s + g] = act
            term = dg(act, packs.get(s, WU, WU + 192, lanes), 1, 0)
            outer[g] = term if outer[g] is None else outer[g] + term
    outer = jnp.concatenate(outer, axis=1) + lines_ref[3:4, :]
    normed2, inverse2 = norm(outer + low.astype(f32))
    out_ref[...] = (normed2 * gain2 + lines_ref[5:6, :]).astype(bf16)
    cot = cot_ref[...].astype(f32)
    grad_h2 = norm_back(cot, normed2, inverse2, gain2)
    zed = grad_h2.astype(bf16)
    zed_ref[...] = zed
    halves = [zed[:, 0:192], zed[:, 192:384]]
    back = [None, None]
    for g in range(2):
        lanes = slice(192 * g, 192 * g + 192)
        for s in range(4):
            grad_act = dg(halves[g], packs.get(s, WU, WU + 192, lanes), 1, 1)
            gpre = (grad_act * slope_scr[2 * s + g]).astype(bf16)
            gpre_ref[2 * s + g] = gpre
            term = dg(gpre, packs.get(s, WI, WI + 192, lanes), 1, 1)
            back[g] = term if back[g] is None else back[g] + term
    grad_norm1 = jnp.concatenate(back, axis=1) + grad_h2
    grad_h1 = norm_back(grad_norm1, normed1, inverse1, gain1)
    gh_ref[...] = grad_h1
    gm = grad_h1.astype(bf16)
    gm_ref[...] = gm
    grads = dg(w_out, gm, 1, 1)
    for s, ref in enumerate((c0, c1, c23.at[0:48], c23.at[48:96])):
        ref[...] = grads[96 * s : 96 * s + 48].astype(bf16)
        gmix_ref[48 * s : 48 * s + 48, :] = grads[96 * s + 48 : 96 * s + 96]
    sums = [gm.astype(f32), grad_norm1 * normed1, grad_norm1, zed.astype(f32), cot * normed2, cot]
    lines = [jnp.sum(item, axis=0, keepdims=True) for item in sums]
    lines.append(jnp.zeros((2, 384), f32))
    vec_ref[...] = jnp.concatenate(lines, axis=0)


def weights_body(
    x_ref, xe_ref, a_ref, act_ref, gpre_ref, low_ref, zed_ref, gm_ref, vec_ref,
    pre_ref, depth_ref, gk_ref, kb_ref, dpt_ref, cve_ref, ex_ref, o0, o1, o2, o3, mark_ref,
    *, quarter, taps,
):
    outs = (o0, o1, o2, o3)
    mark_ref[...] = jnp.zeros_like(mark_ref)
    x_own = x_ref[...]
    extra, spread = ex_ref[...], cve_ref[...]
    g_query = dg(extra, x_own, 1, 0)
    q_bias = jnp.sum(extra.astype(f32), axis=1, keepdims=True)
    g_conv = dg(spread, xe_ref[...], 1, 0)
    c_bias = jnp.sum(spread.astype(f32), axis=1, keepdims=True)
    pre = pre_ref[...]
    g_point = dg(pre, depth_ref[...], 1, 0)
    p_bias = jnp.sum(pre.astype(f32), axis=1, keepdims=True)
    low, zed, gm = low_ref[...], zed_ref[...], gm_ref[...]
    lane = lax.broadcasted_iota(jnp.int32, (48, 128), 1)
    ones = jnp.ones((8, quarter), bf16)
    for s, out in enumerate(outs):
        own = slice(48 * s, 48 * s + 48)
        out[GP : GP + 48, :] = g_point[own].astype(bf16)
        out[GC : GC + 48, :] = g_conv[own].astype(bf16)
        out[GQ : GQ + 48, :] = g_query[own].astype(bf16)
        out[GO : GO + 96, :] = dg(a_ref[96 * s : 96 * s + 96, :], gm, 1, 0).astype(bf16)
        inner, outer, bias = [], [], []
        for g in range(2):
            lanes = slice(192 * g, 192 * g + 192)
            gpre = gpre_ref[2 * s + g]
            inner.append(dg(low[:, lanes], gpre, 0, 0))
            outer.append(dg(act_ref[2 * s + g], zed[:, lanes], 0, 0))
            bias.append(dg(ones, gpre, 1, 0)[0:1])
        out[GI : GI + 192, :] = jnp.concatenate(inner, axis=1).astype(bf16)
        out[GU : GU + 192, :] = jnp.concatenate(outer, axis=1).astype(bf16)
        tile = jnp.concatenate([gk_ref[s], jnp.zeros((48, 80), f32)], axis=1)
        tile = jnp.where(lane == 64, p_bias[own], tile)
        tile = jnp.where(lane == 65, c_bias[own], tile)
        tile = jnp.where(lane == 66, kb_ref[...], tile)
        tile = jnp.where(lane == 67, q_bias[own], tile)
        out[GM : GM + 48, 0:128] = tile.astype(bf16)
        out[GM : GM + 48, 128:384] = jnp.zeros((48, 256), bf16)
        bias = jnp.concatenate(bias, axis=1)
        lines = jnp.concatenate([bias, dpt_ref[0:taps, :], vec_ref[0:6, :]], axis=0)
        out[GV : GV + 16, :] = lines.astype(bf16)
        if out.shape[0] > GRAD_ROWS:
            out[GRAD_ROWS:, :] = jnp.zeros((out.shape[0] - GRAD_ROWS, 384), bf16)


def add_body(a_ref, b_ref, out_ref):
    out_ref[...] = (a_ref[...].astype(f32) + b_ref[...].astype(f32)).astype(out_ref.dtype)


def fold_body(place_ref, a_ref, b_ref, c_ref, keep_ref, give_ref):
    x = place_ref[3]
    half = keep_ref.shape[0]
    for out, part in ((keep_ref, x), (give_ref, 1 - x)):
        rows = pl.ds(pl.multiple_of(part * half, 16), half)
        first = (a_ref[rows, :].astype(f32) + b_ref[rows, :].astype(f32)).astype(bf16).astype(f32)
        out[...] = (first + c_ref[rows, :].astype(f32)).astype(bf16)


def edge_body(place_ref, tok_ref, edge_ref, layer_ref, out_ref):
    mp = place_ref[0]
    rows = tok_ref.shape[0]
    out_ref[0:rows, :] = tok_ref[...]
    out_ref[rows:, :] = layer_ref[...]
    low, high = slice(16, 32), slice(rows - 32, rows - 16)

    @pl.when(mp == 0)
    def _():
        out_ref[low, :] = (tok_ref[low, :].astype(f32) + edge_ref[...]).astype(bf16)

    @pl.when(mp == 3)
    def _():
        out_ref[high, :] = (tok_ref[high, :].astype(f32) + edge_ref[...]).astype(bf16)


def unpack_body(
    place_ref, own_ref, other_ref,
    point_ref, conv_ref, query_ref, out_ref, inner_ref, outer_ref, kernel_ref, qb_ref, ib_ref,
    dep_ref, pb_ref, cb_ref, kb_ref, *refs, taps,
):
    *vec_refs, scr = refs
    x = place_ref[3]
    half = own_ref.shape[0]
    scr[pl.ds(pl.multiple_of(x * half, 16), half), :] = own_ref[...].astype(f32)
    scr[pl.ds(pl.multiple_of((1 - x) * half, 16), half), :] = other_ref[...].astype(f32)
    point_ref[...] = scr[GP : GP + 48, :]
    conv_ref[...] = scr[GC : GC + 48, :]
    query_ref[...] = scr[GQ : GQ + 48, :]
    out_ref[0] = scr[GO : GO + 48, :]
    out_ref[1] = scr[GO + 48 : GO + 96, :]
    for g in range(2):
        lanes = slice(192 * g, 192 * g + 192)
        inner_ref[g] = scr[GI : GI + 192, lanes]
        outer_ref[g] = scr[GU : GU + 192, lanes]
        ib_ref[g : g + 1, :] = scr[GV : GV + 1, lanes]
    kernel_ref[...] = scr[GM : GM + 36, 0:48]
    turned = jnp.transpose(scr[GM : GM + 48, 0:128], (1, 0))
    pb_ref[...] = turned[64]
    cb_ref[...] = turned[65]
    kb_ref[...] = turned[66, 0:36]
    qb_ref[...] = turned[64:72, :]
    dep_ref[...] = scr[GV + 1 : GV + 1 + taps, :]
    for n, ref in enumerate(vec_refs):
        ref[...] = scr[GV + 1 + taps + n, :]


def head_weights_body(g_ref, x_ref, out_ref):
    grads = g_ref[...]
    out_ref[0:144, :] = dg(grads, x_ref[...], 1, 0).astype(bf16)
    out_ref[144:160, :] = jnp.zeros((16, 384), bf16)
    sums = dg(jnp.ones((16, grads.shape[1]), bf16), grads, 1, 1)
    out_ref[144:160, 0:144] = sums.astype(bf16)


def head_unpack_body(
    total_ref, other_ref, part_ref, bias_ref, q_ref, k_ref, v_ref, qb_ref, vb_ref
):
    total = total_ref[...].astype(f32) + other_ref[...].astype(f32)
    q_ref[...] = total[0:48] + part_ref[...]
    k_ref[...] = total[48:96]
    v_ref[...] = total[96:144]
    qb_ref[...] = total[144, 0:48] + bias_ref[3, :]
    vb_ref[...] = total[144, 96:144]


def tokens_body(place_ref, t0, t1, t2, t3, layer_ref, out_ref, acc, *, quarter):
    mp = place_ref[0]
    parts = (t0, t1, t2, t3)
    for s, ref in enumerate(parts):
        at = pl.multiple_of((mp ^ s) * quarter, quarter)
        layer_ref[pl.ds(at, quarter), :] = ref[quarter + 32 :, :]
        acc[pl.ds(at + 16, quarter), :] = ref[16 : quarter + 16, :].astype(f32)
    for s, ref in enumerate(parts):
        at = pl.multiple_of((mp ^ s) * quarter, quarter)
        acc[pl.ds(at, 16), :] += ref[0:16, :].astype(f32)
        acc[pl.ds(at + quarter + 16, 16), :] += ref[quarter + 16 : quarter + 32, :].astype(f32)
    out_ref[...] = acc[16 : 4 * quarter + 16, :]


def input_grad_body(
    g0, g1, g2, g3, p0, p1, p2, p3, tok_ref, out_ref, rows, done, scr, sems, *, quarter
):
    packs = Rows((p0, p1, p2, p3), scr, sems, HEAD_ROWS)
    grads = jnp.concatenate([ref[...] for ref in (g0, g1, g2, g3)], axis=0)
    packs.wait(0)
    weights = packs.all(WQ, WQ + 144)
    copies = []
    for n in range(4):
        span = slice(n * quarter, n * quarter + quarter)
        rows[span, :] = dg(grads[:, span], weights, 0, 0) + tok_ref[span, :]
        at = pl.ds(n * quarter, quarter)
        copies.append(pltpu.make_async_copy(rows.at[at], out_ref.at[at], done.at[n]))
        copies[n].start()
    for copy in copies:
        copy.wait()


def local(
    inputs, w_query, b_query, w_key, w_value, b_value, depth_kernel, w_point, b_point, w_kernel,
    b_kernel, w_conv, b_conv, w_out, b_out, gain_one, shift_one, w_inner, b_inner, w_outer,
    b_outer, gain_two, shift_two, cotangent,
):
    CALLS.clear()
    blocks = lax.axis_size("ctx")
    outer = blocks // 2
    rows_here = inputs.shape[0]
    quarter = rows_here // 4
    taps = depth_kernel.shape[0]
    rim = 64
    ctx, mp = lax.axis_index("ctx"), lax.axis_index("mp")
    x_at, z_at = ctx % 2, ctx // 2
    place = jnp.stack(
        [mp, ctx * rows_here + mp * quarter, blocks * rows_here, x_at, z_at]
    ).astype(jnp.int32)

    def table(change):
        pairs = []
        for z in range(outer):
            for x in range(2):
                for y in range(2):
                    for c in range(2):
                        z2, x2, y2, c2 = change(z, x, y, c)
                        pairs.append(((2 * z + x) * 4 + 2 * y + c, (2 * z2 + x2) * 4 + 2 * y2 + c2))
        return pairs

    def send(value, change):
        return lax.ppermute(value, ("ctx", "mp"), table(change))

    def across_c(z, x, y, c):
        return (z, x, y, c ^ 1)

    def across_y(z, x, y, c):
        return (z, x, y ^ 1, c)

    def across_x(z, x, y, c):
        return (z, x ^ 1, y, c)

    def across_z(i):
        return lambda z, x, y, c: (z ^ i, x, y, c)

    def line(vector):
        return vector.reshape(1, -1)

    def plus(left, right, hbm=(), final=()):
        return call(add_body, [(left.shape, bf16)], [left, right], us=1, hbm=hbm, final=final)[0]

    tick = lax.optimization_barrier
    bits = [1 << n for n in range(outer.bit_length() - 1)]
    rest = [i for i in range(1, outer) if i not in bits]

    kv, q = call(
        project_body,
        [((96, rows_here), bf16), ((48, rows_here), bf16)],
        [inputs, w_query.T, line(b_query), w_key.T, w_value.T, line(b_value)], us=2.4,
        hbm=range(6),
    )
    zkv, skv = [kv] + [None] * (outer - 1), [send(kv, across_x)] + [None] * (outer - 1)
    for i in bits:
        zkv[i] = send(kv, across_z(i))
    pack, lines = call(
        pack_body,
        [((PACK_ROWS, 384), bf16), ((8, 384), f32)],
        [w_query.T, w_key.T, w_value.T, w_point.T, w_conv.T, w_out, w_inner, w_outer, w_kernel.T,
         line(b_query), line(b_point), line(b_conv), b_inner, b_out, gain_one, shift_one, b_outer,
         gain_two, shift_two],
        us=2.2, after=(q,), hbm=range(19), final=(0,),
    )
    rims = jnp.where(mp == 0, inputs[rows_here - rim :], inputs[:rim])
    x_quarter = lax.dynamic_slice_in_dim(inputs, mp * quarter, quarter, 0)
    cot_quarter = lax.dynamic_slice_in_dim(cotangent, mp * quarter, quarter, 0)
    state = flash(q, [kv], None)
    pack, rims, x_quarter, cot_quarter, place, lines, state, skv[0], *got = tick(
        (pack, rims, x_quarter, cot_quarter, place, lines, state, skv[0], *(zkv[i] for i in bits))
    )
    for i, item in zip(bits, got, strict=True):
        zkv[i] = item
        skv[i] = send(item, across_x)
    for i in rest:
        zkv[i] = send(zkv[i & (i - 1)], across_z(i & -i))
    pack_beyond = send(pack, across_y)
    pairs = []
    for i in range(blocks - 1):
        pairs += [(4 * i, 4 * i + 4), (4 * i + 7, 4 * i + 3)]
    beside = lax.ppermute(rims, ("ctx", "mp"), pairs)
    todo = [skv[0], *(zkv[i] for i in bits)]
    for n in range(0, len(todo), 2):
        state = flash(q, todo[n : n + 2], state)
    state, beside, skv[bits[0]], *got = tick(
        (state, beside, skv[bits[0]], *(zkv[i] for i in rest))
    )
    for i, item in zip(rest, got, strict=True):
        zkv[i] = item
        skv[i] = send(item, across_x)
    todo = [skv[bits[0]], *got]
    for n in range(0, len(todo), 2):
        state = flash(q, todo[n : n + 2], state)
    state, pack_beyond, *got = tick((state, pack_beyond, *(skv[i] for i in bits[1:])))
    packs = [pack, send(pack, across_c), pack_beyond, send(pack_beyond, across_c)]
    for i, item in zip(bits[1:], got, strict=True):
        skv[i] = item
    todo = got + [skv[i] for i in rest]
    for n in range(0, len(todo) - 2, 2):
        state = flash(q, todo[n : n + 2], state)
    raw, lse, context, context_c, context_y = flash(q, todo[-2:], state, place)

    context, context_c, context_y, packs = tick((context, context_c, context_y, packs))
    heads_y = send(context_y, across_y)
    heads_c = send(context_c, across_c)
    extended = jnp.concatenate([beside, inputs, beside], axis=0)
    x_ext = lax.dynamic_slice_in_dim(extended, mp * quarter, quarter + 2 * rim, 0)
    ext = quarter + 2 * rim
    mix, depth, q_conv, key_conv, tap_probs, conv_vals = call(
        functools.partial(conv_body, rim=rim, quarter=quarter, taps=taps),
        [((192, quarter), bf16), ((quarter, 384), bf16), ((192, quarter), bf16),
         ((192, quarter), f32), ((8 * taps, quarter), f32), ((192, ext), f32)],
        [place, x_ext, depth_kernel, line(b_kernel), *packs],
        us=4.4, smem=(0,), raw=range(4, 8), hbm=(3,),
        scratch=row_scratch(CONV_ROWS),
    )
    heads_y, heads_c, mix = tick((heads_y, heads_c, mix))
    heads = [context, heads_c, heads_y, send(heads_y, across_c)]
    (layer_quarter, c0, c1, c23, grad_mix, both, act, gpre, low, zed, gm, grad_h1, vec) = call(
        feed_body,
        [((quarter, 384), bf16)] + [((48 * n, quarter), bf16) for n in (1, 1, 2)]
        + [((192, quarter), f32), ((384, quarter), bf16), ((8, quarter, 192), bf16),
           ((8, quarter, 192), bf16), ((quarter, 384), bf16), ((quarter, 384), bf16),
           ((quarter, 384), bf16), ((quarter, 384), f32), ((8, 384), f32)],
        [place, *heads, mix, *packs, x_quarter, cot_quarter, lines],
        us=6.8, smem=(0,), raw=range(6, 10),
        scratch=[pltpu.VMEM((8, quarter, 192), f32), *row_scratch(FEED_ROWS)],
    )
    grads_y = send(c23, across_y)
    grads_c = send(c1, across_c)
    extra, grad_kc, g_kernel, k_bias, g_depth, spread, token_part, edge = call(
        functools.partial(conv_back_body, rim=rim, quarter=quarter, taps=taps),
        [((192, quarter), bf16), ((192, quarter), bf16), ((4, 48, 48), f32), ((48, 128), f32),
         ((16, 384), f32), ((192, ext), bf16), ((quarter + 32, 384), bf16), ((16, 384), f32)],
        [place, x_ext, depth_kernel, *packs, q_conv, key_conv, tap_probs, conv_vals, grad_mix,
         grad_h1],
        us=5.4, smem=(0,), raw=range(3, 7), scratch=row_scratch(BACK_ROWS),
    )
    grads_y, grads_c, extra = tick((grads_y, grads_c, extra))
    grads = [c0, grads_c, grads_y, send(grads_y, across_c)]
    all_rows = -(-GRAD_ROWS // 32) * 32
    *sums, mark = call(
        functools.partial(weights_body, quarter=quarter, taps=taps),
        [((all_rows, 384), bf16)] * 4 + [((8, 128), f32)],
        [x_quarter, x_ext, both, act, gpre, low, zed, gm, vec, grad_kc, depth, g_kernel,
         k_bias, g_depth, spread, extra],
        us=4.6, final=(0,),
    )
    grads, mark = tick((grads, mark))
    q_aug, grad_aug = call(
        back_prepare_body,
        [((112, rows_here), bf16), ((64, rows_here), bf16)],
        [place, q, lse, raw, *grads], us=1.8, smem=(0,),
    )

    order = sorted(range(outer), key=lambda i: (-i.bit_count(), -i))
    edge_pairs = []
    for i in range(blocks - 1):
        edge_pairs += [(4 * i + 4, 4 * i + 3), (4 * i + 3, 4 * i + 4)]
    found = {i: [] for i in range(outer)}
    cross_found = {}

    def cross(pair, dq, after=()):
        dq, (parts,) = back(q, q_aug, grad_aug, [skv[i] for i in pair], dq, after=after)
        return dq, parts

    def spread_out(pair, parts):
        other = send(parts, across_x)
        for n, i in enumerate(pair):
            cross_found[i] = (other, n)

    def own(group, dq, after=()):
        sums = []
        for i in group:
            other, place = cross_found[i]
            sums.append(([other, *found[i]] if i else [other], place))
        dtypes = [bf16 if i else f32 for i in group]
        dq, parts = back(
            q, q_aug, grad_aug, [zkv[i] for i in group], dq, sums, dtypes, after
        )
        dq, parts = tick((dq, parts))
        for i, part in zip(group, parts, strict=True):
            if i:
                found[i & (i - 1)].append(send(part, across_z(i & -i)))
                found[i] = []
        return dq, parts[-1]

    givens = [send(sums[3], across_c), send(sums[1], across_c)]
    edge = lax.ppermute(edge, ("ctx", "mp"), edge_pairs)
    piece = plus(sums[2], givens[0])
    beyond = send(piece, across_y)
    piece, grad_aug = tick((piece, grad_aug))
    dq, parts = cross(order[:1], None)
    dq, parts, edge, layer_quarter = tick((dq, parts, edge, layer_quarter))
    spread_out(order[:1], parts)
    dq, parts = cross(order[1:2], dq)
    dq, parts, given = tick((dq, parts, givens[1]))
    spread_out(order[1:2], parts)
    for n in range(2, outer, 2):
        dq, parts = cross(order[n : n + 2], dq)
        other, at = cross_found[order[n - 2]]
        dq, parts, other = tick((dq, parts, other))
        cross_found[order[n - 2]] = (other, at)
        spread_out(order[n : n + 2], parts)
        dq, _ = own(order[n - 2 : n - 1], dq)
        other, at = cross_found[order[n - 1]]
        dq, other = tick((dq, other))
        cross_found[order[n - 1]] = (other, at)
        if n == outer - 2:
            both_parts = call(
                edge_body, [((2 * quarter + 32, 384), bf16)],
                [place, token_part, edge, layer_quarter], us=1, smem=(0,), final=(0,),
            )[0]
            beyond, dq, found = tick((beyond, dq, found))
            mine, give = call(
                fold_body, [((all_rows // 2, 384), bf16)] * 2, [place, sums[0], given, beyond],
                us=1, smem=(0,), hbm=(1,),
            )
            given = send(give, across_x)
        dq, _ = own(order[n - 1 : n], dq)
    other, _ = cross_found[0]
    dq, other = tick((dq, other, mine))[:2]
    cross_found.update({i: (other, n) for n, i in enumerate(order[-2:])})
    dq, last_part = own(order[-2:], dq, (mine, give))
    given, both_parts, dq = tick((given, both_parts, dq))
    piece = plus(mine, given)
    given = send(piece, across_z(bits[-1]))
    parts_beyond = send(both_parts, across_y)
    parts_beside = send(both_parts, across_c)
    *early, late = found[0]
    early, dq, _ = tick((early, dq, piece))
    last_part = call(
        gather_body, [((96, rows_here), f32)], [last_part, *early], us=JOIN_PACE,
    )[0]
    late, last_part = tick((late, last_part))

    head_grads = call(
        back_join_body, [((144, rows_here), bf16)], [dq, last_part, late], us=2.1,
    )[0]
    head_w = call(
        head_weights_body, [((160, 384), bf16)], [head_grads, inputs], us=2.2,
    )[0]
    head_other = send(head_w, across_x)
    grads_beyond = send(head_grads, across_y)
    grads_beside = send(head_grads, across_c)
    given, parts_beyond, head_w = tick((given, parts_beyond, head_w))
    parts_other = send(parts_beyond, across_c)
    if len(bits) > 1:
        piece = plus(piece, given)
        given = send(piece, across_z(bits[-2]))
    parts_other = tick((parts_other, piece))[0]
    both = [both_parts, parts_beside, parts_beyond, parts_other]
    layer_out, tokens = call(
        functools.partial(tokens_body, quarter=quarter),
        [((rows_here, 384), bf16), ((rows_here, 384), f32)],
        [place, *both], us=2.3, smem=(0,), final=(0,), hbm=(1,), after=(head_w,),
        scratch=[pltpu.VMEM((rows_here + 32, 384), f32)],
    )
    head_other, _ = tick((head_other, layer_out))
    head_w = plus(head_w, head_other)
    head_other = send(head_w, across_z(bits[0]))
    grads_beyond, head_w = tick((grads_beyond, head_w))
    grads_other = send(grads_beyond, across_c)
    for n, bit in enumerate(bits[1:]):
        head_other = tick((head_other, grads_beyond))[0]
        head_w = plus(head_w, head_other)
        head_other = send(head_w, across_z(bit))
        given = tick((given, head_w))[0]
        piece = plus(piece, given)
        given = send(piece, across_z(bits[-3 - n]) if n + 2 < len(bits) else across_x)
    grads_other, _ = tick((grads_other, piece))
    inputs_grad = call(
        functools.partial(input_grad_body, quarter=quarter),
        [((rows_here, 384), f32)],
        [head_grads, grads_beside, grads_beyond, grads_other, *packs, tokens], us=3.0,
        raw=range(4, 8), final=(0,), raw_out=(0,),
        scratch=[
            pltpu.VMEM((rows_here, 384), f32), pltpu.SemaphoreType.DMA((4,)),
            *row_scratch(HEAD_ROWS),
        ],
    )[0]
    other_piece, _ = tick((given, inputs_grad))
    (point, conv, query_part, grad_out, grad_inner, grad_outer, kernel, biases, i_bias, grad_depth,
     p_bias, c_bias, k_bias, *vecs) = call(
        functools.partial(unpack_body, taps=taps),
        [((48, 384), f32)] * 3 + [((2, 48, 384), f32), ((2, 192, 192), f32),
         ((2, 192, 192), f32), ((36, 48), f32), ((8, 48), f32), ((2, 192), f32), ((taps, 384), f32),
         ((48,), f32), ((48,), f32), ((36,), f32)] + [((384,), f32)] * 6,
        [place, piece, other_piece], us=2.3, smem=(0,), final=(0, 1, 3, 4, 5, 6, *range(8, 19)),
        scratch=[pltpu.VMEM((all_rows, 384), f32)],
    )
    query, key, value, q_bias, v_bias = call(
        head_unpack_body,
        [((48, 384), f32)] * 3 + [((48,), f32)] * 2,
        [head_w, head_other, query_part, biases], us=1.7, final=range(5),
    )

    return (
        layer_out, inputs_grad, query.T, q_bias, key.T, value.T, v_bias, grad_depth, point.T,
        p_bias, kernel.T, k_bias, conv.T, c_bias, grad_out, vecs[0], vecs[1], vecs[2], grad_inner,
        i_bias, grad_outer, vecs[3], vecs[4], vecs[5],
    )


def solution(mesh):
    return jax.shard_map(
        local,
        mesh=mesh,
        in_specs=(
            P("ctx", None), P(None, "mp"), P("mp"), P(None, "mp"), P(None, "mp"), P("mp"), P(),
            P(None, "mp"), P("mp"), P("mp", None), P(), P(None, "mp"), P("mp"),
            P(None, "mp", None), P(), P(), P(), P(None, None, "mp"), P(None, "mp"),
            P(None, "mp", None), P(), P(), P(), P("ctx", None),
        ),
        out_specs=(
            P("ctx", None), P("ctx", None), P(None, "mp"), P("mp"), P(None, "mp"), P(None, "mp"),
            P("mp"), P(), P(None, "mp"), P("mp"), P("mp", None), P(), P(None, "mp"), P("mp"),
            P(None, "mp", None), P(), P(), P(), P(None, None, "mp"), P(None, "mp"),
            P(None, "mp", None), P(), P(), P(),
        ),
        check_vma=False,
    )
```
